32 devices in a mesh: dp: 4 (over z), code: 8 (over y, x, core).
Axes of the slice: x: 2, y: 2, z: 4, core: 2. Of those that a mesh axis runs over, the one named last changes fastest.
Arguments:
- residuals: bfloat16 [8192, 1024], P('dp'), may hold values from -6 to 6
- codes: int32 [8192, 128], P('dp', 'code'), may hold values from 0 to 255, as said below
- codebook: float32 [128, 256, 8], P('code'), may hold values from -6 to 6
Outputs:
- rotated: float32 [8192, 1024], P('dp', 'code')
- new_codebook: float32 [128, 256, 8], P('code')
The draws below stay inside these ranges and needn't reach their ends.
Inputs may be any that keep to these rules, and one draw needn't show every extreme that they name: `codes`: each entry names a codeword of its subspace.
All inputs are finite; a program needn't handle non-finite values.
Results may differ from the reference program's by a relative error of at most 0.008.
Values may be sent and summed in bfloat16 or wider, within the bound.
No kernel may reach another device: no remote copies, remote signals or barrier semaphores. Data moves between devices by JAX's collectives and lax.ppermute only.
A program may use at most 64 MiB of HBM per device.

```python
import jax
import jax.numpy as jnp
from jax import lax

D = 1024
M = 128
K = 256
NS_ITERS = 3
DS = 8
ROWS = 8192


def shared_tables(key):
    code_key = jax.random.fold_in(key, 101)
    book_key = jax.random.fold_in(key, 202)
    word_codes = jax.random.randint(code_key, (ROWS, M), 0, K, dtype=jnp.int32)
    word_codes = word_codes.at[0, 0].set(0)
    word_codes = word_codes.at[0, 1].set(K - 1)
    word_book = jax.random.normal(book_key, (M, K, DS), jnp.float32)
    word_book = jnp.clip(word_book, -6.0, 6.0)
    return (word_codes, word_book)


def draw_codes(key, part):
    word_codes, word_book = shared_tables(key)
    return word_codes


def draw_codebook(key, part):
    word_codes, word_book = shared_tables(key)
    return word_book


def draw_residuals(key, part):
    word_codes, word_book = shared_tables(key)
    basis_key = jax.random.fold_in(key, 404)
    jitter_key = jax.random.fold_in(key, 505)
    subspace = jnp.arange(M, dtype=jnp.int32)[None, :]
    rebuilt = word_book[subspace, word_codes].reshape(ROWS, D)
    rank_count = max(D * 3 // 16, 4)
    mixing_basis = jax.random.normal(basis_key, (D, rank_count), jnp.float32) / jnp.sqrt(jnp.float32(D))
    position = jnp.arange(rank_count, dtype=jnp.float32)
    weights = 3.0 * (1.0 + 6.0 * position / rank_count) ** (-0.5)
    projected = jnp.dot(rebuilt, mixing_basis) * weights[None, :]
    signal_part = jnp.dot(projected, mixing_basis.T)
    jitter = jax.random.normal(jitter_key, (ROWS, D), jnp.float32)
    return jnp.clip(jitter + signal_part, -6.0, 6.0).astype(jnp.bfloat16)


def setup_inputs(seed: int = 0) -> dict:
    splits = jax.random.split(jax.random.key(seed), 4)
    residuals = draw_residuals(jax.random.fold_in(splits[3], 71), 0)
    codes = draw_codes(jax.random.fold_in(splits[3], 71), 0)
    codebook = draw_codebook(jax.random.fold_in(splits[3], 71), 0)
    return {"residuals": residuals, "codes": codes, "codebook": codebook}


quintic_a = 3.4445
quintic_b = -4.775
quintic_c = 2.0315
prior_weight = 8.0
epsilon = 1e-06

def reference(residuals, codes, codebook):
    subspace = jnp.arange(M, dtype=jnp.int32)[None, :]
    recon = codebook[subspace, codes].reshape(ROWS, D).astype(jnp.bfloat16)
    cross = jnp.dot(residuals.T, recon, preferred_element_type=jnp.float32)
    frob = jnp.sum(cross * cross)
    iterate = cross / jnp.sqrt(frob + epsilon)
    highest = lax.Precision.HIGHEST
    for iteration in range(NS_ITERS):
        gram = jnp.dot(iterate.T, iterate, precision=highest)
        image = jnp.dot(iterate, gram, precision=highest)
        square = jnp.dot(iterate.T, image, precision=highest)
        iterate = quintic_a * iterate + jnp.dot(iterate, quintic_b * gram + quintic_c * square, precision=highest)
    rotation = iterate.astype(jnp.bfloat16)
    rotated = jnp.dot(residuals, rotation, preferred_element_type=jnp.float32)
    segment_ids = (codes + subspace * K).reshape(-1)
    sums = jax.ops.segment_sum(rotated.reshape(ROWS * M, DS), segment_ids, num_segments=M * K)
    counts = jax.ops.segment_sum(jnp.ones((ROWS * M,), jnp.float32), segment_ids, num_segments=M * K)
    sums = sums.reshape(M, K, DS)
    counts = counts.reshape(M, K)
    new_codebook = (sums + prior_weight * codebook) / (counts[:, :, None] + prior_weight)
    return (rotated, new_codebook)
```

```python
import functools

import jax
import jax.numpy as jnp
from jax import lax
from jax.experimental import pallas as pl
from jax.experimental.pallas import tpu as pltpu
from jax.sharding import PartitionSpec as P

quintic_a = 3.4445
quintic_b = -4.775
quintic_c = 2.0315
prior_weight = 8.0
epsilon = 1e-06
f32, bf16 = jnp.float32, jnp.bfloat16
VMEM_LIMIT = 56 * 1024 * 1024
NT = (((1,), (1,)), ((), ()))


def dot(left, right):
    return jnp.dot(left, right, preferred_element_type=f32)


def dot_nt(left, right):
    return lax.dot_general(left, right, NT, preferred_element_type=f32)


def cross_kernel(codes_ref, book_ref, res_ref, out_ref, recon):
    subs, rows = codes_ref.shape
    width = book_ref.shape[0] // subs
    words = book_ref.shape[1]
    lanes = 128
    for m in range(subs):
        band = pl.ds(m * width, width)
        tables = [book_ref[band, pl.ds(t * lanes, lanes)] for t in range(words // lanes)]
        for c in range(rows // lanes):
            cols = pl.ds(c * lanes, lanes)
            code = jnp.broadcast_to(codes_ref[pl.ds(m, 1), cols], (width, lanes))
            low = jnp.bitwise_and(code, lanes - 1)
            value = jnp.take_along_axis(tables[0], low, axis=1, mode="promise_in_bounds")
            for t in range(1, len(tables)):
                other = jnp.take_along_axis(tables[t], low, axis=1, mode="promise_in_bounds")
                value = jnp.where(code >= t * lanes, other, value)
            recon[band, cols] = value
    out_ref[...] = dot(recon[...].astype(bf16), res_ref[...])


def cross_partial(codes_t, book_t, residuals):
    rows, dim = residuals.shape
    cols = book_t.shape[0]
    return pl.pallas_call(
        cross_kernel,
        out_shape=jax.ShapeDtypeStruct((cols, dim), f32),
        in_specs=[pl.BlockSpec(memory_space=pltpu.VMEM)] * 3,
        out_specs=pl.BlockSpec(memory_space=pltpu.VMEM),
        scratch_shapes=[pltpu.VMEM((cols, rows), f32)],
        compiler_params=pltpu.CompilerParams(vmem_limit_bytes=VMEM_LIMIT),
        name="cross_partial",
    )(codes_t, book_t, residuals)


def polar_kernel(place_ref, *refs, blocks, pieces, chunk):
    block_refs = refs[:blocks]
    res_ref, codes_ref, rotated_ref, sums_ref = refs[blocks : blocks + 4]
    raw, gram, gram_b, poly_b, iterate, iterate_b, res, rot_b, rot_t, res_sem = refs[blocks + 4 :]
    dim = raw.shape[0]
    own = rot_b.shape[0]
    steps = dim // chunk
    load = pltpu.make_async_copy(res_ref, res, res_sem)
    load.start()
    at = 0
    for block in block_refs:
        raw[pl.ds(at, block.shape[0]), :] = block[...]
        at += block.shape[0]

    def rows_of(i):
        return pl.ds(pl.multiple_of(i * chunk, chunk), chunk)

    def gram_step(source, i, trace):
        rows = rows_of(i)
        part = dot_nt(source[rows, :], source[...])
        gram[rows, :] = part
        gram_b[rows, :] = part.astype(bf16)
        if trace is None:
            return None
        r = lax.broadcasted_iota(jnp.int32, (chunk, dim), 0) + i * chunk
        c = lax.broadcasted_iota(jnp.int32, (chunk, dim), 1)
        return trace + jnp.sum(jnp.where(r == c, part, 0.0))

    frob = lax.fori_loop(0, steps, lambda i, t: gram_step(raw, i, t), jnp.zeros((), f32))
    scale2 = 1.0 / (frob + epsilon)
    scale = lax.rsqrt(frob + epsilon)

    def poly_step(i, wb, wc):
        rows = rows_of(i)
        square = dot(gram_b[rows, :], gram_b[...])
        poly_b[rows, :] = (wb * gram[rows, :] + wc * square).astype(bf16)

    @pl.loop(0, steps)
    def _(i):
        poly_step(i, quintic_b * scale2, quintic_c * scale2 * scale2)

    @pl.loop(0, steps)
    def _(i):
        rows = rows_of(i)
        value = scale * (quintic_a * raw[rows, :].astype(f32) + dot(poly_b[rows, :], raw[...]))
        iterate[rows, :] = value
        iterate_b[rows, :] = value.astype(bf16)

    @pl.loop(0, steps)
    def _(i):
        gram_step(iterate_b, i, None)

    @pl.loop(0, steps)
    def _(i):
        poly_step(i, quintic_b, quintic_c)

    @pl.loop(0, steps)
    def _(i):
        rows = rows_of(i)
        value = quintic_a * iterate[rows, :] + dot(poly_b[rows, :], iterate_b[...])
        iterate[rows, :] = value
        raw[rows, :] = value.astype(bf16)

    mine = pl.ds(0, own)
    g = dot_nt(raw[mine, :], raw[...])
    image = dot(g.astype(bf16), raw[...])
    square = dot_nt(image.astype(bf16), raw[...])
    last = quintic_a * iterate[mine, :] + dot(
        (quintic_b * g + quintic_c * square).astype(bf16), raw[...]
    )
    size = own // pieces
    for p in range(pieces):
        to = 0 if pieces == 1 else pl.multiple_of(jnp.bitwise_xor(place_ref[0], p) * size, size)
        rot_b[pl.ds(to, size), :] = last[p * size : (p + 1) * size, :].astype(bf16)

    load.wait()
    rows_all = res.shape[0]
    step = 256

    @pl.loop(0, rows_all // step)
    def _(i):
        rows = pl.ds(pl.multiple_of(i * step, step), step)
        part = dot_nt(rot_b[...], res[rows, :])
        rot_t[:, rows] = part.astype(bf16)
        rotated_ref[rows, :] = part.T

    subs = codes_ref.shape[0]
    words = sums_ref.shape[1]
    width = own // subs
    for m in range(subs):
        band = pl.ds(m * width, width)
        code = codes_ref[pl.ds(m, 1), :]
        word = lax.broadcasted_iota(jnp.int32, (words, rows_all), 0)
        onehot = (word == code).astype(f32).astype(bf16)
        tall = jnp.concatenate([rot_t[band, :], jnp.ones((8, rows_all), bf16)], axis=0)
        part = dot_nt(tall, onehot)
        sums_ref[band, :] = part[:width, :]
        sums_ref[pl.ds(own + m, 1), :] = part[width : width + 1, :]


def polar(place, block_list, residuals, codes_t, own, words, pieces):
    rows, dim = residuals.shape
    subs = codes_t.shape[0]
    vmem = pl.BlockSpec(memory_space=pltpu.VMEM)
    chunk = 256
    kernel = functools.partial(polar_kernel, blocks=len(block_list), pieces=pieces, chunk=chunk)
    return pl.pallas_call(
        kernel,
        out_shape=(
            jax.ShapeDtypeStruct((rows, own), f32),
            jax.ShapeDtypeStruct((own + subs, words), f32),
        ),
        in_specs=[pl.BlockSpec(memory_space=pltpu.SMEM)]
        + [vmem] * len(block_list)
        + [pl.BlockSpec(memory_space=pl.ANY), vmem],
        out_specs=(vmem, vmem),
        scratch_shapes=[
            pltpu.VMEM((dim, dim), bf16),
            pltpu.VMEM((dim, dim), f32),
            pltpu.VMEM((dim, dim), bf16),
            pltpu.VMEM((dim, dim), bf16),
            pltpu.VMEM((dim, dim), f32),
            pltpu.VMEM((dim, dim), bf16),
            pltpu.VMEM((rows, dim), bf16),
            pltpu.VMEM((own, dim), bf16),
            pltpu.VMEM((own, rows), bf16),
            pltpu.SemaphoreType.DMA,
        ],
        compiler_params=pltpu.CompilerParams(vmem_limit_bytes=VMEM_LIMIT),
        name="polar",
    )(place, *block_list, residuals, codes_t)


def swap(value, axis, size, mask):
    return lax.ppermute(value, axis, [(i, i ^ mask) for i in range(size)])


def exchange_sum(value, axis, size, place):
    piece = value.shape[0] // size
    take = lambda q: lax.dynamic_slice_in_dim(value, q * piece, piece, 0)
    total = take(place)
    got = [swap(take(place ^ k).astype(bf16), axis, size, k) for k in range(1, size)]
    for part in got:
        total = total + part.astype(f32)
    return total


def make_body(dp, code):
    def body(residuals, codes, codebook):
        rows, dim = residuals.shape
        subs, words, width = codebook.shape
        own = subs * width
        place = lax.axis_index("dp")
        codes_t = codes.T
        book_t = jnp.transpose(codebook, (0, 2, 1)).reshape(own, words)
        partial = cross_partial(codes_t, book_t, residuals)
        piece = exchange_sum(partial, "dp", dp, place).astype(bf16)
        pieces = [piece] + [swap(piece, "dp", dp, k) for k in range(1, dp)]
        size = own // dp
        if size % 16 == 0:
            block, parts = jnp.concatenate(pieces, axis=0), dp
        else:
            block, parts = jnp.zeros((own, dim), bf16), 1
            for k, value in enumerate(pieces):
                block = lax.dynamic_update_slice_in_dim(block, value, (place ^ k) * size, 0)
        strides = []
        s = 1
        while s < code:
            strides.append(s)
            s *= 2
        strides = strides[::-1]
        far, near = strides[:-1], strides[-1:]
        half = own // 2
        top, bottom = block[:half], block[half:]
        tops, bottoms = [top], [bottom]
        for one, two in zip(far, far[::-1]):
            tops = tops + [swap(t, "code", code, one) for t in tops]
            bottoms = bottoms + [swap(t, "code", code, two) for t in bottoms]
        held = tops + bottoms
        for stride in near:
            held = held + [swap(t, "code", code, stride) for t in held]
        held = [held[0], held[len(tops)]] + held[1 : len(tops)] + held[len(tops) + 1 :]
        rotated, sums = polar(
            place.astype(jnp.int32).reshape(1), held, residuals, codes_t, own, words, parts
        )
        sums_b = sums.astype(bf16)
        total = sums
        for k in range(1, dp):
            total = total + swap(sums_b, "dp", dp, k).astype(f32)
        sums_t = total[:own].reshape(subs, width, words)
        counts = total[own:]
        book = (sums_t + prior_weight * book_t.reshape(subs, width, words)) / (
            counts[:, None, :] + prior_weight
        )
        return rotated, jnp.transpose(book, (0, 2, 1))

    return body


def solution(mesh):
    dp, code = mesh.shape["dp"], mesh.shape["code"]
    in_specs = (P("dp", None), P("dp", "code"), P("code", None, None))
    out_specs = (P("dp", "code"), P("code", None, None))
    return jax.shard_map(
        make_body(dp, code), mesh=mesh, in_specs=in_specs, out_specs=out_specs, check_vma=False
    )
```

```python
import functools

import jax
import jax.numpy as jnp
from jax import lax
from jax.experimental import pallas as pl
from jax.experimental.pallas import tpu as pltpu
from jax.sharding import PartitionSpec as P

quintic_a = 3.4445
quintic_b = -4.775
quintic_c = 2.0315
prior_weight = 8.0
epsilon = 1e-06
f32, bf16 = jnp.float32, jnp.bfloat16
MIB = 1024 * 1024
NT = (((1,), (1,)), ((), ()))


def dot(left, right):
    return jnp.dot(left, right, preferred_element_type=f32)


def dot_nt(left, right):
    return lax.dot_general(left, right, NT, preferred_element_type=f32)


def cross_kernel(codes_ref, book_ref, res_ref, out_ref, recon):
    subs, rows = codes_ref.shape
    width = book_ref.shape[0] // subs
    words = book_ref.shape[1]
    lanes = 128
    for m in range(subs):
        band = pl.ds(m * width, width)
        tables = [book_ref[band, pl.ds(t * lanes, lanes)] for t in range(words // lanes)]
        for c in range(rows // lanes):
            cols = pl.ds(c * lanes, lanes)
            code = jnp.broadcast_to(codes_ref[pl.ds(m, 1), cols], (width, lanes))
            low = jnp.bitwise_and(code, lanes - 1)
            value = jnp.take_along_axis(tables[0], low, axis=1, mode="promise_in_bounds")
            for t in range(1, len(tables)):
                other = jnp.take_along_axis(tables[t], low, axis=1, mode="promise_in_bounds")
                value = jnp.where(code >= t * lanes, other, value)
            recon[band, cols] = value
    out_ref[...] = dot(recon[...].astype(bf16), res_ref[...]).astype(bf16)


def cross_partial(codes_t, book_t, residuals):
    rows, dim = residuals.shape
    cols = book_t.shape[0]
    return pl.pallas_call(
        cross_kernel,
        out_shape=jax.ShapeDtypeStruct((cols, dim), bf16),
        in_specs=[pl.BlockSpec(memory_space=pltpu.VMEM)] * 3,
        out_specs=pl.BlockSpec(memory_space=pltpu.VMEM),
        scratch_shapes=[pltpu.VMEM((cols, rows), f32)],
        compiler_params=pltpu.CompilerParams(vmem_limit_bytes=16 * MIB),
        name="cross_partial",
    )(codes_t, book_t, residuals)


def polar_kernel(*refs, blocks, chunk):
    block_refs = refs[:blocks]
    res_ref, codes_ref, rotated_ref, sent_ref = refs[blocks : blocks + 4]
    raw, gram, gram_b, poly_b, iterate, iterate_b, res, rot_b, rot_t, sums_ref, res_sem = refs[
        blocks + 4 :
    ]
    dim = raw.shape[0]
    own = rot_b.shape[0]
    steps = dim // chunk
    load = pltpu.make_async_copy(res_ref, res, res_sem)
    load.start()
    at = 0
    for block in block_refs:
        raw[pl.ds(at, block.shape[0]), :] = block[...]
        at += block.shape[0]

    def rows_of(i):
        return pl.ds(pl.multiple_of(i * chunk, chunk), chunk)

    def gram_step(source, i, trace):
        rows = rows_of(i)
        part = dot_nt(source[rows, :], source[...])
        gram[rows, :] = part
        gram_b[rows, :] = part.astype(bf16)
        if trace is None:
            return None
        r = lax.broadcasted_iota(jnp.int32, (chunk, dim), 0) + i * chunk
        c = lax.broadcasted_iota(jnp.int32, (chunk, dim), 1)
        return trace + jnp.sum(jnp.where(r == c, part, 0.0))

    frob = lax.fori_loop(0, steps, lambda i, t: gram_step(raw, i, t), jnp.zeros((), f32))
    scale2 = 1.0 / (frob + epsilon)
    scale = lax.rsqrt(frob + epsilon)

    def poly_step(i, wb, wc):
        rows = rows_of(i)
        square = dot(gram_b[rows, :], gram_b[...])
        poly_b[rows, :] = (wb * gram[rows, :] + wc * square).astype(bf16)

    @pl.loop(0, steps)
    def _(i):
        poly_step(i, quintic_b * scale2, quintic_c * scale2 * scale2)

    @pl.loop(0, steps)
    def _(i):
        rows = rows_of(i)
        value = scale * (quintic_a * raw[rows, :].astype(f32) + dot(poly_b[rows, :], raw[...]))
        iterate[rows, :] = value
        iterate_b[rows, :] = value.astype(bf16)

    @pl.loop(0, steps)
    def _(i):
        gram_step(iterate_b, i, None)

    @pl.loop(0, steps)
    def _(i):
        poly_step(i, quintic_b, quintic_c)

    @pl.loop(0, steps)
    def _(i):
        rows = rows_of(i)
        value = quintic_a * iterate[rows, :] + dot(poly_b[rows, :], iterate_b[...])
        iterate[rows, :] = value
        raw[rows, :] = value.astype(bf16)

    mine = pl.ds(0, own)
    g = dot_nt(raw[mine, :], raw[...])
    image = dot(g.astype(bf16), raw[...])
    square = dot_nt(image.astype(bf16), raw[...])
    last = quintic_a * iterate[mine, :] + dot(
        (quintic_b * g + quintic_c * square).astype(bf16), raw[...]
    )
    rot_b[...] = last.astype(bf16)

    load.wait()
    rows_all = res.shape[0]
    step = 256

    @pl.loop(0, rows_all // step)
    def _(i):
        rows = pl.ds(pl.multiple_of(i * step, step), step)
        part = dot_nt(res[rows, :], rot_b[...])
        rotated_ref[rows, :] = part
        rot_t[:, rows] = part.T

    subs = codes_ref.shape[0]
    words = sums_ref.shape[1]
    width = own // subs
    lows = 64
    highs = words // lows
    group = min(subs, 256 // lows)
    low_word = lax.broadcasted_iota(jnp.int32, (lows, rows_all), 0)
    high_word = lax.broadcasted_iota(jnp.int32, (8, rows_all), 0)
    for first in range(0, subs, group):
        onehots, values, marks = [], [], []
        for m in range(first, first + group):
            code = codes_ref[pl.ds(m, 1), :]
            low, high = jnp.bitwise_and(code, lows - 1), jnp.right_shift(code, 6)
            onehots.append(jnp.where(low_word == low, 1.0, 0.0).astype(bf16))
            band = rot_t[pl.ds(m * width, width), :]
            values += [jnp.where(high == h, band, 0.0) for h in range(highs)]
            marks.append(jnp.where(high_word == high, 1.0, 0.0))
        tall = jnp.concatenate(values + marks, axis=0).astype(bf16)
        part = dot_nt(tall, jnp.concatenate(onehots, axis=0))
        for s in range(group):
            m = first + s
            cols = slice(s * lows, (s + 1) * lows)
            for h in range(highs):
                to = pl.ds(h * lows, lows)
                at = (s * highs + h) * width
                sums_ref[pl.ds(m * width, width), to] = part[at : at + width, cols]
                at = group * highs * width + s * 8 + h
                sums_ref[pl.ds(own + m, 1), to] = part[at : at + 1, cols]
    total = sums_ref[...].astype(bf16)
    for q in range(sent_ref.shape[0]):
        sent_ref[q] = total


def polar(block_list, residuals, codes_t, own, words, peers):
    rows, dim = residuals.shape
    subs = codes_t.shape[0]
    vmem = pl.BlockSpec(memory_space=pltpu.VMEM)
    chunk = 256
    kernel = functools.partial(polar_kernel, blocks=len(block_list), chunk=chunk)
    return pl.pallas_call(
        kernel,
        out_shape=(
            jax.ShapeDtypeStruct((rows, own), f32),
            jax.ShapeDtypeStruct((peers, own + subs, words), bf16),
        ),
        in_specs=[vmem] * len(block_list)
        + [pl.BlockSpec(memory_space=pl.ANY), vmem],
        out_specs=(vmem, vmem),
        scratch_shapes=[
            pltpu.VMEM((dim, dim), bf16),
            pltpu.VMEM((dim, dim), f32),
            pltpu.VMEM((dim, dim), bf16),
            pltpu.VMEM((dim, dim), bf16),
            pltpu.VMEM((dim, dim), f32),
            pltpu.VMEM((dim, dim), bf16),
            pltpu.VMEM((rows, dim), bf16),
            pltpu.VMEM((own, dim), bf16),
            pltpu.VMEM((own, rows), f32),
            pltpu.VMEM((own + subs, words), f32),
            pltpu.SemaphoreType.DMA,
        ],
        compiler_params=pltpu.CompilerParams(vmem_limit_bytes=36 * MIB),
        name="polar",
    )(*block_list, residuals, codes_t)


def swap(value, axis, size, mask):
    return lax.ppermute(value, axis, [(i, i ^ mask) for i in range(size)])


def share_kernel(parts_ref, out_ref):
    total = parts_ref[0].astype(f32)
    for q in range(1, parts_ref.shape[0]):
        total = total + parts_ref[q].astype(f32)
    for q in range(out_ref.shape[0]):
        out_ref[q] = total.astype(bf16)


def book_kernel(sums_ref, book_ref, out_ref):
    own = book_ref.shape[0]
    subs = sums_ref.shape[1] - own
    width = own // subs
    total = sums_ref[0].astype(f32)
    for q in range(1, sums_ref.shape[0]):
        total = total + sums_ref[q].astype(f32)
    for m in range(subs):
        band = pl.ds(m * width, width)
        count = total[own + m : own + m + 1, :] + prior_weight
        part = total[m * width : (m + 1) * width, :]
        out_ref[band, :] = (part + prior_weight * book_ref[band, :]) / count


def small_call(kernel, name, shape, dtype, *operands):
    vmem = pl.BlockSpec(memory_space=pltpu.VMEM)
    return pl.pallas_call(
        kernel,
        out_shape=jax.ShapeDtypeStruct(shape, dtype),
        in_specs=[vmem] * len(operands),
        out_specs=vmem,
        compiler_params=pltpu.CompilerParams(vmem_limit_bytes=16 * MIB),
        name=name,
    )(*operands)


def swap_all(value, axis):
    return lax.all_to_all(value, axis, 0, 0)


def make_body(dp, code):
    def body(residuals, codes, codebook):
        rows, dim = residuals.shape
        subs, words, width = codebook.shape
        own = subs * width
        codes_t = codes.T
        book_t = jnp.transpose(codebook, (0, 2, 1)).reshape(own, words)
        partial = cross_partial(codes_t, book_t, residuals)
        shares = swap_all(partial.reshape(dp, own // dp, dim), "dp")
        pieces = small_call(share_kernel, "share", shares.shape, bf16, shares)
        block = swap_all(pieces, "dp").reshape(own, dim)
        strides = []
        s = 1
        while s < code:
            strides.append(s)
            s *= 2
        strides = strides[::-1]
        far, near = strides[:-1], strides[-1:]
        half = own // 2
        top, bottom = block[:half], block[half:]
        tops, bottoms = [top], [bottom]
        for one, two in zip(far, far[::-1]):
            tops = tops + [swap(t, "code", code, one) for t in tops]
            bottoms = bottoms + [swap(t, "code", code, two) for t in bottoms]
        held = tops + bottoms
        for stride in near:
            held = held + [swap(t, "code", code, stride) for t in held]
        held = [held[0], held[len(tops)]] + held[1 : len(tops)] + held[len(tops) + 1 :]
        rotated, sums = polar(held, residuals, codes_t, own, words, dp)
        sums = swap_all(sums, "dp")
        book = small_call(book_kernel, "book", (own, words), f32, sums, book_t)
        return rotated, jnp.transpose(book.reshape(subs, width, words), (0, 2, 1))

    return body


def solution(mesh):
    dp, code = mesh.shape["dp"], mesh.shape["code"]
    in_specs = (P("dp", None), P("dp", "code"), P("code", None, None))
    out_specs = (P("dp", "code"), P("code", None, None))
    return jax.shard_map(
        make_body(dp, code), mesh=mesh, in_specs=in_specs, out_specs=out_specs, check_vma=False
    )
```

```python
import functools

import jax
import jax.numpy as jnp
from jax import lax
from jax.experimental import pallas as pl
from jax.experimental.pallas import tpu as pltpu
from jax.sharding import PartitionSpec as P

quintic_a = 3.4445
quintic_b = -4.775
quintic_c = 2.0315
prior_weight = 8.0
epsilon = 1e-06
f32, bf16 = jnp.float32, jnp.bfloat16
MIB = 1024 * 1024
NT = (((1,), (1,)), ((), ()))


def dot(left, right):
    return jnp.dot(left, right, preferred_element_type=f32)


def dot_nt(left, right):
    return lax.dot_general(left, right, NT, preferred_element_type=f32)


def cross_kernel(codes_hbm, book_hbm, res_hbm, *refs, dp):
    outs = refs[: dp or 1]
    codes_ref, book_ref, res_ref, recon, cross, sems = refs[dp or 1 :]
    loads = [
        pltpu.make_async_copy(codes_hbm, codes_ref, sems.at[0]),
        pltpu.make_async_copy(book_hbm, book_ref, sems.at[1]),
        pltpu.make_async_copy(res_hbm, res_ref, sems.at[2]),
    ]
    for load in loads:
        load.start()
    loads[0].wait()
    loads[1].wait()
    subs, rows = codes_ref.shape
    width = book_ref.shape[0] // subs
    words = book_ref.shape[1]
    lanes = 128
    for m in range(subs):
        band = pl.ds(m * width, width)
        tables = [book_ref[band, pl.ds(t * lanes, lanes)] for t in range(words // lanes)]
        for c in range(rows // lanes):
            cols = pl.ds(c * lanes, lanes)
            code = jnp.broadcast_to(codes_ref[pl.ds(m, 1), cols], (width, lanes))
            low = jnp.bitwise_and(code, lanes - 1)
            value = jnp.take_along_axis(tables[0], low, axis=1, mode="promise_in_bounds")
            for t in range(1, len(tables)):
                other = jnp.take_along_axis(tables[t], low, axis=1, mode="promise_in_bounds")
                value = jnp.where(code >= t * lanes, other, value)
            recon[band, cols] = value
    loads[2].wait()
    if dp is None:
        outs[0][...] = dot(recon[...].astype(bf16), res_ref[...])
        return
    cross[...] = dot(recon[...].astype(bf16), res_ref[...])
    place = lax.axis_index("dp")
    size = outs[0].shape[0]
    for k, out in enumerate(outs):
        at = pl.multiple_of(jnp.bitwise_xor(place, k) * size, size)
        out[...] = cross[pl.ds(at, size), :].astype(out.dtype)


def cross_partial(codes_t, book_t, residuals, dp):
    rows, dim = residuals.shape
    cols = book_t.shape[0]
    if dp is None:
        shapes = (jax.ShapeDtypeStruct((cols, dim), f32),)
    else:
        shapes = tuple(
            jax.ShapeDtypeStruct((cols // dp, dim), bf16 if k else f32) for k in range(dp)
        )
    return pl.pallas_call(
        functools.partial(cross_kernel, dp=dp),
        out_shape=shapes,
        in_specs=[pl.BlockSpec(memory_space=pl.ANY)] * 3,
        out_specs=(pl.BlockSpec(memory_space=pltpu.VMEM),) * len(shapes),
        scratch_shapes=[
            pltpu.VMEM(codes_t.shape, codes_t.dtype),
            pltpu.VMEM(book_t.shape, book_t.dtype),
            pltpu.VMEM(residuals.shape, residuals.dtype),
            pltpu.VMEM((cols, rows), f32),
            pltpu.VMEM((cols, dim), f32),
            pltpu.SemaphoreType.DMA((3,)),
        ],
        compiler_params=pltpu.CompilerParams(vmem_limit_bytes=60 * MIB),
        name="cross_partial",
    )(codes_t, book_t, residuals)


def polar_kernel(*refs, blocks, pieces, chunk):
    block_refs = refs[:blocks]
    res_hbm, codes_hbm, rotated_ref, sent_ref = refs[blocks : blocks + 4]
    raw, gram, gram_b, poly_b, iterate, iterate_b, rot_b, rot_t, sums_ref = refs[blocks + 4 : -3]
    res, codes_ref, sems = refs[-3:]
    dim = raw.shape[0]
    own = rot_b.shape[0]
    steps = dim // chunk
    loads = [
        pltpu.make_async_copy(res_hbm, res, sems.at[0]),
        pltpu.make_async_copy(codes_hbm, codes_ref, sems.at[1]),
    ]
    for load in loads:
        load.start()
    at = 0
    for block in block_refs:
        raw[pl.ds(at, block.shape[0]), :] = block[...]
        at += block.shape[0]

    def band_of(i):
        return pl.ds(pl.multiple_of(i * chunk, chunk), chunk)

    def gram_step(source, i):
        part = dot_nt(source[...], source[band_of(i), :])
        gram[:, band_of(i)] = part
        gram_b[:, band_of(i)] = part.astype(bf16)

    def trace_step(i, total):
        r = lax.broadcasted_iota(jnp.int32, (chunk, chunk), 0)
        c = lax.broadcasted_iota(jnp.int32, (chunk, chunk), 1)
        gram_step(raw, i)
        return total + jnp.sum(jnp.where(r == c, gram[band_of(i), band_of(i)], 0.0))

    frob = lax.fori_loop(0, steps, trace_step, jnp.zeros((), f32))
    scale2 = 1.0 / (frob + epsilon)
    scale = lax.rsqrt(frob + epsilon)

    def poly_step(i, wb, wc):
        cols = band_of(i)
        square = dot(gram_b[...], gram_b[:, cols])
        poly_b[:, cols] = (wb * gram[:, cols] + wc * square).astype(bf16)

    @pl.loop(0, steps)
    def _(i):
        poly_step(i, quintic_b * scale2, quintic_c * scale2 * scale2)

    @pl.loop(0, steps)
    def _(i):
        cols = band_of(i)
        value = scale * (quintic_a * raw[:, cols].astype(f32) + dot(poly_b[...], raw[:, cols]))
        iterate[:, cols] = value
        iterate_b[:, cols] = value.astype(bf16)

    @pl.loop(0, steps)
    def _(i):
        gram_step(iterate_b, i)

    @pl.loop(0, steps)
    def _(i):
        poly_step(i, quintic_b, quintic_c)

    @pl.loop(0, steps)
    def _(i):
        cols = band_of(i)
        value = quintic_a * iterate[:, cols] + dot(poly_b[...], iterate_b[:, cols])
        iterate[:, cols] = value
        raw[:, cols] = value.astype(bf16)

    mine = pl.ds(0, own)
    g = dot_nt(raw[mine, :], raw[...])
    image = dot(g.astype(bf16), raw[...])
    square = dot_nt(image.astype(bf16), raw[...])
    last = quintic_a * iterate[mine, :] + dot(
        (quintic_b * g + quintic_c * square).astype(bf16), raw[...]
    )
    size = own // pieces
    for p in range(pieces):
        to = 0
        if pieces > 1:
            to = pl.multiple_of(jnp.bitwise_xor(lax.axis_index("dp"), p) * size, size)
        rot_b[pl.ds(to, size), :] = last[p * size : (p + 1) * size, :].astype(bf16)

    for load in loads:
        load.wait()
    rows_all = res.shape[0]
    step = 256

    @pl.loop(0, rows_all // step)
    def _(i):
        rows = pl.ds(pl.multiple_of(i * step, step), step)
        part = dot_nt(res[rows, :], rot_b[...])
        rotated_ref[rows, :] = part
        rot_t[:, rows] = part.T

    subs = codes_ref.shape[0]
    words = sums_ref.shape[1]
    width = own // subs
    lows = 64
    highs = words // lows
    group = min(subs, 256 // lows)
    low_word = lax.broadcasted_iota(jnp.int32, (lows, rows_all), 0)
    high_word = lax.broadcasted_iota(jnp.int32, (8, rows_all), 0)
    for first in range(0, subs, group):
        onehots, values, marks = [], [], []
        for m in range(first, first + group):
            code = codes_ref[pl.ds(m, 1), :]
            low, high = jnp.bitwise_and(code, lows - 1), jnp.right_shift(code, 6)
            onehots.append(jnp.where(low_word == low, 1.0, 0.0).astype(bf16))
            band = rot_t[pl.ds(m * width, width), :]
            values += [jnp.where(high == h, band, 0.0) for h in range(highs)]
            marks.append(jnp.where(high_word == high, 1.0, 0.0))
        tall = jnp.concatenate(values + marks, axis=0).astype(bf16)
        part = dot_nt(tall, jnp.concatenate(onehots, axis=0))
        for s in range(group):
            m = first + s
            cols = slice(s * lows, (s + 1) * lows)
            for h in range(highs):
                to = pl.ds(h * lows, lows)
                at = (s * highs + h) * width
                sums_ref[pl.ds(m * width, width), to] = part[at : at + width, cols]
                at = group * highs * width + s * 8 + h
                sums_ref[pl.ds(own + m, 1), to] = part[at : at + 1, cols]
    sent_ref[...] = sums_ref[...].astype(bf16)


def polar(block_list, residuals, codes_t, own, words, pieces):
    rows, dim = residuals.shape
    subs = codes_t.shape[0]
    vmem = pl.BlockSpec(memory_space=pltpu.VMEM)
    chunk = 256
    kernel = functools.partial(polar_kernel, blocks=len(block_list), pieces=pieces, chunk=chunk)
    return pl.pallas_call(
        kernel,
        out_shape=(
            jax.ShapeDtypeStruct((rows, own), f32),
            jax.ShapeDtypeStruct((own + subs, words), bf16),
        ),
        in_specs=[vmem] * len(block_list)
        + [pl.BlockSpec(memory_space=pl.ANY)] * 2,
        out_specs=(vmem, vmem),
        scratch_shapes=[
            pltpu.VMEM((dim, dim), bf16),
            pltpu.VMEM((dim, dim), f32),
            pltpu.VMEM((dim, dim), bf16),
            pltpu.VMEM((dim, dim), bf16),
            pltpu.VMEM((dim, dim), f32),
            pltpu.VMEM((dim, dim), bf16),
            pltpu.VMEM((own, dim), bf16),
            pltpu.VMEM((own, rows), f32),
            pltpu.VMEM((own + subs, words), f32),
            pltpu.VMEM((rows, dim), bf16),
            pltpu.VMEM(codes_t.shape, codes_t.dtype),
            pltpu.SemaphoreType.DMA((2,)),
        ],
        compiler_params=pltpu.CompilerParams(vmem_limit_bytes=50 * MIB),
        name="polar",
    )(*block_list, residuals, codes_t)


def share_kernel(*refs):
    total = refs[0][...].astype(f32)
    for part in refs[1:-1]:
        total = total + part[...].astype(f32)
    refs[-1][...] = total.astype(refs[-1].dtype)


def book_kernel(book_ref, *refs):
    sums, out_ref = refs[:-1], refs[-1]
    own = book_ref.shape[0]
    subs = sums[0].shape[0] - own
    width = own // subs
    total = sums[0][...].astype(f32)
    for part in sums[1:]:
        total = total + part[...].astype(f32)
    for m in range(subs):
        band = pl.ds(m * width, width)
        count = total[own + m : own + m + 1, :] + prior_weight
        part = total[m * width : (m + 1) * width, :]
        out_ref[band, :] = (part + prior_weight * book_ref[band, :]) / count


def small_call(kernel, name, shape, dtype, *operands):
    vmem = pl.BlockSpec(memory_space=pltpu.VMEM)
    return pl.pallas_call(
        kernel,
        out_shape=jax.ShapeDtypeStruct(shape, dtype),
        in_specs=[vmem] * len(operands),
        out_specs=vmem,
        compiler_params=pltpu.CompilerParams(vmem_limit_bytes=16 * MIB),
        name=name,
    )(*operands)


def swap(value, axis, size, mask, odd_mask=None):
    odd_mask = mask if odd_mask is None else odd_mask
    return lax.ppermute(value, axis, [(i, i ^ (odd_mask if i % 2 else mask)) for i in range(size)])


def make_body(dp, code):
    def body(residuals, codes, codebook):
        rows, dim = residuals.shape
        subs, words, width = codebook.shape
        own = subs * width
        codes_t = codes.T
        book_t = jnp.transpose(codebook, (0, 2, 1)).reshape(own, words)
        size = own // dp
        thin = size % 16 != 0
        if thin:
            place = lax.axis_index("dp")
            (partial,) = cross_partial(codes_t, book_t, residuals, None)
            cut = [
                lax.dynamic_slice_in_dim(partial, (place ^ k) * size, size, 0) for k in range(dp)
            ]
            parts = [cut[0]] + [part.astype(bf16) for part in cut[1:]]
        else:
            parts = cross_partial(codes_t, book_t, residuals, dp)
        far_first = range(dp - 1, 0, -1)
        got = [swap(parts[k], "dp", dp, k) for k in far_first]
        piece = small_call(share_kernel, "share", (size, dim), bf16, parts[0], *got)
        pieces = {0: piece}
        for k in far_first:
            pieces[k] = swap(piece, "dp", dp, k)
        if thin:
            block = jnp.zeros((own, dim), bf16)
            for k in range(dp):
                block = lax.dynamic_update_slice_in_dim(block, pieces[k], (place ^ k) * size, 0)
            held = [block]
        else:
            half = max(dp // 2, 1)
            held = [
                jnp.concatenate([pieces[k] for k in range(at, min(at + half, dp))], axis=0)
                for at in range(0, dp, half)
            ]
        strides = [1 << b for b in reversed(range(code.bit_length() - 1))]
        far = strides[:-1]
        for even, odd in zip(far, far[::-1]):
            held = held + [swap(t, "code", code, even, odd) for t in held]
        for stride in strides[-1:]:
            held = held + [swap(t, "code", code, stride) for t in held]
        rotated, sums = polar(held, residuals, codes_t, own, words, 1 if thin else dp)
        others = [swap(sums, "dp", dp, k) for k in far_first]
        book = small_call(book_kernel, "book", (own, words), f32, book_t, sums, *others)
        return rotated, jnp.transpose(book.reshape(subs, width, words), (0, 2, 1))

    return body


def solution(mesh):
    dp, code = mesh.shape["dp"], mesh.shape["code"]
    in_specs = (P("dp", None), P("dp", "code"), P("code", None, None))
    out_specs = (P("dp", "code"), P("code", None, None))
    return jax.shard_map(
        make_body(dp, code), mesh=mesh, in_specs=in_specs, out_specs=out_specs, check_vma=False
    )
```

```python
import functools

import jax
import jax.numpy as jnp
from jax import lax
from jax.experimental import pallas as pl
from jax.experimental.pallas import tpu as pltpu
from jax.sharding import PartitionSpec as P

quintic_a = 3.4445
quintic_b = -4.775
quintic_c = 2.0315
prior_weight = 8.0
epsilon = 1e-06
f32, bf16 = jnp.float32, jnp.bfloat16
MIB = 1024 * 1024
NT = (((1,), (1,)), ((), ()))


def dot(left, right):
    return jnp.dot(left, right, preferred_element_type=f32)


def dot_nt(left, right):
    return lax.dot_general(left, right, NT, preferred_element_type=f32)


def cross_kernel(codes_hbm, book_hbm, res_hbm, *refs, dp):
    outs = refs[: dp or 1]
    codes_ref, book_ref, res_ref, recon, cross, sems = refs[dp or 1 :]
    loads = [
        pltpu.make_async_copy(codes_hbm, codes_ref, sems.at[0]),
        pltpu.make_async_copy(book_hbm, book_ref, sems.at[1]),
        pltpu.make_async_copy(res_hbm, res_ref, sems.at[2]),
    ]
    for load in loads:
        load.start()
    loads[0].wait()
    loads[1].wait()
    subs, rows = codes_ref.shape
    width = book_ref.shape[0] // subs
    words = book_ref.shape[1]
    lanes = 128
    for m in range(subs):
        band = pl.ds(m * width, width)
        tables = [book_ref[band, pl.ds(t * lanes, lanes)] for t in range(words // lanes)]
        for c in range(rows // lanes):
            cols = pl.ds(c * lanes, lanes)
            code = jnp.broadcast_to(codes_ref[pl.ds(m, 1), cols], (width, lanes))
            low = jnp.bitwise_and(code, lanes - 1)
            value = jnp.take_along_axis(tables[0], low, axis=1, mode="promise_in_bounds")
            for t in range(1, len(tables)):
                other = jnp.take_along_axis(tables[t], low, axis=1, mode="promise_in_bounds")
                value = jnp.where(code >= t * lanes, other, value)
            recon[band, cols] = value
    loads[2].wait()
    if dp is None:
        outs[0][...] = dot(recon[...].astype(bf16), res_ref[...])
        return
    cross[...] = dot(recon[...].astype(bf16), res_ref[...])
    place = lax.axis_index("dp")
    size = outs[0].shape[0]
    for k, out in enumerate(outs):
        at = pl.multiple_of(jnp.bitwise_xor(place, k) * size, size)
        out[...] = cross[pl.ds(at, size), :].astype(out.dtype)


def cross_partial(codes_t, book_t, residuals, dp):
    rows, dim = residuals.shape
    cols = book_t.shape[0]
    if dp is None:
        shapes = (jax.ShapeDtypeStruct((cols, dim), f32),)
    else:
        shapes = tuple(
            jax.ShapeDtypeStruct((cols // dp, dim), bf16 if k else f32) for k in range(dp)
        )
    shapes += tuple(jax.ShapeDtypeStruct(x.shape, x.dtype) for x in (codes_t, book_t, residuals))
    return pl.pallas_call(
        functools.partial(cross_kernel, dp=dp),
        out_shape=shapes,
        in_specs=[pl.BlockSpec(memory_space=pltpu.HBM)] * 3,
        out_specs=(pl.BlockSpec(memory_space=pltpu.VMEM),) * len(shapes),
        scratch_shapes=[
            pltpu.VMEM((cols, rows), f32),
            pltpu.VMEM((cols, dim), f32),
            pltpu.SemaphoreType.DMA((3,)),
        ],
        compiler_params=pltpu.CompilerParams(vmem_limit_bytes=24 * MIB),
        name="cross_partial",
    )(*[pltpu.with_memory_space_constraint(x, pltpu.HBM) for x in (codes_t, book_t, residuals)])


def polar_kernel(*refs, blocks, pieces, chunk):
    block_refs = refs[:blocks]
    rot_b = refs[blocks]
    raw, gram, gram_b, poly_b, iterate, iterate_b = refs[blocks + 1 :]
    dim = raw.shape[0]
    own = rot_b.shape[0]
    steps = dim // chunk
    at = 0
    for block in block_refs:
        raw[pl.ds(at, block.shape[0]), :] = block[...]
        at += block.shape[0]

    def band_of(i):
        return pl.ds(pl.multiple_of(i * chunk, chunk), chunk)

    def gram_step(source, i):
        part = dot_nt(source[...], source[band_of(i), :])
        gram[:, band_of(i)] = part
        gram_b[:, band_of(i)] = part.astype(bf16)

    def trace_step(i, total):
        r = lax.broadcasted_iota(jnp.int32, (chunk, chunk), 0)
        c = lax.broadcasted_iota(jnp.int32, (chunk, chunk), 1)
        gram_step(raw, i)
        return total + jnp.sum(jnp.where(r == c, gram[band_of(i), band_of(i)], 0.0))

    frob = lax.fori_loop(0, steps, trace_step, jnp.zeros((), f32))
    scale2 = 1.0 / (frob + epsilon)
    scale = lax.rsqrt(frob + epsilon)

    def poly_step(i, wb, wc):
        cols = band_of(i)
        square = dot(gram_b[...], gram_b[:, cols])
        poly_b[:, cols] = (wb * gram[:, cols] + wc * square).astype(bf16)

    @pl.loop(0, steps)
    def _(i):
        poly_step(i, quintic_b * scale2, quintic_c * scale2 * scale2)

    @pl.loop(0, steps)
    def _(i):
        cols = band_of(i)
        value = scale * (quintic_a * raw[:, cols].astype(f32) + dot(poly_b[...], raw[:, cols]))
        iterate[:, cols] = value
        iterate_b[:, cols] = value.astype(bf16)

    @pl.loop(0, steps)
    def _(i):
        gram_step(iterate_b, i)

    @pl.loop(0, steps)
    def _(i):
        poly_step(i, quintic_b, quintic_c)

    @pl.loop(0, steps)
    def _(i):
        cols = band_of(i)
        value = quintic_a * iterate[:, cols] + dot(poly_b[...], iterate_b[:, cols])
        iterate[:, cols] = value
        raw[:, cols] = value.astype(bf16)

    mine = pl.ds(0, own)
    g = dot_nt(raw[mine, :], raw[...])
    image = dot(g.astype(bf16), raw[...])
    square = dot_nt(image.astype(bf16), raw[...])
    last = quintic_a * iterate[mine, :] + dot(
        (quintic_b * g + quintic_c * square).astype(bf16), raw[...]
    )
    size = own // pieces
    for p in range(pieces):
        to = 0
        if pieces > 1:
            to = pl.multiple_of(jnp.bitwise_xor(lax.axis_index("dp"), p) * size, size)
        rot_b[pl.ds(to, size), :] = last[p * size : (p + 1) * size, :].astype(bf16)


def sums_kernel(rot_ref, res_ref, codes_ref, sent_ref, rot_t, sums_ref):
    own, rows_all = rot_t.shape
    step = 256

    @pl.loop(0, rows_all // step)
    def _(i):
        rows = pl.ds(pl.multiple_of(i * step, step), step)
        rot_t[:, rows] = dot_nt(rot_ref[...], res_ref[rows, :])

    subs = codes_ref.shape[0]
    words = sums_ref.shape[1]
    width = own // subs
    lows = 64
    highs = words // lows
    group = min(subs, 256 // lows)
    low_word = lax.broadcasted_iota(jnp.int32, (lows, rows_all), 0)
    high_word = lax.broadcasted_iota(jnp.int32, (8, rows_all), 0)
    for first in range(0, subs, group):
        onehots, values, marks = [], [], []
        for m in range(first, first + group):
            code = codes_ref[pl.ds(m, 1), :]
            low, high = jnp.bitwise_and(code, lows - 1), jnp.right_shift(code, 6)
            onehots.append(jnp.where(low_word == low, 1.0, 0.0).astype(bf16))
            band = rot_t[pl.ds(m * width, width), :]
            values += [jnp.where(high == h, band, 0.0) for h in range(highs)]
            marks.append(jnp.where(high_word == high, 1.0, 0.0))
        tall = jnp.concatenate(values + marks, axis=0).astype(bf16)
        part = dot_nt(tall, jnp.concatenate(onehots, axis=0))
        for s in range(group):
            m = first + s
            cols = slice(s * lows, (s + 1) * lows)
            for h in range(highs):
                to = pl.ds(h * lows, lows)
                at = (s * highs + h) * width
                sums_ref[pl.ds(m * width, width), to] = part[at : at + width, cols]
                at = group * highs * width + s * 8 + h
                sums_ref[pl.ds(own + m, 1), to] = part[at : at + 1, cols]
    sent_ref[...] = sums_ref[...].astype(bf16)


def rotated_kernel(rot_ref, res_ref, rotated_ref):
    rows_all = res_ref.shape[0]
    step = 512

    @pl.loop(0, rows_all // step)
    def _(i):
        rows = pl.ds(pl.multiple_of(i * step, step), step)
        rotated_ref[rows, :] = dot_nt(res_ref[rows, :], rot_ref[...])


def polar(block_list, own, pieces):
    dim = block_list[0].shape[1]
    vmem = pl.BlockSpec(memory_space=pltpu.VMEM)
    kernel = functools.partial(polar_kernel, blocks=len(block_list), pieces=pieces, chunk=256)
    return pl.pallas_call(
        kernel,
        out_shape=jax.ShapeDtypeStruct((own, dim), bf16),
        in_specs=[vmem] * len(block_list),
        out_specs=vmem,
        scratch_shapes=[
            pltpu.VMEM((dim, dim), bf16),
            pltpu.VMEM((dim, dim), f32),
            pltpu.VMEM((dim, dim), bf16),
            pltpu.VMEM((dim, dim), bf16),
            pltpu.VMEM((dim, dim), f32),
            pltpu.VMEM((dim, dim), bf16),
        ],
        compiler_params=pltpu.CompilerParams(vmem_limit_bytes=36 * MIB),
        name="polar",
    )(*block_list)


def share_kernel(*refs):
    total = refs[0][...].astype(f32)
    for part in refs[1:-1]:
        total = total + part[...].astype(f32)
    refs[-1][...] = total.astype(refs[-1].dtype)


def book_kernel(book_ref, *refs):
    sums, out_ref = refs[:-1], refs[-1]
    own = book_ref.shape[0]
    subs = sums[0].shape[0] - own
    width = own // subs
    total = sums[0][...].astype(f32)
    for part in sums[1:]:
        total = total + part[...].astype(f32)
    for m in range(subs):
        band = pl.ds(m * width, width)
        count = total[own + m : own + m + 1, :] + prior_weight
        part = total[m * width : (m + 1) * width, :]
        out_ref[band, :] = (part + prior_weight * book_ref[band, :]) / count


def small_call(kernel, name, shape, dtype, *operands, scratch=()):
    vmem = pl.BlockSpec(memory_space=pltpu.VMEM)
    return pl.pallas_call(
        kernel,
        out_shape=jax.ShapeDtypeStruct(shape, dtype),
        in_specs=[vmem] * len(operands),
        out_specs=vmem,
        scratch_shapes=scratch,
        compiler_params=pltpu.CompilerParams(vmem_limit_bytes=24 * MIB),
        name=name,
    )(*operands)


def swap(value, axis, size, mask, odd_mask=None):
    odd_mask = mask if odd_mask is None else odd_mask
    return lax.ppermute(value, axis, [(i, i ^ (odd_mask if i % 2 else mask)) for i in range(size)])


def make_body(dp, code):
    def body(residuals, codes, codebook):
        rows, dim = residuals.shape
        subs, words, width = codebook.shape
        own = subs * width
        codes_t = codes.T
        book_t = jnp.transpose(codebook, (0, 2, 1)).reshape(own, words)
        size = own // dp
        thin = size % 16 != 0
        if thin:
            place = lax.axis_index("dp")
            partial, codes_v, book_v, res_v = cross_partial(codes_t, book_t, residuals, None)
            cut = [
                lax.dynamic_slice_in_dim(partial, (place ^ k) * size, size, 0) for k in range(dp)
            ]
            parts = [cut[0]] + [part.astype(bf16) for part in cut[1:]]
        else:
            *parts, codes_v, book_v, res_v = cross_partial(codes_t, book_t, residuals, dp)
        far_first = range(dp - 1, 0, -1)
        got = [swap(parts[k], "dp", dp, k) for k in far_first]
        piece = small_call(share_kernel, "share", (size, dim), bf16, parts[0], *got)
        pieces = {0: piece}
        for k in far_first:
            pieces[k] = swap(piece, "dp", dp, k)
        if thin:
            block = jnp.zeros((own, dim), bf16)
            for k in range(dp):
                block = lax.dynamic_update_slice_in_dim(block, pieces[k], (place ^ k) * size, 0)
            held = [block]
        else:
            half = max(dp // 2, 1)
            held = [
                jnp.concatenate([pieces[k] for k in range(at, min(at + half, dp))], axis=0)
                for at in range(0, dp, half)
            ]
        strides = [1 << b for b in reversed(range(code.bit_length() - 1))]
        far = strides[:-1]
        for even, odd in zip(far, far[::-1]):
            held = held + [swap(t, "code", code, even, odd) for t in held]
        for stride in strides[-1:]:
            held = held + [swap(t, "code", code, stride) for t in held]
        rotation_t = polar(held, own, 1 if thin else dp)
        scratch = [pltpu.VMEM((own, rows), f32), pltpu.VMEM((own + subs, words), f32)]
        shape = (own + subs, words)
        sums = small_call(
            sums_kernel, "sums", shape, bf16, rotation_t, res_v, codes_v, scratch=scratch
        )
        rotated = small_call(rotated_kernel, "rotated", (rows, own), f32, rotation_t, res_v)
        others = [swap(sums, "dp", dp, k) for k in far_first]
        book = small_call(book_kernel, "book", (own, words), f32, book_v, sums, *others)
        return rotated, jnp.transpose(book.reshape(subs, width, words), (0, 2, 1))

    return body


def solution(mesh):
    dp, code = mesh.shape["dp"], mesh.shape["code"]
    in_specs = (P("dp", None), P("dp", "code"), P("code", None, None))
    out_specs = (P("dp", "code"), P("code", None, None))
    return jax.shard_map(
        make_body(dp, code), mesh=mesh, in_specs=in_specs, out_specs=out_specs, check_vma=False
    )
```

```python
import functools

import jax
import jax.numpy as jnp
from jax import lax
from jax.experimental import pallas as pl
from jax.experimental.pallas import tpu as pltpu
from jax.sharding import PartitionSpec as P

quintic_a = 3.4445
quintic_b = -4.775
quintic_c = 2.0315
prior_weight = 8.0
epsilon = 1e-06
f32, bf16 = jnp.float32, jnp.bfloat16
MIB = 1024 * 1024
NT = (((1,), (1,)), ((), ()))


def dot(left, right):
    return jnp.dot(left, right, preferred_element_type=f32)


def dot_nt(left, right):
    return lax.dot_general(left, right, NT, preferred_element_type=f32)


def cross_kernel(codes_hbm, book_hbm, res_hbm, *refs, dp):
    outs = refs[: dp or 1]
    codes_ref, book_ref, res_ref, recon, cross, sems = refs[dp or 1 :]
    loads = [
        pltpu.make_async_copy(codes_hbm, codes_ref, sems.at[0]),
        pltpu.make_async_copy(book_hbm, book_ref, sems.at[1]),
        pltpu.make_async_copy(res_hbm, res_ref, sems.at[2]),
    ]
    for load in loads:
        load.start()
    loads[0].wait()
    loads[1].wait()
    subs, rows = codes_ref.shape
    width = book_ref.shape[0] // subs
    words = book_ref.shape[1]
    lanes = 128
    for m in range(subs):
        band = pl.ds(m * width, width)
        tables = [book_ref[band, pl.ds(t * lanes, lanes)] for t in range(words // lanes)]
        for c in range(rows // lanes):
            cols = pl.ds(c * lanes, lanes)
            code = jnp.broadcast_to(codes_ref[pl.ds(m, 1), cols], (width, lanes))
            low = jnp.bitwise_and(code, lanes - 1)
            value = jnp.take_along_axis(tables[0], low, axis=1, mode="promise_in_bounds")
            for t in range(1, len(tables)):
                other = jnp.take_along_axis(tables[t], low, axis=1, mode="promise_in_bounds")
                value = jnp.where(code >= t * lanes, other, value)
            recon[band, cols] = value
    loads[2].wait()
    if dp is None:
        outs[0][...] = dot(recon[...].astype(bf16), res_ref[...])
        return
    cross[...] = dot(recon[...].astype(bf16), res_ref[...])
    place = lax.axis_index("dp")
    size = outs[0].shape[0]
    for k, out in enumerate(outs):
        at = pl.multiple_of(jnp.bitwise_xor(place, k) * size, size)
        out[...] = cross[pl.ds(at, size), :].astype(out.dtype)


def cross_partial(codes_t, book_t, residuals, dp):
    rows, dim = residuals.shape
    cols = book_t.shape[0]
    if dp is None:
        shapes = (jax.ShapeDtypeStruct((cols, dim), f32),)
    else:
        shapes = tuple(
            jax.ShapeDtypeStruct((cols // dp, dim), bf16 if k else f32) for k in range(dp)
        )
    shapes += tuple(jax.ShapeDtypeStruct(x.shape, x.dtype) for x in (codes_t, book_t, residuals))
    return pl.pallas_call(
        functools.partial(cross_kernel, dp=dp),
        out_shape=shapes,
        in_specs=[pl.BlockSpec(memory_space=pltpu.HBM)] * 3,
        out_specs=(pl.BlockSpec(memory_space=pltpu.VMEM),) * len(shapes),
        scratch_shapes=[
            pltpu.VMEM((cols, rows), f32),
            pltpu.VMEM((cols, dim), f32),
            pltpu.SemaphoreType.DMA((3,)),
        ],
        compiler_params=pltpu.CompilerParams(vmem_limit_bytes=24 * MIB),
        name="cross_partial",
    )(*[pltpu.with_memory_space_constraint(x, pltpu.HBM) for x in (codes_t, book_t, residuals)])


def polar_kernel(*refs, blocks, pieces, chunk):
    block_refs = refs[:blocks]
    rot_b = refs[blocks]
    raw, gram, gram_b, poly_b, iterate, iterate_b = refs[blocks + 1 :]
    dim = raw.shape[0]
    own = rot_b.shape[0]
    steps = dim // chunk
    at = 0
    for block in block_refs:
        raw[pl.ds(at, block.shape[0]), :] = block[...]
        at += block.shape[0]

    def band_of(i):
        return pl.ds(pl.multiple_of(i * chunk, chunk), chunk)

    def lower(j):
        return pl.ds(j * chunk, dim - j * chunk), pl.ds(j * chunk, chunk)

    def mirror(target, j, value):
        rows, cols = lower(j)
        target[rows, cols] = value.astype(bf16)
        for i in range(j + 1, steps):
            at = (i - j) * chunk
            target[cols, pl.ds(i * chunk, chunk)] = value[at : at + chunk, :].T.astype(bf16)

    def gram_of(source):
        r = lax.broadcasted_iota(jnp.int32, (chunk, chunk), 0)
        c = lax.broadcasted_iota(jnp.int32, (chunk, chunk), 1)
        trace = jnp.zeros((), f32)
        for j in range(steps):
            rows, cols = lower(j)
            part = dot_nt(source[rows, :], source[cols, :])
            gram[rows, cols] = part
            mirror(gram_b, j, part)
            trace = trace + jnp.sum(jnp.where(r == c, part[:chunk, :], 0.0))
        return trace

    def poly_of(wb, wc):
        for j in range(steps):
            rows, cols = lower(j)
            square = dot(gram_b[rows, :], gram_b[:, cols])
            mirror(poly_b, j, wb * gram[rows, cols] + wc * square)

    frob = gram_of(raw)
    scale2 = 1.0 / (frob + epsilon)
    scale = lax.rsqrt(frob + epsilon)
    poly_of(quintic_b * scale2, quintic_c * scale2 * scale2)

    @pl.loop(0, steps)
    def _(i):
        cols = band_of(i)
        value = scale * (quintic_a * raw[:, cols].astype(f32) + dot(poly_b[...], raw[:, cols]))
        iterate[:, cols] = value
        iterate_b[:, cols] = value.astype(bf16)

    gram_of(iterate_b)
    poly_of(quintic_b, quintic_c)

    @pl.loop(0, steps)
    def _(i):
        cols = band_of(i)
        value = quintic_a * iterate[:, cols] + dot(poly_b[...], iterate_b[:, cols])
        iterate[:, cols] = value
        raw[:, cols] = value.astype(bf16)

    mine = pl.ds(0, own)
    g = dot_nt(raw[mine, :], raw[...])
    image = dot(g.astype(bf16), raw[...])
    square = dot_nt(image.astype(bf16), raw[...])
    last = quintic_a * iterate[mine, :] + dot(
        (quintic_b * g + quintic_c * square).astype(bf16), raw[...]
    )
    size = own // pieces
    for p in range(pieces):
        to = 0
        if pieces > 1:
            to = pl.multiple_of(jnp.bitwise_xor(lax.axis_index("dp"), p) * size, size)
        rot_b[pl.ds(to, size), :] = last[p * size : (p + 1) * size, :].astype(bf16)


def sums_kernel(rot_ref, res_ref, codes_ref, sent_ref, rot_t, sums_ref):
    own, rows_all = rot_t.shape
    step = 256

    @pl.loop(0, rows_all // step)
    def _(i):
        rows = pl.ds(pl.multiple_of(i * step, step), step)
        rot_t[:, rows] = dot_nt(rot_ref[...], res_ref[rows, :])

    subs = codes_ref.shape[0]
    words = sums_ref.shape[1]
    width = own // subs
    lows = 64
    highs = words // lows
    group = min(subs, 256 // lows)
    low_word = lax.broadcasted_iota(jnp.int32, (lows, rows_all), 0)
    high_word = lax.broadcasted_iota(jnp.int32, (8, rows_all), 0)
    for first in range(0, subs, group):
        onehots, values, marks = [], [], []
        for m in range(first, first + group):
            code = codes_ref[pl.ds(m, 1), :]
            low, high = jnp.bitwise_and(code, lows - 1), jnp.right_shift(code, 6)
            onehots.append(jnp.where(low_word == low, 1.0, 0.0).astype(bf16))
            band = rot_t[pl.ds(m * width, width), :]
            values += [jnp.where(high == h, band, 0.0) for h in range(highs)]
            marks.append(jnp.where(high_word == high, 1.0, 0.0))
        tall = jnp.concatenate(values + marks, axis=0).astype(bf16)
        part = dot_nt(tall, jnp.concatenate(onehots, axis=0))
        for s in range(group):
            m = first + s
            cols = slice(s * lows, (s + 1) * lows)
            for h in range(highs):
                to = pl.ds(h * lows, lows)
                at = (s * highs + h) * width
                sums_ref[pl.ds(m * width, width), to] = part[at : at + width, cols]
                at = group * highs * width + s * 8 + h
                sums_ref[pl.ds(own + m, 1), to] = part[at : at + 1, cols]
    sent_ref[...] = sums_ref[...].astype(bf16)


def rotated_kernel(rot_ref, res_ref, rotated_ref):
    rows_all = res_ref.shape[0]
    step = 512

    @pl.loop(0, rows_all // step)
    def _(i):
        rows = pl.ds(pl.multiple_of(i * step, step), step)
        rotated_ref[rows, :] = dot_nt(res_ref[rows, :], rot_ref[...])


def polar(block_list, own, pieces):
    dim = block_list[0].shape[1]
    vmem = pl.BlockSpec(memory_space=pltpu.VMEM)
    kernel = functools.partial(polar_kernel, blocks=len(block_list), pieces=pieces, chunk=256)
    return pl.pallas_call(
        kernel,
        out_shape=jax.ShapeDtypeStruct((own, dim), bf16),
        in_specs=[vmem] * len(block_list),
        out_specs=vmem,
        scratch_shapes=[
            pltpu.VMEM((dim, dim), bf16),
            pltpu.VMEM((dim, dim), f32),
            pltpu.VMEM((dim, dim), bf16),
            pltpu.VMEM((dim, dim), bf16),
            pltpu.VMEM((dim, dim), f32),
            pltpu.VMEM((dim, dim), bf16),
        ],
        compiler_params=pltpu.CompilerParams(vmem_limit_bytes=36 * MIB),
        name="polar",
    )(*block_list)


def share_kernel(*refs):
    total = refs[0][...].astype(f32)
    for part in refs[1:-1]:
        total = total + part[...].astype(f32)
    refs[-1][...] = total.astype(refs[-1].dtype)


def book_kernel(book_ref, *refs):
    sums, out_ref = refs[:-1], refs[-1]
    own = book_ref.shape[0]
    subs = sums[0].shape[0] - own
    width = own // subs
    total = sums[0][...].astype(f32)
    for part in sums[1:]:
        total = total + part[...].astype(f32)
    for m in range(subs):
        band = pl.ds(m * width, width)
        count = total[own + m : own + m + 1, :] + prior_weight
        part = total[m * width : (m + 1) * width, :]
        out_ref[band, :] = (part + prior_weight * book_ref[band, :]) / count


def small_call(kernel, name, shape, dtype, *operands, scratch=()):
    vmem = pl.BlockSpec(memory_space=pltpu.VMEM)
    return pl.pallas_call(
        kernel,
        out_shape=jax.ShapeDtypeStruct(shape, dtype),
        in_specs=[vmem] * len(operands),
        out_specs=vmem,
        scratch_shapes=scratch,
        compiler_params=pltpu.CompilerParams(vmem_limit_bytes=24 * MIB),
        name=name,
    )(*operands)


def swap(value, axis, size, mask, odd_mask=None):
    odd_mask = mask if odd_mask is None else odd_mask
    return lax.ppermute(value, axis, [(i, i ^ (odd_mask if i % 2 else mask)) for i in range(size)])


def make_body(dp, code):
    def body(residuals, codes, codebook):
        rows, dim = residuals.shape
        subs, words, width = codebook.shape
        own = subs * width
        codes_t = codes.T
        book_t = jnp.transpose(codebook, (0, 2, 1)).reshape(own, words)
        size = own // dp
        thin = size % 16 != 0
        if thin:
            place = lax.axis_index("dp")
            partial, codes_v, book_v, res_v = cross_partial(codes_t, book_t, residuals, None)
            cut = [
                lax.dynamic_slice_in_dim(partial, (place ^ k) * size, size, 0) for k in range(dp)
            ]
            parts = [cut[0]] + [part.astype(bf16) for part in cut[1:]]
        else:
            *parts, codes_v, book_v, res_v = cross_partial(codes_t, book_t, residuals, dp)
        far_first = range(dp - 1, 0, -1)
        got = [swap(parts[k], "dp", dp, k) for k in far_first]
        piece = small_call(share_kernel, "share", (size, dim), bf16, parts[0], *got)
        pieces = {0: piece}
        for k in far_first:
            pieces[k] = swap(piece, "dp", dp, k)
        if thin:
            block = jnp.zeros((own, dim), bf16)
            for k in range(dp):
                block = lax.dynamic_update_slice_in_dim(block, pieces[k], (place ^ k) * size, 0)
            held = [block]
        else:
            half = max(dp // 2, 1)
            held = [
                jnp.concatenate([pieces[k] for k in range(at, min(at + half, dp))], axis=0)
                for at in range(0, dp, half)
            ]
        strides = [1 << b for b in reversed(range(code.bit_length() - 1))]
        far = strides[:-1]
        for even, odd in zip(far, far[::-1]):
            held = held + [swap(t, "code", code, even, odd) for t in held]
        for stride in strides[-1:]:
            held = held + [swap(t, "code", code, stride) for t in held]
        rotation_t = polar(held, own, 1 if thin else dp)
        scratch = [pltpu.VMEM((own, rows), f32), pltpu.VMEM((own + subs, words), f32)]
        shape = (own + subs, words)
        sums = small_call(
            sums_kernel, "sums", shape, bf16, rotation_t, res_v, codes_v, scratch=scratch
        )
        rotated = small_call(rotated_kernel, "rotated", (rows, own), f32, rotation_t, res_v)
        others = [swap(sums, "dp", dp, k) for k in far_first]
        book = small_call(book_kernel, "book", (own, words), f32, book_v, sums, *others)
        return rotated, jnp.transpose(book.reshape(subs, width, words), (0, 2, 1))

    return body


def solution(mesh):
    dp, code = mesh.shape["dp"], mesh.shape["code"]
    in_specs = (P("dp", None), P("dp", "code"), P("code", None, None))
    out_specs = (P("dp", "code"), P("code", None, None))
    return jax.shard_map(
        make_body(dp, code), mesh=mesh, in_specs=in_specs, out_specs=out_specs, check_vma=False
    )
```

```python
import functools

import jax
import jax.numpy as jnp
from jax import lax
from jax.experimental import pallas as pl
from jax.experimental.pallas import tpu as pltpu
from jax.sharding import PartitionSpec as P

quintic_a = 3.4445
quintic_b = -4.775
quintic_c = 2.0315
prior_weight = 8.0
epsilon = 1e-06
f32, bf16 = jnp.float32, jnp.bfloat16
MIB = 1024 * 1024
NT = (((1,), (1,)), ((), ()))


def dot(left, right):
    return jnp.dot(left, right, preferred_element_type=f32)


def dot_nt(left, right):
    return lax.dot_general(left, right, NT, preferred_element_type=f32)


def cross_kernel(codes_hbm, book_hbm, res_hbm, *refs, dp):
    outs = refs[: dp or 1]
    codes_ref, book_ref, res_ref, recon, cross, sems = refs[dp or 1 :]
    loads = [
        pltpu.make_async_copy(codes_hbm, codes_ref, sems.at[0]),
        pltpu.make_async_copy(book_hbm, book_ref, sems.at[1]),
        pltpu.make_async_copy(res_hbm, res_ref, sems.at[2]),
    ]
    for load in loads:
        load.start()
    loads[0].wait()
    loads[1].wait()
    subs, rows = codes_ref.shape
    width = book_ref.shape[0] // subs
    words = book_ref.shape[1]
    lanes = 128
    for m in range(subs):
        band = pl.ds(m * width, width)
        tables = [book_ref[band, pl.ds(t * lanes, lanes)] for t in range(words // lanes)]
        for c in range(rows // lanes):
            cols = pl.ds(c * lanes, lanes)
            code = jnp.broadcast_to(codes_ref[pl.ds(m, 1), cols], (width, lanes))
            low = jnp.bitwise_and(code, lanes - 1)
            value = jnp.take_along_axis(tables[0], low, axis=1, mode="promise_in_bounds")
            for t in range(1, len(tables)):
                other = jnp.take_along_axis(tables[t], low, axis=1, mode="promise_in_bounds")
                value = jnp.where(code >= t * lanes, other, value)
            recon[band, cols] = value
    loads[2].wait()
    if dp is None:
        outs[0][...] = dot(recon[...].astype(bf16), res_ref[...])
        return
    cross[...] = dot(recon[...].astype(bf16), res_ref[...])
    place = lax.axis_index("dp")
    size = outs[0].shape[0]
    for k, out in enumerate(outs):
        at = pl.multiple_of(jnp.bitwise_xor(place, k) * size, size)
        out[...] = cross[pl.ds(at, size), :].astype(out.dtype)


def cross_partial(codes_t, book_t, residuals, dp):
    rows, dim = residuals.shape
    cols = book_t.shape[0]
    if dp is None:
        shapes = (jax.ShapeDtypeStruct((cols, dim), f32),)
    else:
        shapes = tuple(
            jax.ShapeDtypeStruct((cols // dp, dim), bf16 if k else f32) for k in range(dp)
        )
    shapes += tuple(jax.ShapeDtypeStruct(x.shape, x.dtype) for x in (codes_t, book_t, residuals))
    return pl.pallas_call(
        functools.partial(cross_kernel, dp=dp),
        out_shape=shapes,
        in_specs=[pl.BlockSpec(memory_space=pltpu.HBM)] * 3,
        out_specs=(pl.BlockSpec(memory_space=pltpu.VMEM),) * len(shapes),
        scratch_shapes=[
            pltpu.VMEM((cols, rows), f32),
            pltpu.VMEM((cols, dim), f32),
            pltpu.SemaphoreType.DMA((3,)),
        ],
        compiler_params=pltpu.CompilerParams(vmem_limit_bytes=24 * MIB),
        name="cross_partial",
    )(*[pltpu.with_memory_space_constraint(x, pltpu.HBM) for x in (codes_t, book_t, residuals)])


def polar_kernel(*refs, blocks, pieces, chunk):
    block_refs = refs[:blocks]
    rot_b = refs[blocks]
    raw, gram, gram_b, poly_b, iterate, iterate_b = refs[blocks + 1 :]
    dim = raw.shape[0]
    own = rot_b.shape[0]
    steps = dim // chunk
    at = 0
    for block in block_refs:
        raw[pl.ds(at, block.shape[0]), :] = block[...]
        at += block.shape[0]

    def band_of(i):
        return pl.ds(i * chunk, chunk)

    def lower(j):
        return pl.ds(j * chunk, dim - j * chunk), pl.ds(j * chunk, chunk)

    def mirror(target, j, value):
        rows, cols = lower(j)
        target[rows, cols] = value.astype(bf16)
        for i in range(j + 1, steps):
            at = (i - j) * chunk
            target[cols, pl.ds(i * chunk, chunk)] = value[at : at + chunk, :].T.astype(bf16)

    def gram_of(source):
        r = lax.broadcasted_iota(jnp.int32, (chunk, chunk), 0)
        c = lax.broadcasted_iota(jnp.int32, (chunk, chunk), 1)
        trace = jnp.zeros((), f32)
        for j in range(steps):
            rows, cols = lower(j)
            part = dot_nt(source[rows, :], source[cols, :])
            gram[rows, cols] = part
            mirror(gram_b, j, part)
            trace = trace + jnp.sum(jnp.where(r == c, part[:chunk, :], 0.0))
        return trace

    def poly_of(wb, wc):
        for j in range(steps):
            rows, cols = lower(j)
            square = dot(gram_b[rows, :], gram_b[:, cols])
            mirror(poly_b, j, wb * gram[rows, cols] + wc * square)

    frob = gram_of(raw)
    scale2 = 1.0 / (frob + epsilon)
    scale = lax.rsqrt(frob + epsilon)
    poly_of(quintic_b * scale2, quintic_c * scale2 * scale2)

    for i in range(steps):
        cols = band_of(i)
        value = scale * (quintic_a * raw[:, cols].astype(f32) + dot(poly_b[...], raw[:, cols]))
        iterate[:, cols] = value
        iterate_b[:, cols] = value.astype(bf16)

    gram_of(iterate_b)
    poly_of(quintic_b, quintic_c)

    for i in range(steps):
        cols = band_of(i)
        value = quintic_a * iterate[:, cols] + dot(poly_b[...], iterate_b[:, cols])
        iterate[:, cols] = value
        raw[:, cols] = value.astype(bf16)

    mine = pl.ds(0, own)
    g = dot_nt(raw[mine, :], raw[...])
    image = dot(g.astype(bf16), raw[...])
    square = dot_nt(image.astype(bf16), raw[...])
    last = quintic_a * iterate[mine, :] + dot(
        (quintic_b * g + quintic_c * square).astype(bf16), raw[...]
    )
    size = own // pieces
    for p in range(pieces):
        to = 0
        if pieces > 1:
            to = pl.multiple_of(jnp.bitwise_xor(lax.axis_index("dp"), p) * size, size)
        rot_b[pl.ds(to, size), :] = last[p * size : (p + 1) * size, :].astype(bf16)


LOWS = 64


def onehot_kernel(codes_ref, onehot_ref, counts_ref):
    subs, rows_all = codes_ref.shape
    highs = counts_ref.shape[1] // LOWS
    low_word = lax.broadcasted_iota(jnp.int32, (LOWS, rows_all), 0)
    high_word = lax.broadcasted_iota(jnp.int32, (8, rows_all), 0)
    for m in range(subs):
        code = codes_ref[pl.ds(m, 1), :]
        low, high = jnp.bitwise_and(code, LOWS - 1), jnp.right_shift(code, 6)
        onehot = jnp.where(low_word == low, 1.0, 0.0).astype(bf16)
        onehot_ref[pl.ds(m * LOWS, LOWS), :] = onehot
        part = dot_nt(jnp.where(high_word == high, 1.0, 0.0).astype(bf16), onehot)
        for h in range(highs):
            counts_ref[pl.ds(m, 1), pl.ds(h * LOWS, LOWS)] = part[h : h + 1, :]


def onehot_call(codes_t, words):
    subs, rows = codes_t.shape
    vmem = pl.BlockSpec(memory_space=pltpu.VMEM)
    return pl.pallas_call(
        onehot_kernel,
        out_shape=(
            jax.ShapeDtypeStruct((subs * LOWS, rows), bf16),
            jax.ShapeDtypeStruct((subs, words), f32),
        ),
        in_specs=[vmem],
        out_specs=(vmem, vmem),
        compiler_params=pltpu.CompilerParams(vmem_limit_bytes=24 * MIB),
        cost_estimate=pl.CostEstimate(
            flops=2 * 256 * subs * LOWS * rows, bytes_accessed=2 * subs * LOWS * rows, transcendentals=0
        ),
        name="onehot",
    )(codes_t)


def sums_kernel(rot_ref, res_ref, codes_ref, onehot_ref, counts_ref, sent_ref, sums_ref):
    subs, rows_all = codes_ref.shape
    own = rot_ref.shape[0]
    words = counts_ref.shape[1]
    width = own // subs
    highs = words // LOWS
    group = min(subs, 256 // LOWS)
    rot_t = dot_nt(rot_ref[...], res_ref[...])
    for first in range(0, subs, group):
        values = []
        for m in range(first, first + group):
            high = jnp.right_shift(codes_ref[pl.ds(m, 1), :], 6)
            band = rot_t[m * width : (m + 1) * width, :]
            values += [jnp.where(high == h, band, 0.0) for h in range(highs)]
        tall = jnp.concatenate(values, axis=0).astype(bf16)
        part = dot_nt(tall, onehot_ref[pl.ds(first * LOWS, group * LOWS), :])
        for s in range(group):
            for h in range(highs):
                at = (s * highs + h) * width
                sums_ref[pl.ds((first + s) * width, width), pl.ds(h * LOWS, LOWS)] = part[
                    at : at + width, s * LOWS : (s + 1) * LOWS
                ]
    sent_ref[pl.ds(0, own), :] = sums_ref[...].astype(bf16)
    sent_ref[pl.ds(own, subs), :] = counts_ref[...].astype(bf16)


def rotated_kernel(rot_ref, res_ref, rotated_ref):
    rows_all = res_ref.shape[0]
    step = 512

    @pl.loop(0, rows_all // step)
    def _(i):
        rows = pl.ds(pl.multiple_of(i * step, step), step)
        rotated_ref[rows, :] = dot_nt(res_ref[rows, :], rot_ref[...])


def polar(block_list, own, pieces):
    dim = block_list[0].shape[1]
    vmem = pl.BlockSpec(memory_space=pltpu.VMEM)
    kernel = functools.partial(polar_kernel, blocks=len(block_list), pieces=pieces, chunk=256)
    return pl.pallas_call(
        kernel,
        out_shape=jax.ShapeDtypeStruct((own, dim), bf16),
        in_specs=[vmem] * len(block_list),
        out_specs=vmem,
        scratch_shapes=[
            pltpu.VMEM((dim, dim), bf16),
            pltpu.VMEM((dim, dim), f32),
            pltpu.VMEM((dim, dim), bf16),
            pltpu.VMEM((dim, dim), bf16),
            pltpu.VMEM((dim, dim), f32),
            pltpu.VMEM((dim, dim), bf16),
        ],
        compiler_params=pltpu.CompilerParams(vmem_limit_bytes=36 * MIB),
        name="polar",
    )(*block_list)


def share_kernel(*refs):
    total = refs[0][...].astype(f32)
    for part in refs[1:-1]:
        total = total + part[...].astype(f32)
    refs[-1][...] = total.astype(refs[-1].dtype)


def book_kernel(book_ref, *refs):
    sums, out_ref = refs[:-1], refs[-1]
    own = book_ref.shape[0]
    subs = sums[0].shape[0] - own
    width = own // subs
    total = sums[0][...].astype(f32)
    for part in sums[1:]:
        total = total + part[...].astype(f32)
    for m in range(subs):
        band = pl.ds(m * width, width)
        count = total[own + m : own + m + 1, :] + prior_weight
        part = total[m * width : (m + 1) * width, :]
        out_ref[band, :] = (part + prior_weight * book_ref[band, :]) / count


def small_call(kernel, name, shape, dtype, *operands, scratch=()):
    vmem = pl.BlockSpec(memory_space=pltpu.VMEM)
    return pl.pallas_call(
        kernel,
        out_shape=jax.ShapeDtypeStruct(shape, dtype),
        in_specs=[vmem] * len(operands),
        out_specs=vmem,
        scratch_shapes=scratch,
        compiler_params=pltpu.CompilerParams(vmem_limit_bytes=24 * MIB),
        name=name,
    )(*operands)


def swap(value, axis, size, mask, odd_mask=None):
    odd_mask = mask if odd_mask is None else odd_mask
    return lax.ppermute(value, axis, [(i, i ^ (odd_mask if i % 2 else mask)) for i in range(size)])


def make_body(dp, code):
    def body(residuals, codes, codebook):
        rows, dim = residuals.shape
        subs, words, width = codebook.shape
        own = subs * width
        codes_t = codes.T
        book_t = jnp.transpose(codebook, (0, 2, 1)).reshape(own, words)
        size = own // dp
        thin = size % 16 != 0
        if thin:
            place = lax.axis_index("dp")
            partial, codes_v, book_v, res_v = cross_partial(codes_t, book_t, residuals, None)
            cut = [
                lax.dynamic_slice_in_dim(partial, (place ^ k) * size, size, 0) for k in range(dp)
            ]
            parts = [cut[0]] + [part.astype(bf16) for part in cut[1:]]
        else:
            *parts, codes_v, book_v, res_v = cross_partial(codes_t, book_t, residuals, dp)
        far_first = range(dp - 1, 0, -1)
        got = [swap(parts[k], "dp", dp, k) for k in far_first]
        onehot, counts = onehot_call(codes_v, words)
        *got, onehot, counts = lax.optimization_barrier((*got, onehot, counts))
        piece = small_call(share_kernel, "share", (size, dim), bf16, parts[0], *got)
        pieces = {0: piece}
        for k in far_first:
            pieces[k] = swap(piece, "dp", dp, k)
        if thin:
            block = jnp.zeros((own, dim), bf16)
            for k in range(dp):
                block = lax.dynamic_update_slice_in_dim(block, pieces[k], (place ^ k) * size, 0)
            held = [block]
        else:
            held = [piece]
            if dp > 1:
                held.append(jnp.concatenate([pieces[k] for k in range(1, dp)], axis=0))
        strides = [1 << b for b in reversed(range(code.bit_length() - 1))]
        far, near = strides[:-1], strides[-1:]

        def spread(blocks, beside=()):
            for even, odd in zip(far, far[::-1]):
                new = [swap(t, "code", code, even, odd) for t in blocks]
                if beside:
                    new, beside = lax.optimization_barrier((new, list(beside)))
                blocks = blocks + new
            return blocks, list(beside)

        def across(block):
            return [swap(block, "code", code, stride) for stride in near]

        if held[1:]:
            first, _ = spread(held[:1])
            known = 1 + len(first) // 2
            early, rest = lax.optimization_barrier((first[:known], held[1]))
            crossed = across(jnp.concatenate(early, axis=0)) + across(rest)
            blocks, beside = spread([rest], first[known:] + crossed)
            late, crossed = beside[: len(first) - known], beside[len(first) - known :]
            held = [early[0], rest] + early[1:] + late + blocks[1:] + crossed
            held += [t for block in late + blocks[1:] for t in across(block)]
        else:
            held, _ = spread(held)
            held += [t for block in held for t in across(block)]
        rotation_t = polar(held, own, 1 if thin else dp)
        scratch = [pltpu.VMEM((own, words), f32)]
        operands = (rotation_t, res_v, codes_v, onehot, counts)
        sums = small_call(sums_kernel, "sums", (own + subs, words), bf16, *operands, scratch=scratch)
        rotated = small_call(rotated_kernel, "rotated", (rows, own), f32, rotation_t, res_v)
        others = [swap(sums, "dp", dp, k) for k in far_first]
        book = small_call(book_kernel, "book", (own, words), f32, book_v, sums, *others)
        return rotated, jnp.transpose(book.reshape(subs, width, words), (0, 2, 1))

    return body


def solution(mesh):
    dp, code = mesh.shape["dp"], mesh.shape["code"]
    in_specs = (P("dp", None), P("dp", "code"), P("code", None, None))
    out_specs = (P("dp", "code"), P("code", None, None))
    return jax.shard_map(
        make_body(dp, code), mesh=mesh, in_specs=in_specs, out_specs=out_specs, check_vma=False
    )
```

```python
import functools

import jax
import jax.numpy as jnp
from jax import lax
from jax.experimental import pallas as pl
from jax.experimental.pallas import tpu as pltpu
from jax.sharding import PartitionSpec as P

quintic_a = 3.4445
quintic_b = -4.775
quintic_c = 2.0315
prior_weight = 8.0
epsilon = 1e-06
f32, bf16 = jnp.float32, jnp.bfloat16
MIB = 1024 * 1024
NT = (((1,), (1,)), ((), ()))


def dot(left, right):
    return jnp.dot(left, right, preferred_element_type=f32)


def dot_nt(left, right):
    return lax.dot_general(left, right, NT, preferred_element_type=f32)


def cross_kernel(codes_hbm, book_hbm, res_hbm, *refs, dp):
    outs = refs[: dp or 1]
    codes_ref, book_ref, res_ref, recon, cross, sems = refs[dp or 1 :]
    loads = [
        pltpu.make_async_copy(codes_hbm, codes_ref, sems.at[0]),
        pltpu.make_async_copy(book_hbm, book_ref, sems.at[1]),
        pltpu.make_async_copy(res_hbm, res_ref, sems.at[2]),
    ]
    for load in loads:
        load.start()
    loads[0].wait()
    loads[1].wait()
    subs, rows = codes_ref.shape
    width = book_ref.shape[0] // subs
    words = book_ref.shape[1]
    lanes = 128
    for m in range(subs):
        band = pl.ds(m * width, width)
        tables = [book_ref[band, pl.ds(t * lanes, lanes)] for t in range(words // lanes)]
        for c in range(rows // lanes):
            cols = pl.ds(c * lanes, lanes)
            code = jnp.broadcast_to(codes_ref[pl.ds(m, 1), cols], (width, lanes))
            low = jnp.bitwise_and(code, lanes - 1)
            value = jnp.take_along_axis(tables[0], low, axis=1, mode="promise_in_bounds")
            for t in range(1, len(tables)):
                other = jnp.take_along_axis(tables[t], low, axis=1, mode="promise_in_bounds")
                value = jnp.where(code >= t * lanes, other, value)
            recon[band, cols] = value
    loads[2].wait()
    if dp is None:
        outs[0][...] = dot(recon[...].astype(bf16), res_ref[...])
        return
    cross[...] = dot(recon[...].astype(bf16), res_ref[...])
    place = lax.axis_index("dp")
    size = outs[0].shape[0]
    for k, out in enumerate(outs):
        at = pl.multiple_of(jnp.bitwise_xor(place, k) * size, size)
        out[...] = cross[pl.ds(at, size), :].astype(out.dtype)


def cross_partial(codes_t, book_t, residuals, dp):
    rows, dim = residuals.shape
    cols = book_t.shape[0]
    if dp is None:
        shapes = (jax.ShapeDtypeStruct((cols, dim), f32),)
    else:
        shapes = tuple(
            jax.ShapeDtypeStruct((cols // dp, dim), bf16 if k else f32) for k in range(dp)
        )
    shapes += tuple(jax.ShapeDtypeStruct(x.shape, x.dtype) for x in (codes_t, book_t, residuals))
    return pl.pallas_call(
        functools.partial(cross_kernel, dp=dp),
        out_shape=shapes,
        in_specs=[pl.BlockSpec(memory_space=pltpu.HBM)] * 3,
        out_specs=(pl.BlockSpec(memory_space=pltpu.VMEM),) * len(shapes),
        scratch_shapes=[
            pltpu.VMEM((cols, rows), f32),
            pltpu.VMEM((cols, dim), f32),
            pltpu.SemaphoreType.DMA((3,)),
        ],
        compiler_params=pltpu.CompilerParams(vmem_limit_bytes=24 * MIB),
        name="cross_partial",
    )(*[pltpu.with_memory_space_constraint(x, pltpu.HBM) for x in (codes_t, book_t, residuals)])


def polar_kernel(*refs, blocks, pieces, chunk):
    block_refs = refs[:blocks]
    rot_b = refs[blocks]
    raw, gram, gram_b, poly_b, iterate, iterate_b = refs[blocks + 1 :]
    dim = raw.shape[0]
    own = rot_b.shape[0]
    steps = dim // chunk
    at = 0
    for block in block_refs:
        raw[pl.ds(at, block.shape[0]), :] = block[...]
        at += block.shape[0]

    def band_of(i):
        return pl.ds(i * chunk, chunk)

    def lower(j):
        return pl.ds(j * chunk, dim - j * chunk), pl.ds(j * chunk, chunk)

    def mirror(target, j, value):
        rows, cols = lower(j)
        target[rows, cols] = value.astype(bf16)
        for i in range(j + 1, steps):
            at = (i - j) * chunk
            target[cols, pl.ds(i * chunk, chunk)] = value[at : at + chunk, :].T.astype(bf16)

    def gram_of(source):
        r = lax.broadcasted_iota(jnp.int32, (chunk, chunk), 0)
        c = lax.broadcasted_iota(jnp.int32, (chunk, chunk), 1)
        trace = jnp.zeros((), f32)
        for j in range(steps):
            rows, cols = lower(j)
            part = dot_nt(source[rows, :], source[cols, :])
            gram[rows, cols] = part
            mirror(gram_b, j, part)
            trace = trace + jnp.sum(jnp.where(r == c, part[:chunk, :], 0.0))
        return trace

    def poly_of(wb, wc):
        for j in range(steps):
            rows, cols = lower(j)
            square = dot(gram_b[rows, :], gram_b[:, cols])
            mirror(poly_b, j, wb * gram[rows, cols] + wc * square)

    frob = gram_of(raw)
    scale2 = 1.0 / (frob + epsilon)
    scale = lax.rsqrt(frob + epsilon)
    poly_of(quintic_b * scale2, quintic_c * scale2 * scale2)

    for i in range(steps):
        cols = band_of(i)
        value = scale * (quintic_a * raw[:, cols].astype(f32) + dot(poly_b[...], raw[:, cols]))
        iterate[:, cols] = value
        iterate_b[:, cols] = value.astype(bf16)

    gram_of(iterate_b)
    poly_of(quintic_b, quintic_c)

    for i in range(steps):
        cols = band_of(i)
        value = quintic_a * iterate[:, cols] + dot(poly_b[...], iterate_b[:, cols])
        iterate[:, cols] = value
        raw[:, cols] = value.astype(bf16)

    mine = pl.ds(0, own)
    g = dot_nt(raw[mine, :], raw[...])
    image = dot(g.astype(bf16), raw[...])
    square = dot_nt(image.astype(bf16), raw[...])
    last = quintic_a * iterate[mine, :] + dot(
        (quintic_b * g + quintic_c * square).astype(bf16), raw[...]
    )
    size = own // pieces
    for p in range(pieces):
        to = 0
        if pieces > 1:
            to = pl.multiple_of(jnp.bitwise_xor(lax.axis_index("dp"), p) * size, size)
        rot_b[pl.ds(to, size), :] = last[p * size : (p + 1) * size, :].astype(bf16)


LOWS = 64


def onehot_kernel(codes_ref, onehot_ref, counts_ref):
    subs, rows_all = codes_ref.shape
    highs = counts_ref.shape[1] // LOWS
    low_word = lax.broadcasted_iota(jnp.int32, (LOWS, rows_all), 0)
    high_word = lax.broadcasted_iota(jnp.int32, (8, rows_all), 0)
    for m in range(subs):
        code = codes_ref[pl.ds(m, 1), :]
        low, high = jnp.bitwise_and(code, LOWS - 1), jnp.right_shift(code, 6)
        onehot = jnp.where(low_word == low, 1.0, 0.0).astype(bf16)
        onehot_ref[pl.ds(m * LOWS, LOWS), :] = onehot
        part = dot_nt(jnp.where(high_word == high, 1.0, 0.0).astype(bf16), onehot)
        for h in range(highs):
            counts_ref[pl.ds(m, 1), pl.ds(h * LOWS, LOWS)] = part[h : h + 1, :]


def onehot_call(codes_t, words):
    subs, rows = codes_t.shape
    vmem = pl.BlockSpec(memory_space=pltpu.VMEM)
    return pl.pallas_call(
        onehot_kernel,
        out_shape=(
            jax.ShapeDtypeStruct((subs * LOWS, rows), bf16),
            jax.ShapeDtypeStruct((subs, words), f32),
        ),
        in_specs=[vmem],
        out_specs=(vmem, vmem),
        compiler_params=pltpu.CompilerParams(vmem_limit_bytes=24 * MIB),
        cost_estimate=pl.CostEstimate(
            flops=2 * 256 * subs * LOWS * rows, bytes_accessed=2 * subs * LOWS * rows, transcendentals=0
        ),
        name="onehot",
    )(codes_t)


def sums_kernel(rot_ref, res_ref, codes_ref, onehot_ref, counts_ref, sent_ref, sums_ref):
    subs, rows_all = codes_ref.shape
    own = rot_ref.shape[0]
    words = counts_ref.shape[1]
    width = own // subs
    highs = words // LOWS
    group = min(subs, 256 // LOWS)
    rot_t = dot_nt(rot_ref[...], res_ref[...])
    for first in range(0, subs, group):
        values = []
        for m in range(first, first + group):
            high = jnp.right_shift(codes_ref[pl.ds(m, 1), :], 6)
            band = rot_t[m * width : (m + 1) * width, :]
            values += [jnp.where(high == h, band, 0.0) for h in range(highs)]
        tall = jnp.concatenate(values, axis=0).astype(bf16)
        part = dot_nt(tall, onehot_ref[pl.ds(first * LOWS, group * LOWS), :])
        for s in range(group):
            for h in range(highs):
                at = (s * highs + h) * width
                sums_ref[pl.ds((first + s) * width, width), pl.ds(h * LOWS, LOWS)] = part[
                    at : at + width, s * LOWS : (s + 1) * LOWS
                ]
    sent_ref[pl.ds(0, own), :] = sums_ref[...].astype(bf16)
    sent_ref[pl.ds(own, subs), :] = counts_ref[...].astype(bf16)


def rotated_kernel(rot_ref, res_ref, rotated_ref):
    rows_all = res_ref.shape[0]
    step = 512

    @pl.loop(0, rows_all // step)
    def _(i):
        rows = pl.ds(pl.multiple_of(i * step, step), step)
        rotated_ref[rows, :] = dot_nt(res_ref[rows, :], rot_ref[...])


def polar(block_list, own, pieces):
    dim = block_list[0].shape[1]
    vmem = pl.BlockSpec(memory_space=pltpu.VMEM)
    kernel = functools.partial(polar_kernel, blocks=len(block_list), pieces=pieces, chunk=256)
    return pl.pallas_call(
        kernel,
        out_shape=jax.ShapeDtypeStruct((own, dim), bf16),
        in_specs=[vmem] * len(block_list),
        out_specs=vmem,
        scratch_shapes=[
            pltpu.VMEM((dim, dim), bf16),
            pltpu.VMEM((dim, dim), f32),
            pltpu.VMEM((dim, dim), bf16),
            pltpu.VMEM((dim, dim), bf16),
            pltpu.VMEM((dim, dim), f32),
            pltpu.VMEM((dim, dim), bf16),
        ],
        compiler_params=pltpu.CompilerParams(vmem_limit_bytes=36 * MIB),
        name="polar",
    )(*block_list)


def share_kernel(*refs):
    total = refs[0][...].astype(f32)
    for part in refs[1:-1]:
        total = total + part[...].astype(f32)
    refs[-1][...] = total.astype(refs[-1].dtype)


def book_kernel(book_ref, *refs):
    sums, out_ref = refs[:-1], refs[-1]
    own = book_ref.shape[0]
    subs = sums[0].shape[0] - own
    width = own // subs
    total = sums[0][...].astype(f32)
    for part in sums[1:]:
        total = total + part[...].astype(f32)
    for m in range(subs):
        band = pl.ds(m * width, width)
        count = total[own + m : own + m + 1, :] + prior_weight
        part = total[m * width : (m + 1) * width, :]
        out_ref[band, :] = (part + prior_weight * book_ref[band, :]) / count


def small_call(kernel, name, shape, dtype, *operands, scratch=()):
    vmem = pl.BlockSpec(memory_space=pltpu.VMEM)
    return pl.pallas_call(
        kernel,
        out_shape=jax.ShapeDtypeStruct(shape, dtype),
        in_specs=[vmem] * len(operands),
        out_specs=vmem,
        scratch_shapes=scratch,
        compiler_params=pltpu.CompilerParams(vmem_limit_bytes=24 * MIB),
        name=name,
    )(*operands)


def swap(value, axis, size, mask, odd_mask=None):
    odd_mask = mask if odd_mask is None else odd_mask
    return lax.ppermute(value, axis, [(i, i ^ (odd_mask if i % 2 else mask)) for i in range(size)])


def make_body(dp, code):
    def body(residuals, codes, codebook):
        rows, dim = residuals.shape
        subs, words, width = codebook.shape
        own = subs * width
        codes_t = codes.T
        book_t = jnp.transpose(codebook, (0, 2, 1)).reshape(own, words)
        size = own // dp
        thin = size % 16 != 0
        if thin:
            place = lax.axis_index("dp")
            partial, codes_v, book_v, res_v = cross_partial(codes_t, book_t, residuals, None)
            cut = [
                lax.dynamic_slice_in_dim(partial, (place ^ k) * size, size, 0) for k in range(dp)
            ]
            parts = [cut[0]] + [part.astype(bf16) for part in cut[1:]]
        else:
            *parts, codes_v, book_v, res_v = cross_partial(codes_t, book_t, residuals, dp)
        far_first = range(dp - 1, 0, -1)
        got = [swap(parts[k], "dp", dp, k) for k in far_first]
        onehot, counts = onehot_call(codes_v, words)
        *got, onehot, counts = lax.optimization_barrier((*got, onehot, counts))
        piece = small_call(share_kernel, "share", (size, dim), bf16, parts[0], *got)
        pieces = {0: piece}
        for k in far_first:
            pieces[k] = swap(piece, "dp", dp, k)
        if thin:
            block = jnp.zeros((own, dim), bf16)
            for k in range(dp):
                block = lax.dynamic_update_slice_in_dim(block, pieces[k], (place ^ k) * size, 0)
            held = [block]
        else:
            half = max(dp // 2, 1)
            held = [
                jnp.concatenate([pieces[k] for k in range(at, min(at + half, dp))], axis=0)
                for at in range(0, dp, half)
            ]
        strides = [1 << b for b in reversed(range(code.bit_length() - 1))]
        far, near = strides[:-1], strides[-1:]
        others = []
        for block in held:
            have = [block]
            for even, odd in zip(far, far[::-1]):
                send = have[0] if len(have) == 1 else jnp.concatenate(have, axis=0)
                have.append(swap(send, "code", code, even, odd))
            for stride in near:
                early = have[:-1] or have
                crossed = [swap(jnp.concatenate(early, axis=0), "code", code, stride)]
                if have[1:]:
                    crossed.append(swap(have[-1], "code", code, stride))
                have += crossed
            others += have[1:]
        held += others
        rotation_t = polar(held, own, 1 if thin else dp)
        scratch = [pltpu.VMEM((own, words), f32)]
        operands = (rotation_t, res_v, codes_v, onehot, counts)
        sums = small_call(sums_kernel, "sums", (own + subs, words), bf16, *operands, scratch=scratch)
        rotated = small_call(rotated_kernel, "rotated", (rows, own), f32, rotation_t, res_v)
        others = [swap(sums, "dp", dp, k) for k in far_first]
        book = small_call(book_kernel, "book", (own, words), f32, book_v, sums, *others)
        return rotated, jnp.transpose(book.reshape(subs, width, words), (0, 2, 1))

    return body


def solution(mesh):
    dp, code = mesh.shape["dp"], mesh.shape["code"]
    in_specs = (P("dp", None), P("dp", "code"), P("code", None, None))
    out_specs = (P("dp", "code"), P("code", None, None))
    return jax.shard_map(
        make_body(dp, code), mesh=mesh, in_specs=in_specs, out_specs=out_specs, check_vma=False
    )
```

```python
import functools

import jax
import jax.numpy as jnp
from jax import lax
from jax.experimental import pallas as pl
from jax.experimental.pallas import tpu as pltpu
from jax.sharding import PartitionSpec as P

quintic_a = 3.4445
quintic_b = -4.775
quintic_c = 2.0315
prior_weight = 8.0
epsilon = 1e-06
f32, bf16 = jnp.float32, jnp.bfloat16
MIB = 1024 * 1024
NT = (((1,), (1,)), ((), ()))


def dot(left, right):
    return jnp.dot(left, right, preferred_element_type=f32)


def dot_nt(left, right):
    return lax.dot_general(left, right, NT, preferred_element_type=f32)


def cross_kernel(codes_hbm, book_hbm, res_hbm, *refs, dp):
    outs = refs[: dp or 1]
    codes_ref, book_ref, res_ref, recon, cross, sems = refs[dp or 1 :]
    loads = [
        pltpu.make_async_copy(codes_hbm, codes_ref, sems.at[0]),
        pltpu.make_async_copy(book_hbm, book_ref, sems.at[1]),
        pltpu.make_async_copy(res_hbm, res_ref, sems.at[2]),
    ]
    for load in loads:
        load.start()
    loads[0].wait()
    loads[1].wait()
    subs, rows = codes_ref.shape
    width = book_ref.shape[0] // subs
    words = book_ref.shape[1]
    lanes = 128
    for m in range(subs):
        band = pl.ds(m * width, width)
        tables = [book_ref[band, pl.ds(t * lanes, lanes)] for t in range(words // lanes)]
        for c in range(rows // lanes):
            cols = pl.ds(c * lanes, lanes)
            code = jnp.broadcast_to(codes_ref[pl.ds(m, 1), cols], (width, lanes))
            low = jnp.bitwise_and(code, lanes - 1)
            value = jnp.take_along_axis(tables[0], low, axis=1, mode="promise_in_bounds")
            for t in range(1, len(tables)):
                other = jnp.take_along_axis(tables[t], low, axis=1, mode="promise_in_bounds")
                value = jnp.where(code >= t * lanes, other, value)
            recon[band, cols] = value
    loads[2].wait()
    if dp is None:
        outs[0][...] = dot(recon[...].astype(bf16), res_ref[...])
        return
    cross[...] = dot(recon[...].astype(bf16), res_ref[...])
    place = lax.axis_index("dp")
    size = outs[0].shape[0]
    for k, out in enumerate(outs):
        at = pl.multiple_of(jnp.bitwise_xor(place, k) * size, size)
        out[...] = cross[pl.ds(at, size), :].astype(out.dtype)


def cross_partial(codes_t, book_t, residuals, dp):
    rows, dim = residuals.shape
    cols = book_t.shape[0]
    if dp is None:
        shapes = (jax.ShapeDtypeStruct((cols, dim), f32),)
    else:
        shapes = tuple(
            jax.ShapeDtypeStruct((cols // dp, dim), bf16 if k else f32) for k in range(dp)
        )
    shapes += tuple(jax.ShapeDtypeStruct(x.shape, x.dtype) for x in (codes_t, book_t, residuals))
    return pl.pallas_call(
        functools.partial(cross_kernel, dp=dp),
        out_shape=shapes,
        in_specs=[pl.BlockSpec(memory_space=pltpu.HBM)] * 3,
        out_specs=(pl.BlockSpec(memory_space=pltpu.VMEM),) * len(shapes),
        scratch_shapes=[
            pltpu.VMEM((cols, rows), f32),
            pltpu.VMEM((cols, dim), f32),
            pltpu.SemaphoreType.DMA((3,)),
        ],
        compiler_params=pltpu.CompilerParams(vmem_limit_bytes=24 * MIB),
        name="cross_partial",
    )(*[pltpu.with_memory_space_constraint(x, pltpu.HBM) for x in (codes_t, book_t, residuals)])


def polar_kernel(*refs, blocks, pieces, chunk):
    block_refs = refs[:blocks]
    rot_b = refs[blocks]
    raw, gram, gram_b, poly_b, iterate, iterate_b = refs[blocks + 1 :]
    dim = raw.shape[0]
    own = rot_b.shape[0]
    steps = dim // chunk
    at = 0
    for block in block_refs:
        raw[pl.ds(at, block.shape[0]), :] = block[...]
        at += block.shape[0]

    def band_of(i):
        return pl.ds(i * chunk, chunk)

    def lower(j):
        return pl.ds(j * chunk, dim - j * chunk), pl.ds(j * chunk, chunk)

    def mirror(target, j, value):
        rows, cols = lower(j)
        target[rows, cols] = value.astype(bf16)
        for i in range(j + 1, steps):
            at = (i - j) * chunk
            target[cols, pl.ds(i * chunk, chunk)] = value[at : at + chunk, :].T.astype(bf16)

    def gram_of(source):
        r = lax.broadcasted_iota(jnp.int32, (chunk, chunk), 0)
        c = lax.broadcasted_iota(jnp.int32, (chunk, chunk), 1)
        trace = jnp.zeros((), f32)
        for j in range(steps):
            rows, cols = lower(j)
            part = dot_nt(source[rows, :], source[cols, :])
            gram[rows, cols] = part
            mirror(gram_b, j, part)
            trace = trace + jnp.sum(jnp.where(r == c, part[:chunk, :], 0.0))
        return trace

    def poly_of(wb, wc):
        for j in range(steps):
            rows, cols = lower(j)
            square = dot(gram_b[rows, :], gram_b[:, cols])
            mirror(poly_b, j, wb * gram[rows, cols] + wc * square)

    frob = gram_of(raw)
    scale2 = 1.0 / (frob + epsilon)
    scale = lax.rsqrt(frob + epsilon)
    poly_of(quintic_b * scale2, quintic_c * scale2 * scale2)

    for i in range(steps):
        cols = band_of(i)
        value = scale * (quintic_a * raw[:, cols].astype(f32) + dot(poly_b[...], raw[:, cols]))
        iterate[:, cols] = value
        iterate_b[:, cols] = value.astype(bf16)

    gram_of(iterate_b)
    poly_of(quintic_b, quintic_c)

    for i in range(steps):
        cols = band_of(i)
        value = quintic_a * iterate[:, cols] + dot(poly_b[...], iterate_b[:, cols])
        iterate[pl.ds(0, own), cols] = value[:own, :]
        raw[:, cols] = value.astype(bf16)

    mine = pl.ds(0, own)
    g = dot_nt(raw[mine, :], raw[...])
    image = dot(g.astype(bf16), raw[...])
    square = dot_nt(image.astype(bf16), raw[...])
    last = quintic_a * iterate[mine, :] + dot(
        (quintic_b * g + quintic_c * square).astype(bf16), raw[...]
    )
    size = own // pieces
    for p in range(pieces):
        to = 0
        if pieces > 1:
            to = pl.multiple_of(jnp.bitwise_xor(lax.axis_index("dp"), p) * size, size)
        rot_b[pl.ds(to, size), :] = last[p * size : (p + 1) * size, :].astype(bf16)


LOWS = 64


def onehot_kernel(codes_ref, onehot_ref, counts_ref):
    subs, rows_all = codes_ref.shape
    highs = counts_ref.shape[1] // LOWS
    low_word = lax.broadcasted_iota(jnp.int32, (LOWS, rows_all), 0)
    high_word = lax.broadcasted_iota(jnp.int32, (8, rows_all), 0)
    for m in range(subs):
        code = codes_ref[pl.ds(m, 1), :]
        low, high = jnp.bitwise_and(code, LOWS - 1), jnp.right_shift(code, 6)
        onehot = jnp.where(low_word == low, 1.0, 0.0).astype(bf16)
        onehot_ref[pl.ds(m * LOWS, LOWS), :] = onehot
        part = dot_nt(jnp.where(high_word == high, 1.0, 0.0).astype(bf16), onehot)
        for h in range(highs):
            counts_ref[pl.ds(m, 1), pl.ds(h * LOWS, LOWS)] = part[h : h + 1, :]


def onehot_call(codes_t, words):
    subs, rows = codes_t.shape
    vmem = pl.BlockSpec(memory_space=pltpu.VMEM)
    return pl.pallas_call(
        onehot_kernel,
        out_shape=(
            jax.ShapeDtypeStruct((subs * LOWS, rows), bf16),
            jax.ShapeDtypeStruct((subs, words), f32),
        ),
        in_specs=[vmem],
        out_specs=(vmem, vmem),
        compiler_params=pltpu.CompilerParams(vmem_limit_bytes=24 * MIB),
        cost_estimate=pl.CostEstimate(
            flops=2 * 256 * subs * LOWS * rows, bytes_accessed=2 * subs * LOWS * rows, transcendentals=0
        ),
        name="onehot",
    )(codes_t)


def sums_kernel(rot_ref, res_ref, codes_ref, onehot_ref, counts_ref, sent_ref, sums_ref):
    subs, rows_all = codes_ref.shape
    own = rot_ref.shape[0]
    words = counts_ref.shape[1]
    width = own // subs
    highs = words // LOWS
    group = min(subs, 256 // LOWS)
    rot_t = dot_nt(rot_ref[...], res_ref[...])
    for first in range(0, subs, group):
        values = []
        for m in range(first, first + group):
            high = jnp.right_shift(codes_ref[pl.ds(m, 1), :], 6)
            band = rot_t[m * width : (m + 1) * width, :]
            values += [jnp.where(high == h, band, 0.0) for h in range(highs)]
        tall = jnp.concatenate(values, axis=0).astype(bf16)
        part = dot_nt(tall, onehot_ref[pl.ds(first * LOWS, group * LOWS), :])
        for s in range(group):
            for h in range(highs):
                at = (s * highs + h) * width
                sums_ref[pl.ds((first + s) * width, width), pl.ds(h * LOWS, LOWS)] = part[
                    at : at + width, s * LOWS : (s + 1) * LOWS
                ]
    sent_ref[pl.ds(0, own), :] = sums_ref[...].astype(bf16)
    sent_ref[pl.ds(own, subs), :] = counts_ref[...].astype(bf16)


def rotated_kernel(rot_ref, res_ref, rotated_ref):
    rows_all = res_ref.shape[0]
    step = 512

    @pl.loop(0, rows_all // step)
    def _(i):
        rows = pl.ds(pl.multiple_of(i * step, step), step)
        rotated_ref[rows, :] = dot_nt(res_ref[rows, :], rot_ref[...])


def polar(block_list, own, pieces):
    dim = block_list[0].shape[1]
    vmem = pl.BlockSpec(memory_space=pltpu.VMEM)
    kernel = functools.partial(polar_kernel, blocks=len(block_list), pieces=pieces, chunk=256)
    return pl.pallas_call(
        kernel,
        out_shape=jax.ShapeDtypeStruct((own, dim), bf16),
        in_specs=[vmem] * len(block_list),
        out_specs=vmem,
        scratch_shapes=[
            pltpu.VMEM((dim, dim), bf16),
            pltpu.VMEM((dim, dim), f32),
            pltpu.VMEM((dim, dim), bf16),
            pltpu.VMEM((dim, dim), bf16),
            pltpu.VMEM((dim, dim), f32),
            pltpu.VMEM((dim, dim), bf16),
        ],
        compiler_params=pltpu.CompilerParams(vmem_limit_bytes=36 * MIB),
        name="polar",
    )(*block_list)


def share_kernel(*refs):
    total = refs[0][...].astype(f32)
    for part in refs[1:-1]:
        total = total + part[...].astype(f32)
    refs[-1][...] = total.astype(refs[-1].dtype)


def book_kernel(book_ref, *refs):
    sums, out_ref = refs[:-1], refs[-1]
    own = book_ref.shape[0]
    subs = sums[0].shape[0] - own
    width = own // subs
    total = sums[0][...].astype(f32)
    for part in sums[1:]:
        total = total + part[...].astype(f32)
    for m in range(subs):
        band = pl.ds(m * width, width)
        count = total[own + m : own + m + 1, :] + prior_weight
        part = total[m * width : (m + 1) * width, :]
        out_ref[band, :] = (part + prior_weight * book_ref[band, :]) / count


def small_call(kernel, name, shape, dtype, *operands, scratch=()):
    vmem = pl.BlockSpec(memory_space=pltpu.VMEM)
    return pl.pallas_call(
        kernel,
        out_shape=jax.ShapeDtypeStruct(shape, dtype),
        in_specs=[vmem] * len(operands),
        out_specs=vmem,
        scratch_shapes=scratch,
        compiler_params=pltpu.CompilerParams(vmem_limit_bytes=24 * MIB),
        name=name,
    )(*operands)


def swap(value, axis, size, mask, odd_mask=None):
    odd_mask = mask if odd_mask is None else odd_mask
    return lax.ppermute(value, axis, [(i, i ^ (odd_mask if i % 2 else mask)) for i in range(size)])


def make_body(dp, code):
    def body(residuals, codes, codebook):
        rows, dim = residuals.shape
        subs, words, width = codebook.shape
        own = subs * width
        codes_t = codes.T
        book_t = jnp.transpose(codebook, (0, 2, 1)).reshape(own, words)
        size = own // dp
        thin = size % 16 != 0
        if thin:
            place = lax.axis_index("dp")
            partial, codes_v, book_v, res_v = cross_partial(codes_t, book_t, residuals, None)
            cut = [
                lax.dynamic_slice_in_dim(partial, (place ^ k) * size, size, 0) for k in range(dp)
            ]
            parts = [cut[0]] + [part.astype(bf16) for part in cut[1:]]
        else:
            *parts, codes_v, book_v, res_v = cross_partial(codes_t, book_t, residuals, dp)
        far_first = range(dp - 1, 0, -1)
        got = [swap(parts[k], "dp", dp, k) for k in far_first]
        onehot, counts = onehot_call(codes_v, words)
        *got, onehot, counts = lax.optimization_barrier((*got, onehot, counts))
        piece = small_call(share_kernel, "share", (size, dim), bf16, parts[0], *got)
        pieces = {0: piece}
        for k in far_first:
            pieces[k] = swap(piece, "dp", dp, k)
        if thin:
            block = jnp.zeros((own, dim), bf16)
            for k in range(dp):
                block = lax.dynamic_update_slice_in_dim(block, pieces[k], (place ^ k) * size, 0)
            held = [block]
        else:
            half = max(dp // 2, 1)
            held = [
                jnp.concatenate([pieces[k] for k in range(at, min(at + half, dp))], axis=0)
                for at in range(0, dp, half)
            ]
        strides = [1 << b for b in reversed(range(code.bit_length() - 1))]
        far = strides[:-1]
        for even, odd in zip(far, far[::-1]):
            held = held + [swap(t, "code", code, even, odd) for t in held]
        for stride in strides[-1:]:
            held = held + [swap(t, "code", code, stride) for t in held]
        rotation_t = polar(held, own, 1 if thin else dp)
        scratch = [pltpu.VMEM((own, words), f32)]
        operands = (rotation_t, res_v, codes_v, onehot, counts)
        sums = small_call(sums_kernel, "sums", (own + subs, words), bf16, *operands, scratch=scratch)
        rotated = small_call(rotated_kernel, "rotated", (rows, own), f32, rotation_t, res_v)
        others = [swap(sums, "dp", dp, k) for k in far_first]
        book = small_call(book_kernel, "book", (own, words), f32, book_v, sums, *others)
        return rotated, jnp.transpose(book.reshape(subs, width, words), (0, 2, 1))

    return body


def solution(mesh):
    dp, code = mesh.shape["dp"], mesh.shape["code"]
    in_specs = (P("dp", None), P("dp", "code"), P("code", None, None))
    out_specs = (P("dp", "code"), P("code", None, None))
    return jax.shard_map(
        make_body(dp, code), mesh=mesh, in_specs=in_specs, out_specs=out_specs, check_vma=False
    )
```

```python
import functools

import jax
import jax.numpy as jnp
from jax import lax
from jax.experimental import pallas as pl
from jax.experimental.pallas import tpu as pltpu
from jax.sharding import PartitionSpec as P

quintic_a = 3.4445
quintic_b = -4.775
quintic_c = 2.0315
prior_weight = 8.0
epsilon = 1e-06
f32, bf16 = jnp.float32, jnp.bfloat16
MIB = 1024 * 1024
NT = (((1,), (1,)), ((), ()))


def dot(left, right):
    return jnp.dot(left, right, preferred_element_type=f32)


def dot_nt(left, right):
    return lax.dot_general(left, right, NT, preferred_element_type=f32)


def cross_kernel(codes_hbm, book_hbm, res_hbm, *refs, dp):
    outs = refs[: dp or 1]
    codes_ref, book_ref, res_ref, recon, cross, sems = refs[dp or 1 :]
    loads = [
        pltpu.make_async_copy(codes_hbm, codes_ref, sems.at[0]),
        pltpu.make_async_copy(book_hbm, book_ref, sems.at[1]),
        pltpu.make_async_copy(res_hbm, res_ref, sems.at[2]),
    ]
    for load in loads:
        load.start()
    loads[0].wait()
    loads[1].wait()
    subs, rows = codes_ref.shape
    width = book_ref.shape[0] // subs
    words = book_ref.shape[1]
    lanes = 128
    for m in range(subs):
        band = pl.ds(m * width, width)
        tables = [book_ref[band, pl.ds(t * lanes, lanes)] for t in range(words // lanes)]
        for c in range(rows // lanes):
            cols = pl.ds(c * lanes, lanes)
            code = jnp.broadcast_to(codes_ref[pl.ds(m, 1), cols], (width, lanes))
            low = jnp.bitwise_and(code, lanes - 1)
            value = jnp.take_along_axis(tables[0], low, axis=1, mode="promise_in_bounds")
            for t in range(1, len(tables)):
                other = jnp.take_along_axis(tables[t], low, axis=1, mode="promise_in_bounds")
                value = jnp.where(code >= t * lanes, other, value)
            recon[band, cols] = value
    loads[2].wait()
    if dp is None:
        outs[0][...] = dot(recon[...].astype(bf16), res_ref[...])
        return
    cross[...] = dot(recon[...].astype(bf16), res_ref[...])
    place = lax.axis_index("dp")
    size = outs[0].shape[0]
    for k, out in enumerate(outs):
        at = pl.multiple_of(jnp.bitwise_xor(place, k) * size, size)
        out[...] = cross[pl.ds(at, size), :].astype(out.dtype)


def cross_partial(codes_t, book_t, residuals, dp):
    rows, dim = residuals.shape
    cols = book_t.shape[0]
    if dp is None:
        shapes = (jax.ShapeDtypeStruct((cols, dim), f32),)
    else:
        shapes = tuple(
            jax.ShapeDtypeStruct((cols // dp, dim), bf16 if k else f32) for k in range(dp)
        )
    shapes += tuple(jax.ShapeDtypeStruct(x.shape, x.dtype) for x in (codes_t, book_t, residuals))
    return pl.pallas_call(
        functools.partial(cross_kernel, dp=dp),
        out_shape=shapes,
        in_specs=[pl.BlockSpec(memory_space=pltpu.HBM)] * 3,
        out_specs=(pl.BlockSpec(memory_space=pltpu.VMEM),) * len(shapes),
        scratch_shapes=[
            pltpu.VMEM((cols, rows), f32),
            pltpu.VMEM((cols, dim), f32),
            pltpu.SemaphoreType.DMA((3,)),
        ],
        compiler_params=pltpu.CompilerParams(vmem_limit_bytes=24 * MIB),
        name="cross_partial",
    )(*[pltpu.with_memory_space_constraint(x, pltpu.HBM) for x in (codes_t, book_t, residuals)])


def polar_kernel(*refs, blocks, pieces, chunk):
    block_refs = refs[:blocks]
    rot_b = refs[blocks]
    raw, gram, gram_b, poly_b, iterate, iterate_b = refs[blocks + 1 :]
    dim = raw.shape[0]
    own = rot_b.shape[0]
    steps = dim // chunk
    at = 0
    for block in block_refs:
        raw[pl.ds(at, block.shape[0]), :] = block[...]
        at += block.shape[0]

    def band_of(i):
        return pl.ds(i * chunk, chunk)

    def lower(j):
        return pl.ds(j * chunk, dim - j * chunk), pl.ds(j * chunk, chunk)

    def mirror(target, j, value):
        rows, cols = lower(j)
        target[rows, cols] = value.astype(bf16)
        for i in range(j + 1, steps):
            at = (i - j) * chunk
            target[cols, pl.ds(i * chunk, chunk)] = value[at : at + chunk, :].T.astype(bf16)

    def gram_of(source):
        r = lax.broadcasted_iota(jnp.int32, (chunk, chunk), 0)
        c = lax.broadcasted_iota(jnp.int32, (chunk, chunk), 1)
        trace = jnp.zeros((), f32)
        for j in range(steps):
            rows, cols = lower(j)
            part = dot_nt(source[rows, :], source[cols, :])
            gram[rows, cols] = part
            mirror(gram_b, j, part)
            trace = trace + jnp.sum(jnp.where(r == c, part[:chunk, :], 0.0))
        return trace

    def poly_of(wb, wc):
        for j in range(steps):
            rows, cols = lower(j)
            square = dot(gram_b[rows, :], gram_b[:, cols])
            mirror(poly_b, j, wb * gram[rows, cols] + wc * square)

    frob = gram_of(raw)
    scale2 = 1.0 / (frob + epsilon)
    scale = lax.rsqrt(frob + epsilon)
    poly_of(quintic_b * scale2, quintic_c * scale2 * scale2)

    for i in range(steps):
        cols = band_of(i)
        value = scale * (quintic_a * raw[:, cols].astype(f32) + dot(poly_b[...], raw[:, cols]))
        iterate[:, cols] = value
        iterate_b[:, cols] = value.astype(bf16)

    gram_of(iterate_b)
    poly_of(quintic_b, quintic_c)

    for i in range(steps):
        cols = band_of(i)
        value = quintic_a * iterate[:, cols] + dot(poly_b[...], iterate_b[:, cols])
        iterate[pl.ds(0, own), cols] = value[:own, :]
        raw[:, cols] = value.astype(bf16)

    mine = pl.ds(0, own)
    g = dot_nt(raw[mine, :], raw[...])
    image = dot(g.astype(bf16), raw[...])
    square = dot_nt(image.astype(bf16), raw[...])
    last = quintic_a * iterate[mine, :] + dot(
        (quintic_b * g + quintic_c * square).astype(bf16), raw[...]
    )
    size = own // pieces
    for p in range(pieces):
        to = 0
        if pieces > 1:
            to = pl.multiple_of(jnp.bitwise_xor(lax.axis_index("dp"), p) * size, size)
        rot_b[pl.ds(to, size), :] = last[p * size : (p + 1) * size, :].astype(bf16)


LOWS = 64


def onehot_kernel(codes_ref, onehot_ref, counts_ref):
    subs, rows_all = codes_ref.shape
    highs = counts_ref.shape[1] // LOWS
    low_word = lax.broadcasted_iota(jnp.int32, (LOWS, rows_all), 0)
    high_word = lax.broadcasted_iota(jnp.int32, (8, rows_all), 0)
    for m in range(subs):
        code = codes_ref[pl.ds(m, 1), :]
        low, high = jnp.bitwise_and(code, LOWS - 1), jnp.right_shift(code, 6)
        onehot = jnp.where(low_word == low, 1.0, 0.0).astype(bf16)
        onehot_ref[pl.ds(m * LOWS, LOWS), :] = onehot
        part = dot_nt(jnp.where(high_word == high, 1.0, 0.0).astype(bf16), onehot)
        for h in range(highs):
            counts_ref[pl.ds(m, 1), pl.ds(h * LOWS, LOWS)] = part[h : h + 1, :]


def onehot_call(codes_t, words):
    subs, rows = codes_t.shape
    vmem = pl.BlockSpec(memory_space=pltpu.VMEM)
    return pl.pallas_call(
        onehot_kernel,
        out_shape=(
            jax.ShapeDtypeStruct((subs * LOWS, rows), bf16),
            jax.ShapeDtypeStruct((subs, words), f32),
        ),
        in_specs=[vmem],
        out_specs=(vmem, vmem),
        compiler_params=pltpu.CompilerParams(vmem_limit_bytes=24 * MIB),
        cost_estimate=pl.CostEstimate(
            flops=2 * 256 * subs * LOWS * rows, bytes_accessed=2 * subs * LOWS * rows, transcendentals=0
        ),
        name="onehot",
    )(codes_t)


def sums_kernel(rot_ref, res_ref, codes_ref, onehot_ref, counts_ref, sent_ref, sums_ref):
    subs, rows_all = codes_ref.shape
    own = rot_ref.shape[0]
    words = counts_ref.shape[1]
    width = own // subs
    highs = words // LOWS
    group = min(subs, 256 // LOWS)
    rot_t = dot_nt(rot_ref[...], res_ref[...])
    for first in range(0, subs, group):
        values = []
        for m in range(first, first + group):
            high = jnp.right_shift(codes_ref[pl.ds(m, 1), :], 6)
            band = rot_t[m * width : (m + 1) * width, :]
            values += [jnp.where(high == h, band, 0.0) for h in range(highs)]
        tall = jnp.concatenate(values, axis=0).astype(bf16)
        part = dot_nt(tall, onehot_ref[pl.ds(first * LOWS, group * LOWS), :])
        for s in range(group):
            for h in range(highs):
                at = (s * highs + h) * width
                sums_ref[pl.ds((first + s) * width, width), pl.ds(h * LOWS, LOWS)] = part[
                    at : at + width, s * LOWS : (s + 1) * LOWS
                ]
    sent_ref[pl.ds(0, own), :] = sums_ref[...].astype(bf16)
    sent_ref[pl.ds(own, subs), :] = counts_ref[...].astype(bf16)


def rotated_kernel(rot_ref, res_ref, rotated_ref):
    rows_all = res_ref.shape[0]
    step = 512

    @pl.loop(0, rows_all // step)
    def _(i):
        rows = pl.ds(pl.multiple_of(i * step, step), step)
        rotated_ref[rows, :] = dot_nt(res_ref[rows, :], rot_ref[...])


def polar(block_list, own, pieces):
    dim = block_list[0].shape[1]
    vmem = pl.BlockSpec(memory_space=pltpu.VMEM)
    kernel = functools.partial(polar_kernel, blocks=len(block_list), pieces=pieces, chunk=256)
    return pl.pallas_call(
        kernel,
        out_shape=jax.ShapeDtypeStruct((own, dim), bf16),
        in_specs=[vmem] * len(block_list),
        out_specs=vmem,
        scratch_shapes=[
            pltpu.VMEM((dim, dim), bf16),
            pltpu.VMEM((dim, dim), f32),
            pltpu.VMEM((dim, dim), bf16),
            pltpu.VMEM((dim, dim), bf16),
            pltpu.VMEM((dim, dim), f32),
            pltpu.VMEM((dim, dim), bf16),
        ],
        compiler_params=pltpu.CompilerParams(vmem_limit_bytes=36 * MIB),
        name="polar",
    )(*block_list)


def share_kernel(*refs):
    total = refs[0][...].astype(f32)
    for part in refs[1:-1]:
        total = total + part[...].astype(f32)
    refs[-1][...] = total.astype(refs[-1].dtype)


def book_kernel(book_ref, *refs):
    sums, out_ref = refs[:-1], refs[-1]
    own = book_ref.shape[0]
    subs = sums[0].shape[0] - own
    width = own // subs
    total = sums[0][...].astype(f32)
    for part in sums[1:]:
        total = total + part[...].astype(f32)
    for m in range(subs):
        band = pl.ds(m * width, width)
        count = total[own + m : own + m + 1, :] + prior_weight
        part = total[m * width : (m + 1) * width, :]
        out_ref[band, :] = (part + prior_weight * book_ref[band, :]) / count


def small_call(kernel, name, shape, dtype, *operands, scratch=()):
    vmem = pl.BlockSpec(memory_space=pltpu.VMEM)
    return pl.pallas_call(
        kernel,
        out_shape=jax.ShapeDtypeStruct(shape, dtype),
        in_specs=[vmem] * len(operands),
        out_specs=vmem,
        scratch_shapes=scratch,
        compiler_params=pltpu.CompilerParams(vmem_limit_bytes=24 * MIB),
        name=name,
    )(*operands)


def swap(value, axis, size, mask, odd_mask=None):
    odd_mask = mask if odd_mask is None else odd_mask
    return lax.ppermute(value, axis, [(i, i ^ (odd_mask if i % 2 else mask)) for i in range(size)])


def spread(value, axis, size, beside=()):
    values = {0: value}
    for k in sorted(range(1, size), key=lambda k: (bin(k).count("1"), -k)):
        bit = k & -k
        if beside and k != bit:
            values[k ^ bit], beside = lax.optimization_barrier((values[k ^ bit], beside))
        values[k] = swap(values[k ^ bit], axis, size, bit)
    return [values[k] for k in range(size)], beside


def join(blocks):
    return blocks[0] if len(blocks) == 1 else jnp.concatenate(blocks, axis=0)


def make_body(dp, code):
    def body(residuals, codes, codebook):
        rows, dim = residuals.shape
        subs, words, width = codebook.shape
        own = subs * width
        codes_t = codes.T
        book_t = jnp.transpose(codebook, (0, 2, 1)).reshape(own, words)
        size = own // dp
        thin = size % 16 != 0
        if thin:
            place = lax.axis_index("dp")
            partial, codes_v, book_v, res_v = cross_partial(codes_t, book_t, residuals, None)
            cut = [
                lax.dynamic_slice_in_dim(partial, (place ^ k) * size, size, 0) for k in range(dp)
            ]
            parts = [cut[0]] + [part.astype(bf16) for part in cut[1:]]
        else:
            *parts, codes_v, book_v, res_v = cross_partial(codes_t, book_t, residuals, dp)
        far_first = range(dp - 1, 0, -1)
        got = [swap(parts[k], "dp", dp, k) for k in far_first]
        onehot, counts = onehot_call(codes_v, words)
        *got, onehot, counts = lax.optimization_barrier((*got, onehot, counts))
        piece = small_call(share_kernel, "share", (size, dim), bf16, parts[0], *got)
        pieces, _ = spread(piece, "dp", dp)
        if thin:
            block = jnp.zeros((own, dim), bf16)
            for k in range(dp):
                block = lax.dynamic_update_slice_in_dim(block, pieces[k], (place ^ k) * size, 0)
            held = [block]
        else:
            held = [jnp.concatenate(pieces[: max(dp - 1, 1)], axis=0)] + pieces[max(dp - 1, 1) :]
        strides = [1 << b for b in reversed(range(code.bit_length() - 1))]
        far, near = strides[:-1], strides[-1:]
        others = []
        for at, block in enumerate(held):
            have = [[block]]
            for even, odd in zip(far, far[::-1]):
                new = [[swap(join(t), "code", code, even, odd)] for t in have]
                have = have + new if at == 0 else [sum(have + new, [])]
            crossed = []
            for stride in near:
                groups = have if at == 0 or len(have[0]) == 1 else [have[0][:-1], have[0][-1:]]
                crossed = [[swap(join(t), "code", code, stride)] for t in groups]
            others += sum(have + crossed, [])[1:]
        held += others
        rotation_t = polar(held, own, 1 if thin else dp)
        scratch = [pltpu.VMEM((own, words), f32)]
        operands = (rotation_t, res_v, codes_v, onehot, counts)
        sums = small_call(sums_kernel, "sums", (own + subs, words), bf16, *operands, scratch=scratch)
        rotated = small_call(rotated_kernel, "rotated", (rows, own), f32, rotation_t, res_v)
        totals, (rotated,) = spread(sums, "dp", dp, (rotated,))
        book = small_call(book_kernel, "book", (own, words), f32, book_v, *totals)
        return rotated, jnp.transpose(book.reshape(subs, width, words), (0, 2, 1))

    return body


def solution(mesh):
    dp, code = mesh.shape["dp"], mesh.shape["code"]
    in_specs = (P("dp", None), P("dp", "code"), P("code", None, None))
    out_specs = (P("dp", "code"), P("code", None, None))
    return jax.shard_map(
        make_body(dp, code), mesh=mesh, in_specs=in_specs, out_specs=out_specs, check_vma=False
    )
```

```python
import functools

import jax
import jax.numpy as jnp
from jax import lax
from jax.experimental import pallas as pl
from jax.experimental.pallas import tpu as pltpu
from jax.sharding import PartitionSpec as P

quintic_a = 3.4445
quintic_b = -4.775
quintic_c = 2.0315
prior_weight = 8.0
epsilon = 1e-06
f32, bf16 = jnp.float32, jnp.bfloat16
MIB = 1024 * 1024
NT = (((1,), (1,)), ((), ()))


def dot(left, right):
    return jnp.dot(left, right, preferred_element_type=f32)


def dot_nt(left, right):
    return lax.dot_general(left, right, NT, preferred_element_type=f32)


def cross_kernel(codes_hbm, book_hbm, res_hbm, *refs, dp):
    outs = refs[: dp or 1]
    codes_ref, book_ref, res_ref, recon, cross, sems = refs[dp or 1 :]
    loads = [
        pltpu.make_async_copy(codes_hbm, codes_ref, sems.at[0]),
        pltpu.make_async_copy(book_hbm, book_ref, sems.at[1]),
        pltpu.make_async_copy(res_hbm, res_ref, sems.at[2]),
    ]
    for load in loads:
        load.start()
    loads[0].wait()
    loads[1].wait()
    subs, rows = codes_ref.shape
    width = book_ref.shape[0] // subs
    words = book_ref.shape[1]
    lanes = 128
    for m in range(subs):
        band = pl.ds(m * width, width)
        tables = [book_ref[band, pl.ds(t * lanes, lanes)] for t in range(words // lanes)]
        for c in range(rows // lanes):
            cols = pl.ds(c * lanes, lanes)
            code = jnp.broadcast_to(codes_ref[pl.ds(m, 1), cols], (width, lanes))
            low = jnp.bitwise_and(code, lanes - 1)
            value = jnp.take_along_axis(tables[0], low, axis=1, mode="promise_in_bounds")
            for t in range(1, len(tables)):
                other = jnp.take_along_axis(tables[t], low, axis=1, mode="promise_in_bounds")
                value = jnp.where(code >= t * lanes, other, value)
            recon[band, cols] = value
    loads[2].wait()
    if dp is None:
        outs[0][...] = dot(recon[...].astype(bf16), res_ref[...])
        return
    cross[...] = dot(recon[...].astype(bf16), res_ref[...])
    place = lax.axis_index("dp")
    size = outs[0].shape[0]
    for k, out in enumerate(outs):
        at = pl.multiple_of(jnp.bitwise_xor(place, k) * size, size)
        out[...] = cross[pl.ds(at, size), :].astype(out.dtype)


def cross_partial(codes_t, book_t, residuals, dp):
    rows, dim = residuals.shape
    cols = book_t.shape[0]
    if dp is None:
        shapes = (jax.ShapeDtypeStruct((cols, dim), f32),)
    else:
        shapes = tuple(
            jax.ShapeDtypeStruct((cols // dp, dim), bf16 if k else f32) for k in range(dp)
        )
    shapes += tuple(jax.ShapeDtypeStruct(x.shape, x.dtype) for x in (codes_t, book_t, residuals))
    return pl.pallas_call(
        functools.partial(cross_kernel, dp=dp),
        out_shape=shapes,
        in_specs=[pl.BlockSpec(memory_space=pltpu.HBM)] * 3,
        out_specs=(pl.BlockSpec(memory_space=pltpu.VMEM),) * len(shapes),
        scratch_shapes=[
            pltpu.VMEM((cols, rows), f32),
            pltpu.VMEM((cols, dim), f32),
            pltpu.SemaphoreType.DMA((3,)),
        ],
        compiler_params=pltpu.CompilerParams(vmem_limit_bytes=24 * MIB),
        name="cross_partial",
    )(*[pltpu.with_memory_space_constraint(x, pltpu.HBM) for x in (codes_t, book_t, residuals)])


def polar_kernel(*refs, blocks, pieces, chunk):
    block_refs = refs[:blocks]
    rot_b = refs[blocks]
    raw, gram, gram_b, poly_b, iterate, iterate_b = refs[blocks + 1 :]
    dim = raw.shape[0]
    own = rot_b.shape[0]
    steps = dim // chunk
    at = 0
    for block in block_refs:
        raw[pl.ds(at, block.shape[0]), :] = block[...]
        at += block.shape[0]

    def band_of(i):
        return pl.ds(i * chunk, chunk)

    def lower(j):
        return pl.ds(j * chunk, dim - j * chunk), pl.ds(j * chunk, chunk)

    def mirror(target, j, value):
        rows, cols = lower(j)
        target[rows, cols] = value.astype(bf16)
        for i in range(j + 1, steps):
            at = (i - j) * chunk
            target[cols, pl.ds(i * chunk, chunk)] = value[at : at + chunk, :].T.astype(bf16)

    def gram_of(source):
        r = lax.broadcasted_iota(jnp.int32, (chunk, chunk), 0)
        c = lax.broadcasted_iota(jnp.int32, (chunk, chunk), 1)
        trace = jnp.zeros((), f32)
        for j in range(steps):
            rows, cols = lower(j)
            part = dot_nt(source[rows, :], source[cols, :])
            gram[rows, cols] = part
            mirror(gram_b, j, part)
            trace = trace + jnp.sum(jnp.where(r == c, part[:chunk, :], 0.0))
        return trace

    def poly_of(wb, wc):
        for j in range(steps):
            rows, cols = lower(j)
            square = dot(gram_b[rows, :], gram_b[:, cols])
            mirror(poly_b, j, wb * gram[rows, cols] + wc * square)

    frob = gram_of(raw)
    scale2 = 1.0 / (frob + epsilon)
    scale = lax.rsqrt(frob + epsilon)
    poly_of(quintic_b * scale2, quintic_c * scale2 * scale2)

    for i in range(steps):
        cols = band_of(i)
        value = scale * (quintic_a * raw[:, cols].astype(f32) + dot(poly_b[...], raw[:, cols]))
        iterate[:, cols] = value
        iterate_b[:, cols] = value.astype(bf16)

    gram_of(iterate_b)
    poly_of(quintic_b, quintic_c)

    for i in range(steps):
        cols = band_of(i)
        value = quintic_a * iterate[:, cols] + dot(poly_b[...], iterate_b[:, cols])
        iterate[pl.ds(0, own), cols] = value[:own, :]
        raw[:, cols] = value.astype(bf16)

    mine = pl.ds(0, own)
    g = dot_nt(raw[mine, :], raw[...])
    image = dot(g.astype(bf16), raw[...])
    square = dot_nt(image.astype(bf16), raw[...])
    last = quintic_a * iterate[mine, :] + dot(
        (quintic_b * g + quintic_c * square).astype(bf16), raw[...]
    )
    size = own // pieces
    for p in range(pieces):
        to = 0
        if pieces > 1:
            to = pl.multiple_of(jnp.bitwise_xor(lax.axis_index("dp"), p) * size, size)
        rot_b[pl.ds(to, size), :] = last[p * size : (p + 1) * size, :].astype(bf16)


LOWS = 64


def onehot_kernel(codes_ref, onehot_ref, counts_ref):
    subs, rows_all = codes_ref.shape
    highs = counts_ref.shape[1] // LOWS
    low_word = lax.broadcasted_iota(jnp.int32, (LOWS, rows_all), 0)
    high_word = lax.broadcasted_iota(jnp.int32, (8, rows_all), 0)
    for m in range(subs):
        code = codes_ref[pl.ds(m, 1), :]
        low, high = jnp.bitwise_and(code, LOWS - 1), jnp.right_shift(code, 6)
        onehot = jnp.where(low_word == low, 1.0, 0.0).astype(bf16)
        onehot_ref[pl.ds(m * LOWS, LOWS), :] = onehot
        part = dot_nt(jnp.where(high_word == high, 1.0, 0.0).astype(bf16), onehot)
        for h in range(highs):
            counts_ref[pl.ds(m, 1), pl.ds(h * LOWS, LOWS)] = part[h : h + 1, :]


def onehot_call(codes_t, words):
    subs, rows = codes_t.shape
    vmem = pl.BlockSpec(memory_space=pltpu.VMEM)
    return pl.pallas_call(
        onehot_kernel,
        out_shape=(
            jax.ShapeDtypeStruct((subs * LOWS, rows), bf16),
            jax.ShapeDtypeStruct((subs, words), f32),
        ),
        in_specs=[vmem],
        out_specs=(vmem, vmem),
        compiler_params=pltpu.CompilerParams(vmem_limit_bytes=24 * MIB),
        cost_estimate=pl.CostEstimate(
            flops=2 * 256 * subs * LOWS * rows, bytes_accessed=2 * subs * LOWS * rows, transcendentals=0
        ),
        name="onehot",
    )(codes_t)


def sums_kernel(rot_ref, res_ref, codes_ref, onehot_ref, counts_ref, sent_ref, sums_ref):
    subs, rows_all = codes_ref.shape
    own = rot_ref.shape[0]
    words = counts_ref.shape[1]
    width = own // subs
    highs = words // LOWS
    group = min(subs, 256 // LOWS)
    rot_t = dot_nt(rot_ref[...], res_ref[...])
    for first in range(0, subs, group):
        values = []
        for m in range(first, first + group):
            high = jnp.right_shift(codes_ref[pl.ds(m, 1), :], 6)
            band = rot_t[m * width : (m + 1) * width, :]
            values += [jnp.where(high == h, band, 0.0) for h in range(highs)]
        tall = jnp.concatenate(values, axis=0).astype(bf16)
        part = dot_nt(tall, onehot_ref[pl.ds(first * LOWS, group * LOWS), :])
        for s in range(group):
            for h in range(highs):
                at = (s * highs + h) * width
                sums_ref[pl.ds((first + s) * width, width), pl.ds(h * LOWS, LOWS)] = part[
                    at : at + width, s * LOWS : (s + 1) * LOWS
                ]
    sent_ref[pl.ds(0, own), :] = sums_ref[...].astype(bf16)
    sent_ref[pl.ds(own, subs), :] = counts_ref[...].astype(bf16)


def rotated_kernel(rot_ref, res_ref, rotated_ref):
    rows_all = res_ref.shape[0]
    step = 512

    @pl.loop(0, rows_all // step)
    def _(i):
        rows = pl.ds(pl.multiple_of(i * step, step), step)
        rotated_ref[rows, :] = dot_nt(res_ref[rows, :], rot_ref[...])


def polar(block_list, own, pieces):
    dim = block_list[0].shape[1]
    vmem = pl.BlockSpec(memory_space=pltpu.VMEM)
    kernel = functools.partial(polar_kernel, blocks=len(block_list), pieces=pieces, chunk=256)
    return pl.pallas_call(
        kernel,
        out_shape=jax.ShapeDtypeStruct((own, dim), bf16),
        in_specs=[vmem] * len(block_list),
        out_specs=vmem,
        scratch_shapes=[
            pltpu.VMEM((dim, dim), bf16),
            pltpu.VMEM((dim, dim), f32),
            pltpu.VMEM((dim, dim), bf16),
            pltpu.VMEM((dim, dim), bf16),
            pltpu.VMEM((dim, dim), f32),
            pltpu.VMEM((dim, dim), bf16),
        ],
        compiler_params=pltpu.CompilerParams(vmem_limit_bytes=36 * MIB),
        name="polar",
    )(*block_list)


def share_kernel(*refs):
    total = refs[0][...].astype(f32)
    for part in refs[1:-1]:
        total = total + part[...].astype(f32)
    refs[-1][...] = total.astype(refs[-1].dtype)


def book_kernel(book_ref, *refs):
    sums, out_ref = refs[:-1], refs[-1]
    own = book_ref.shape[0]
    subs = sums[0].shape[0] - own
    width = own // subs
    total = sums[0][...].astype(f32)
    for part in sums[1:]:
        total = total + part[...].astype(f32)
    for m in range(subs):
        band = pl.ds(m * width, width)
        count = total[own + m : own + m + 1, :] + prior_weight
        part = total[m * width : (m + 1) * width, :]
        out_ref[band, :] = (part + prior_weight * book_ref[band, :]) / count


def small_call(kernel, name, shape, dtype, *operands, scratch=()):
    vmem = pl.BlockSpec(memory_space=pltpu.VMEM)
    return pl.pallas_call(
        kernel,
        out_shape=jax.ShapeDtypeStruct(shape, dtype),
        in_specs=[vmem] * len(operands),
        out_specs=vmem,
        scratch_shapes=scratch,
        compiler_params=pltpu.CompilerParams(vmem_limit_bytes=24 * MIB),
        name=name,
    )(*operands)


def swap(value, axis, size, mask, odd_mask=None):
    odd_mask = mask if odd_mask is None else odd_mask
    return lax.ppermute(value, axis, [(i, i ^ (odd_mask if i % 2 else mask)) for i in range(size)])


def make_body(dp, code):
    def body(residuals, codes, codebook):
        rows, dim = residuals.shape
        subs, words, width = codebook.shape
        own = subs * width
        codes_t = codes.T
        book_t = jnp.transpose(codebook, (0, 2, 1)).reshape(own, words)
        size = own // dp
        thin = size % 16 != 0
        if thin:
            place = lax.axis_index("dp")
            partial, codes_v, book_v, res_v = cross_partial(codes_t, book_t, residuals, None)
            cut = [
                lax.dynamic_slice_in_dim(partial, (place ^ k) * size, size, 0) for k in range(dp)
            ]
            parts = [cut[0]] + [part.astype(bf16) for part in cut[1:]]
        else:
            *parts, codes_v, book_v, res_v = cross_partial(codes_t, book_t, residuals, dp)
        far_first = range(dp - 1, 0, -1)
        got = [swap(parts[k], "dp", dp, k) for k in far_first]
        onehot, counts = onehot_call(codes_v, words)
        *got, onehot, counts = lax.optimization_barrier((*got, onehot, counts))
        piece = small_call(share_kernel, "share", (size, dim), bf16, parts[0], *got)
        pieces = {0: piece}
        for k in far_first:
            pieces[k] = swap(piece, "dp", dp, k)
        if thin:
            block = jnp.zeros((own, dim), bf16)
            for k in range(dp):
                block = lax.dynamic_update_slice_in_dim(block, pieces[k], (place ^ k) * size, 0)
            held = [block]
        else:
            half = max(dp // 2, 1)
            held = [
                jnp.concatenate([pieces[k] for k in range(at, min(at + half, dp))], axis=0)
                for at in range(0, dp, half)
            ]
        count = len(held)
        near = min(code, 2)
        for stride in range(code - near, 0, -near):
            held = held + [swap(t, "code", code, stride) for t in held[:count]]
        if near > 1:
            held = held + [swap(t, "code", code, 1) for t in held]
        rotation_t = polar(held, own, 1 if thin else dp)
        scratch = [pltpu.VMEM((own, words), f32)]
        operands = (rotation_t, res_v, codes_v, onehot, counts)
        sums = small_call(sums_kernel, "sums", (own + subs, words), bf16, *operands, scratch=scratch)
        rotated = small_call(rotated_kernel, "rotated", (rows, own), f32, rotation_t, res_v)
        others = [swap(sums, "dp", dp, k) for k in far_first]
        book = small_call(book_kernel, "book", (own, words), f32, book_v, sums, *others)
        return rotated, jnp.transpose(book.reshape(subs, width, words), (0, 2, 1))

    return body


def solution(mesh):
    dp, code = mesh.shape["dp"], mesh.shape["code"]
    in_specs = (P("dp", None), P("dp", "code"), P("code", None, None))
    out_specs = (P("dp", "code"), P("code", None, None))
    return jax.shard_map(
        make_body(dp, code), mesh=mesh, in_specs=in_specs, out_specs=out_specs, check_vma=False
    )
```

```python
import functools

import jax
import jax.numpy as jnp
from jax import lax
from jax.experimental import pallas as pl
from jax.experimental.pallas import tpu as pltpu
from jax.sharding import PartitionSpec as P

quintic_a = 3.4445
quintic_b = -4.775
quintic_c = 2.0315
prior_weight = 8.0
epsilon = 1e-06
f32, bf16 = jnp.float32, jnp.bfloat16
MIB = 1024 * 1024
ROW_CHUNKS = 4
NT = (((1,), (1,)), ((), ()))


def dot(left, right):
    return jnp.dot(left, right, preferred_element_type=f32)


def dot_nt(left, right):
    return lax.dot_general(left, right, NT, preferred_element_type=f32)


def cross_kernel(codes_hbm, book_hbm, res_hbm, *refs, dp):
    outs = refs[: dp or 1]
    codes_ref, book_ref, res_ref, recon, cross, sems = refs[dp or 1 :]
    subs, rows = codes_ref.shape
    width = book_ref.shape[0] // subs
    words = book_ref.shape[1]
    lanes = 128
    chunks = sems.shape[0] - 2
    step = rows // chunks
    loads = [
        pltpu.make_async_copy(codes_hbm, codes_ref, sems.at[0]),
        pltpu.make_async_copy(book_hbm, book_ref, sems.at[1]),
    ]
    for i in range(chunks):
        part = pl.ds(i * step, step)
        loads.append(pltpu.make_async_copy(res_hbm.at[part], res_ref.at[part], sems.at[2 + i]))
    for load in loads:
        load.start()
    loads[0].wait()
    loads[1].wait()
    total = outs[0] if dp is None else cross
    for i in range(chunks):
        part = pl.ds(i * step, step)
        for m in range(subs):
            band = pl.ds(m * width, width)
            tables = [book_ref[band, pl.ds(t * lanes, lanes)] for t in range(words // lanes)]
            for c in range(i * step // lanes, (i + 1) * step // lanes):
                cols = pl.ds(c * lanes, lanes)
                code = jnp.broadcast_to(codes_ref[pl.ds(m, 1), cols], (width, lanes))
                low = jnp.bitwise_and(code, lanes - 1)
                value = jnp.take_along_axis(tables[0], low, axis=1, mode="promise_in_bounds")
                for t in range(1, len(tables)):
                    other = jnp.take_along_axis(tables[t], low, axis=1, mode="promise_in_bounds")
                    value = jnp.where(code >= t * lanes, other, value)
                recon[band, cols] = value
        loads[2 + i].wait()
        product = dot(recon[:, part].astype(bf16), res_ref[part, :])
        total[...] = product if i == 0 else total[...] + product
    if dp is None:
        return
    place = lax.axis_index("dp")
    size = outs[0].shape[0]
    for k, out in enumerate(outs):
        at = pl.multiple_of(jnp.bitwise_xor(place, k) * size, size)
        out[...] = cross[pl.ds(at, size), :].astype(out.dtype)


def cross_partial(codes_t, book_t, residuals, dp):
    rows, dim = residuals.shape
    cols = book_t.shape[0]
    if dp is None:
        shapes = (jax.ShapeDtypeStruct((cols, dim), f32),)
    else:
        shapes = tuple(
            jax.ShapeDtypeStruct((cols // dp, dim), bf16 if k else f32) for k in range(dp)
        )
    shapes += tuple(jax.ShapeDtypeStruct(x.shape, x.dtype) for x in (codes_t, book_t, residuals))
    return pl.pallas_call(
        functools.partial(cross_kernel, dp=dp),
        out_shape=shapes,
        in_specs=[pl.BlockSpec(memory_space=pltpu.HBM)] * 3,
        out_specs=(pl.BlockSpec(memory_space=pltpu.VMEM),) * len(shapes),
        scratch_shapes=[
            pltpu.VMEM((cols, rows), f32),
            pltpu.VMEM((cols, dim), f32),
            pltpu.SemaphoreType.DMA((2 + ROW_CHUNKS,)),
        ],
        compiler_params=pltpu.CompilerParams(vmem_limit_bytes=24 * MIB),
        name="cross_partial",
    )(*[pltpu.with_memory_space_constraint(x, pltpu.HBM) for x in (codes_t, book_t, residuals)])


def polar_kernel(*refs, blocks, pieces, chunk):
    block_refs = refs[:blocks]
    rot_b = refs[blocks]
    raw, gram, gram_b, poly_b, iterate, iterate_b = refs[blocks + 1 :]
    dim = raw.shape[0]
    own = rot_b.shape[0]
    steps = dim // chunk
    at = 0
    for block in block_refs:
        raw[pl.ds(at, block.shape[0]), :] = block[...]
        at += block.shape[0]

    def band_of(i):
        return pl.ds(i * chunk, chunk)

    def lower(j):
        return pl.ds(j * chunk, dim - j * chunk), pl.ds(j * chunk, chunk)

    def mirror(target, j, value):
        rows, cols = lower(j)
        target[rows, cols] = value.astype(bf16)
        for i in range(j + 1, steps):
            at = (i - j) * chunk
            target[cols, pl.ds(i * chunk, chunk)] = value[at : at + chunk, :].T.astype(bf16)

    def gram_of(source):
        r = lax.broadcasted_iota(jnp.int32, (chunk, chunk), 0)
        c = lax.broadcasted_iota(jnp.int32, (chunk, chunk), 1)
        trace = jnp.zeros((), f32)
        for j in range(steps):
            rows, cols = lower(j)
            part = dot_nt(source[rows, :], source[cols, :])
            gram[rows, cols] = part
            mirror(gram_b, j, part)
            trace = trace + jnp.sum(jnp.where(r == c, part[:chunk, :], 0.0))
        return trace

    def poly_of(wb, wc):
        for j in range(steps):
            rows, cols = lower(j)
            square = dot(gram_b[rows, :], gram_b[:, cols])
            mirror(poly_b, j, wb * gram[rows, cols] + wc * square)

    frob = gram_of(raw)
    scale2 = 1.0 / (frob + epsilon)
    scale = lax.rsqrt(frob + epsilon)
    poly_of(quintic_b * scale2, quintic_c * scale2 * scale2)

    for i in range(steps):
        cols = band_of(i)
        value = scale * (quintic_a * raw[:, cols].astype(f32) + dot(poly_b[...], raw[:, cols]))
        iterate[:, cols] = value
        iterate_b[:, cols] = value.astype(bf16)

    gram_of(iterate_b)
    poly_of(quintic_b, quintic_c)

    for i in range(steps):
        cols = band_of(i)
        value = quintic_a * iterate[:, cols] + dot(poly_b[...], iterate_b[:, cols])
        iterate[pl.ds(0, own), cols] = value[:own, :]
        raw[:, cols] = value.astype(bf16)

    mine = pl.ds(0, own)
    g = dot_nt(raw[mine, :], raw[...])
    image = dot(g.astype(bf16), raw[...])
    square = dot_nt(image.astype(bf16), raw[...])
    last = quintic_a * iterate[mine, :] + dot(
        (quintic_b * g + quintic_c * square).astype(bf16), raw[...]
    )
    size = own // pieces
    for p in range(pieces):
        to = 0
        if pieces > 1:
            to = pl.multiple_of(jnp.bitwise_xor(lax.axis_index("dp"), p) * size, size)
        rot_b[pl.ds(to, size), :] = last[p * size : (p + 1) * size, :].astype(bf16)


LOWS = 64


def onehot_kernel(codes_ref, onehot_ref, counts_ref):
    subs, rows_all = codes_ref.shape
    highs = counts_ref.shape[1] // LOWS
    low_word = lax.broadcasted_iota(jnp.int32, (LOWS, rows_all), 0)
    high_word = lax.broadcasted_iota(jnp.int32, (8, rows_all), 0)
    for m in range(subs):
        code = codes_ref[pl.ds(m, 1), :]
        low, high = jnp.bitwise_and(code, LOWS - 1), jnp.right_shift(code, 6)
        onehot = jnp.where(low_word == low, 1.0, 0.0).astype(bf16)
        onehot_ref[pl.ds(m * LOWS, LOWS), :] = onehot
        part = dot_nt(jnp.where(high_word == high, 1.0, 0.0).astype(bf16), onehot)
        for h in range(highs):
            counts_ref[pl.ds(m, 1), pl.ds(h * LOWS, LOWS)] = part[h : h + 1, :]


def onehot_call(codes_t, words):
    subs, rows = codes_t.shape
    vmem = pl.BlockSpec(memory_space=pltpu.VMEM)
    return pl.pallas_call(
        onehot_kernel,
        out_shape=(
            jax.ShapeDtypeStruct((subs * LOWS, rows), bf16),
            jax.ShapeDtypeStruct((subs, words), f32),
        ),
        in_specs=[vmem],
        out_specs=(vmem, vmem),
        compiler_params=pltpu.CompilerParams(vmem_limit_bytes=24 * MIB),
        cost_estimate=pl.CostEstimate(
            flops=2 * 256 * subs * LOWS * rows, bytes_accessed=2 * subs * LOWS * rows, transcendentals=0
        ),
        name="onehot",
    )(codes_t)


def sums_kernel(rot_ref, res_ref, codes_ref, onehot_ref, counts_ref, sent_ref, sums_ref):
    subs, rows_all = codes_ref.shape
    own = rot_ref.shape[0]
    words = counts_ref.shape[1]
    width = own // subs
    highs = words // LOWS
    group = min(subs, 256 // LOWS)
    rot_t = dot_nt(rot_ref[...], res_ref[...])
    for first in range(0, subs, group):
        values = []
        for m in range(first, first + group):
            high = jnp.right_shift(codes_ref[pl.ds(m, 1), :], 6)
            band = rot_t[m * width : (m + 1) * width, :]
            values += [jnp.where(high == h, band, 0.0) for h in range(highs)]
        tall = jnp.concatenate(values, axis=0).astype(bf16)
        part = dot_nt(tall, onehot_ref[pl.ds(first * LOWS, group * LOWS), :])
        for s in range(group):
            for h in range(highs):
                at = (s * highs + h) * width
                sums_ref[pl.ds((first + s) * width, width), pl.ds(h * LOWS, LOWS)] = part[
                    at : at + width, s * LOWS : (s + 1) * LOWS
                ]
    sent_ref[pl.ds(0, own), :] = sums_ref[...].astype(bf16)
    sent_ref[pl.ds(own, subs), :] = counts_ref[...].astype(bf16)


def rotated_kernel(rot_ref, res_ref, rotated_ref):
    rows_all = res_ref.shape[0]
    step = 512

    @pl.loop(0, rows_all // step)
    def _(i):
        rows = pl.ds(pl.multiple_of(i * step, step), step)
        rotated_ref[rows, :] = dot_nt(res_ref[rows, :], rot_ref[...])


def polar(block_list, own, pieces):
    dim = block_list[0].shape[1]
    vmem = pl.BlockSpec(memory_space=pltpu.VMEM)
    kernel = functools.partial(polar_kernel, blocks=len(block_list), pieces=pieces, chunk=256)
    return pl.pallas_call(
        kernel,
        out_shape=jax.ShapeDtypeStruct((own, dim), bf16),
        in_specs=[vmem] * len(block_list),
        out_specs=vmem,
        scratch_shapes=[
            pltpu.VMEM((dim, dim), bf16),
            pltpu.VMEM((dim, dim), f32),
            pltpu.VMEM((dim, dim), bf16),
            pltpu.VMEM((dim, dim), bf16),
            pltpu.VMEM((dim, dim), f32),
            pltpu.VMEM((dim, dim), bf16),
        ],
        compiler_params=pltpu.CompilerParams(vmem_limit_bytes=36 * MIB),
        name="polar",
    )(*block_list)


def share_kernel(*refs):
    total = refs[0][...].astype(f32)
    for part in refs[1:-1]:
        total = total + part[...].astype(f32)
    refs[-1][...] = total.astype(refs[-1].dtype)


def book_kernel(book_ref, *refs):
    sums, out_ref = refs[:-1], refs[-1]
    own = book_ref.shape[0]
    subs = sums[0].shape[0] - own
    width = own // subs
    total = sums[0][...].astype(f32)
    for part in sums[1:]:
        total = total + part[...].astype(f32)
    for m in range(subs):
        band = pl.ds(m * width, width)
        count = total[own + m : own + m + 1, :] + prior_weight
        part = total[m * width : (m + 1) * width, :]
        out_ref[band, :] = (part + prior_weight * book_ref[band, :]) / count


def small_call(kernel, name, shape, dtype, *operands, scratch=()):
    vmem = pl.BlockSpec(memory_space=pltpu.VMEM)
    return pl.pallas_call(
        kernel,
        out_shape=jax.ShapeDtypeStruct(shape, dtype),
        in_specs=[vmem] * len(operands),
        out_specs=vmem,
        scratch_shapes=scratch,
        compiler_params=pltpu.CompilerParams(vmem_limit_bytes=24 * MIB),
        name=name,
    )(*operands)


def swap(value, axis, size, mask, odd_mask=None):
    odd_mask = mask if odd_mask is None else odd_mask
    return lax.ppermute(value, axis, [(i, i ^ (odd_mask if i % 2 else mask)) for i in range(size)])


def make_body(dp, code):
    def body(residuals, codes, codebook):
        rows, dim = residuals.shape
        subs, words, width = codebook.shape
        own = subs * width
        codes_t = codes.T
        book_t = jnp.transpose(codebook, (0, 2, 1)).reshape(own, words)
        size = own // dp
        thin = size % 16 != 0
        if thin:
            place = lax.axis_index("dp")
            partial, codes_v, book_v, res_v = cross_partial(codes_t, book_t, residuals, None)
            cut = [
                lax.dynamic_slice_in_dim(partial, (place ^ k) * size, size, 0) for k in range(dp)
            ]
            parts = [cut[0]] + [part.astype(bf16) for part in cut[1:]]
        else:
            *parts, codes_v, book_v, res_v = cross_partial(codes_t, book_t, residuals, dp)
        far_first = range(dp - 1, 0, -1)
        got = [swap(parts[k], "dp", dp, k) for k in far_first]
        onehot, counts = onehot_call(codes_v, words)
        *got, onehot, counts = lax.optimization_barrier((*got, onehot, counts))
        piece = small_call(share_kernel, "share", (size, dim), bf16, parts[0], *got)
        pieces = {0: piece}
        for k in far_first:
            pieces[k] = swap(piece, "dp", dp, k)
        if thin:
            block = jnp.zeros((own, dim), bf16)
            for k in range(dp):
                block = lax.dynamic_update_slice_in_dim(block, pieces[k], (place ^ k) * size, 0)
            held = [block]
        else:
            half = max(dp // 2, 1)
            held = [
                jnp.concatenate([pieces[k] for k in range(at, min(at + half, dp))], axis=0)
                for at in range(0, dp, half)
            ]
        strides = [1 << b for b in reversed(range(code.bit_length() - 1))]
        far = strides[:-1]
        for even, odd in zip(far, far[::-1]):
            held = held + [swap(t, "code", code, even, odd) for t in held]
        for stride in strides[-1:]:
            held = held + [swap(t, "code", code, stride) for t in held]
        rotation_t = polar(held, own, 1 if thin else dp)
        scratch = [pltpu.VMEM((own, words), f32)]
        operands = (rotation_t, res_v, codes_v, onehot, counts)
        sums = small_call(sums_kernel, "sums", (own + subs, words), bf16, *operands, scratch=scratch)
        rotated = small_call(rotated_kernel, "rotated", (rows, own), f32, rotation_t, res_v)
        others = [swap(sums, "dp", dp, k) for k in range(1, dp)]
        book = small_call(book_kernel, "book", (own, words), f32, book_v, sums, *others)
        return rotated, jnp.transpose(book.reshape(subs, width, words), (0, 2, 1))

    return body


def solution(mesh):
    dp, code = mesh.shape["dp"], mesh.shape["code"]
    in_specs = (P("dp", None), P("dp", "code"), P("code", None, None))
    out_specs = (P("dp", "code"), P("code", None, None))
    return jax.shard_map(
        make_body(dp, code), mesh=mesh, in_specs=in_specs, out_specs=out_specs, check_vma=False
    )
```

```python
import functools

import jax
import jax.numpy as jnp
from jax import lax
from jax.experimental import pallas as pl
from jax.experimental.pallas import tpu as pltpu
from jax.sharding import PartitionSpec as P

quintic_a = 3.4445
quintic_b = -4.775
quintic_c = 2.0315
prior_weight = 8.0
epsilon = 1e-06
f32, bf16 = jnp.float32, jnp.bfloat16
MIB = 1024 * 1024
ROW_CHUNKS = 4
NT = (((1,), (1,)), ((), ()))


def dot(left, right):
    return jnp.dot(left, right, preferred_element_type=f32)


def dot_nt(left, right):
    return lax.dot_general(left, right, NT, preferred_element_type=f32)


def cross_kernel(codes_hbm, book_hbm, res_hbm, *refs, dp):
    outs = refs[: dp or 1]
    codes_ref, book_ref, res_ref, recon, cross, sems = refs[dp or 1 :]
    subs, rows = codes_ref.shape
    width = book_ref.shape[0] // subs
    words = book_ref.shape[1]
    lanes = 128
    chunks = sems.shape[0] - 2
    step = rows // chunks
    loads = [
        pltpu.make_async_copy(codes_hbm, codes_ref, sems.at[0]),
        pltpu.make_async_copy(book_hbm, book_ref, sems.at[1]),
    ]
    for i in range(chunks):
        part = pl.ds(i * step, step)
        loads.append(pltpu.make_async_copy(res_hbm.at[part], res_ref.at[part], sems.at[2 + i]))
    for load in loads:
        load.start()
    loads[0].wait()
    loads[1].wait()
    total = outs[0] if dp is None else cross
    for i in range(chunks):
        part = pl.ds(i * step, step)
        for m in range(subs):
            band = pl.ds(m * width, width)
            tables = [book_ref[band, pl.ds(t * lanes, lanes)] for t in range(words // lanes)]
            for c in range(i * step // lanes, (i + 1) * step // lanes):
                cols = pl.ds(c * lanes, lanes)
                code = jnp.broadcast_to(codes_ref[pl.ds(m, 1), cols], (width, lanes))
                low = jnp.bitwise_and(code, lanes - 1)
                value = jnp.take_along_axis(tables[0], low, axis=1, mode="promise_in_bounds")
                for t in range(1, len(tables)):
                    other = jnp.take_along_axis(tables[t], low, axis=1, mode="promise_in_bounds")
                    value = jnp.where(code >= t * lanes, other, value)
                recon[band, cols] = value
        loads[2 + i].wait()
        product = dot(recon[:, part].astype(bf16), res_ref[part, :])
        total[...] = product if i == 0 else total[...] + product
    if dp is None:
        return
    place = lax.axis_index("dp")
    size = outs[0].shape[0]
    for k, out in enumerate(outs):
        at = pl.multiple_of(jnp.bitwise_xor(place, k) * size, size)
        out[...] = cross[pl.ds(at, size), :].astype(out.dtype)


def cross_partial(codes_t, book_t, residuals, dp):
    rows, dim = residuals.shape
    cols = book_t.shape[0]
    if dp is None:
        shapes = (jax.ShapeDtypeStruct((cols, dim), f32),)
    else:
        shapes = tuple(
            jax.ShapeDtypeStruct((cols // dp, dim), bf16 if k else f32) for k in range(dp)
        )
    shapes += tuple(jax.ShapeDtypeStruct(x.shape, x.dtype) for x in (codes_t, book_t, residuals))
    return pl.pallas_call(
        functools.partial(cross_kernel, dp=dp),
        out_shape=shapes,
        in_specs=[pl.BlockSpec(memory_space=pltpu.HBM)] * 3,
        out_specs=(pl.BlockSpec(memory_space=pltpu.VMEM),) * len(shapes),
        scratch_shapes=[
            pltpu.VMEM((cols, rows), f32),
            pltpu.VMEM((cols, dim), f32),
            pltpu.SemaphoreType.DMA((2 + ROW_CHUNKS,)),
        ],
        compiler_params=pltpu.CompilerParams(vmem_limit_bytes=24 * MIB),
        name="cross_partial",
    )(*[pltpu.with_memory_space_constraint(x, pltpu.HBM) for x in (codes_t, book_t, residuals)])


def polar_kernel(*refs, blocks, pieces, chunk):
    block_refs = refs[:blocks]
    rot_b = refs[blocks]
    raw, gram, gram_b, poly_b, iterate, iterate_b = refs[blocks + 1 :]
    dim = raw.shape[0]
    own = rot_b.shape[0]
    steps = dim // chunk
    at = 0
    for block in block_refs:
        raw[pl.ds(at, block.shape[0]), :] = block[...]
        at += block.shape[0]

    def band_of(i):
        return pl.ds(i * chunk, chunk)

    def lower(j):
        return pl.ds(j * chunk, dim - j * chunk), pl.ds(j * chunk, chunk)

    def mirror(target, j, value):
        rows, cols = lower(j)
        target[rows, cols] = value.astype(bf16)
        for i in range(j + 1, steps):
            at = (i - j) * chunk
            target[cols, pl.ds(i * chunk, chunk)] = value[at : at + chunk, :].T.astype(bf16)

    def gram_of(source):
        r = lax.broadcasted_iota(jnp.int32, (chunk, chunk), 0)
        c = lax.broadcasted_iota(jnp.int32, (chunk, chunk), 1)
        trace = jnp.zeros((), f32)
        for j in range(steps):
            rows, cols = lower(j)
            part = dot_nt(source[rows, :], source[cols, :])
            gram[rows, cols] = part
            mirror(gram_b, j, part)
            trace = trace + jnp.sum(jnp.where(r == c, part[:chunk, :], 0.0))
        return trace

    def poly_of(wb, wc):
        for j in range(steps):
            rows, cols = lower(j)
            square = dot(gram_b[rows, :], gram_b[:, cols])
            mirror(poly_b, j, wb * gram[rows, cols] + wc * square)

    frob = gram_of(raw)
    scale2 = 1.0 / (frob + epsilon)
    scale = lax.rsqrt(frob + epsilon)
    poly_of(quintic_b * scale2, quintic_c * scale2 * scale2)

    for i in range(steps):
        cols = band_of(i)
        value = scale * (quintic_a * raw[:, cols].astype(f32) + dot(poly_b[...], raw[:, cols]))
        iterate[:, cols] = value
        iterate_b[:, cols] = value.astype(bf16)

    gram_of(iterate_b)
    poly_of(quintic_b, quintic_c)

    for i in range(steps):
        cols = band_of(i)
        value = quintic_a * iterate[:, cols] + dot(poly_b[...], iterate_b[:, cols])
        iterate[pl.ds(0, own), cols] = value[:own, :]
        raw[:, cols] = value.astype(bf16)

    mine = pl.ds(0, own)
    g = dot_nt(raw[mine, :], raw[...])
    image = dot(g.astype(bf16), raw[...])
    square = dot_nt(image.astype(bf16), raw[...])
    last = quintic_a * iterate[mine, :] + dot(
        (quintic_b * g + quintic_c * square).astype(bf16), raw[...]
    )
    size = own // pieces
    for p in range(pieces):
        to = 0
        if pieces > 1:
            to = pl.multiple_of(jnp.bitwise_xor(lax.axis_index("dp"), p) * size, size)
        rot_b[pl.ds(to, size), :] = last[p * size : (p + 1) * size, :].astype(bf16)


LOWS = 64


def onehot_kernel(codes_ref, onehot_ref, counts_ref):
    subs, rows_all = codes_ref.shape
    highs = counts_ref.shape[1] // LOWS
    low_word = lax.broadcasted_iota(jnp.int32, (LOWS, rows_all), 0)
    high_word = lax.broadcasted_iota(jnp.int32, (8, rows_all), 0)
    for m in range(subs):
        code = codes_ref[pl.ds(m, 1), :]
        low, high = jnp.bitwise_and(code, LOWS - 1), jnp.right_shift(code, 6)
        onehot = jnp.where(low_word == low, 1.0, 0.0).astype(bf16)
        onehot_ref[pl.ds(m * LOWS, LOWS), :] = onehot
        part = dot_nt(jnp.where(high_word == high, 1.0, 0.0).astype(bf16), onehot)
        for h in range(highs):
            counts_ref[pl.ds(m, 1), pl.ds(h * LOWS, LOWS)] = part[h : h + 1, :]


def onehot_call(codes_t, words):
    subs, rows = codes_t.shape
    vmem = pl.BlockSpec(memory_space=pltpu.VMEM)
    return pl.pallas_call(
        onehot_kernel,
        out_shape=(
            jax.ShapeDtypeStruct((subs * LOWS, rows), bf16),
            jax.ShapeDtypeStruct((subs, words), f32),
        ),
        in_specs=[vmem],
        out_specs=(vmem, vmem),
        compiler_params=pltpu.CompilerParams(vmem_limit_bytes=24 * MIB),
        cost_estimate=pl.CostEstimate(
            flops=2 * 256 * subs * LOWS * rows, bytes_accessed=2 * subs * LOWS * rows, transcendentals=0
        ),
        name="onehot",
    )(codes_t)


def sums_kernel(rot_ref, res_ref, codes_ref, onehot_ref, counts_ref, sent_ref, sums_ref):
    subs, rows_all = codes_ref.shape
    own = rot_ref.shape[0]
    words = counts_ref.shape[1]
    width = own // subs
    highs = words // LOWS
    group = min(subs, 256 // LOWS)
    rot_t = dot_nt(rot_ref[...], res_ref[...])
    for first in range(0, subs, group):
        values = []
        for m in range(first, first + group):
            high = jnp.right_shift(codes_ref[pl.ds(m, 1), :], 6)
            band = rot_t[m * width : (m + 1) * width, :]
            values += [jnp.where(high == h, band, 0.0) for h in range(highs)]
        tall = jnp.concatenate(values, axis=0).astype(bf16)
        part = dot_nt(tall, onehot_ref[pl.ds(first * LOWS, group * LOWS), :])
        for s in range(group):
            for h in range(highs):
                at = (s * highs + h) * width
                sums_ref[pl.ds((first + s) * width, width), pl.ds(h * LOWS, LOWS)] = part[
                    at : at + width, s * LOWS : (s + 1) * LOWS
                ]
    sent_ref[pl.ds(0, own), :] = sums_ref[...].astype(bf16)
    sent_ref[pl.ds(own, subs), :] = counts_ref[...].astype(bf16)


def rotated_kernel(rot_ref, res_ref, rotated_ref):
    rows_all = res_ref.shape[0]
    step = 512

    @pl.loop(0, rows_all // step)
    def _(i):
        rows = pl.ds(pl.multiple_of(i * step, step), step)
        rotated_ref[rows, :] = dot_nt(res_ref[rows, :], rot_ref[...])


def polar(block_list, own, pieces):
    dim = block_list[0].shape[1]
    vmem = pl.BlockSpec(memory_space=pltpu.VMEM)
    kernel = functools.partial(polar_kernel, blocks=len(block_list), pieces=pieces, chunk=256)
    return pl.pallas_call(
        kernel,
        out_shape=jax.ShapeDtypeStruct((own, dim), bf16),
        in_specs=[vmem] * len(block_list),
        out_specs=vmem,
        scratch_shapes=[
            pltpu.VMEM((dim, dim), bf16),
            pltpu.VMEM((dim, dim), f32),
            pltpu.VMEM((dim, dim), bf16),
            pltpu.VMEM((dim, dim), bf16),
            pltpu.VMEM((dim, dim), f32),
            pltpu.VMEM((dim, dim), bf16),
        ],
        compiler_params=pltpu.CompilerParams(vmem_limit_bytes=36 * MIB),
        name="polar",
    )(*block_list)


def share_kernel(*refs):
    total = refs[0][...].astype(f32)
    for part in refs[1:-1]:
        total = total + part[...].astype(f32)
    refs[-1][...] = total.astype(refs[-1].dtype)


def book_kernel(book_ref, *refs):
    sums, out_ref = refs[:-1], refs[-1]
    own = book_ref.shape[0]
    subs = sums[0].shape[0] - own
    width = own // subs
    total = sums[0][...].astype(f32)
    for part in sums[1:]:
        total = total + part[...].astype(f32)
    for m in range(subs):
        band = pl.ds(m * width, width)
        count = total[own + m : own + m + 1, :] + prior_weight
        part = total[m * width : (m + 1) * width, :]
        out_ref[band, :] = (part + prior_weight * book_ref[band, :]) / count


def small_call(kernel, name, shape, dtype, *operands, scratch=()):
    vmem = pl.BlockSpec(memory_space=pltpu.VMEM)
    return pl.pallas_call(
        kernel,
        out_shape=jax.ShapeDtypeStruct(shape, dtype),
        in_specs=[vmem] * len(operands),
        out_specs=vmem,
        scratch_shapes=scratch,
        compiler_params=pltpu.CompilerParams(vmem_limit_bytes=24 * MIB),
        name=name,
    )(*operands)


def swap(value, axis, size, mask, odd_mask=None):
    odd_mask = mask if odd_mask is None else odd_mask
    return lax.ppermute(value, axis, [(i, i ^ (odd_mask if i % 2 else mask)) for i in range(size)])


def make_body(dp, code):
    def body(residuals, codes, codebook):
        rows, dim = residuals.shape
        subs, words, width = codebook.shape
        own = subs * width
        codes_t = codes.T
        book_t = jnp.transpose(codebook, (0, 2, 1)).reshape(own, words)
        size = own // dp
        thin = size % 16 != 0
        if thin:
            place = lax.axis_index("dp")
            partial, codes_v, book_v, res_v = cross_partial(codes_t, book_t, residuals, None)
            cut = [
                lax.dynamic_slice_in_dim(partial, (place ^ k) * size, size, 0) for k in range(dp)
            ]
            parts = [cut[0]] + [part.astype(bf16) for part in cut[1:]]
        else:
            *parts, codes_v, book_v, res_v = cross_partial(codes_t, book_t, residuals, dp)
        far_first = range(dp - 1, 0, -1)
        got = [swap(parts[k], "dp", dp, k) for k in far_first]
        onehot, counts = onehot_call(codes_v, words)
        *got, onehot, counts = lax.optimization_barrier((*got, onehot, counts))
        piece = small_call(share_kernel, "share", (size, dim), bf16, parts[0], *got)
        pieces = {0: piece}
        for k in far_first:
            pieces[k] = swap(piece, "dp", dp, k)
        if thin:
            block = jnp.zeros((own, dim), bf16)
            for k in range(dp):
                block = lax.dynamic_update_slice_in_dim(block, pieces[k], (place ^ k) * size, 0)
            held = [block]
        else:
            half = max(dp // 2, 1)
            held = [
                jnp.concatenate([pieces[k] for k in range(at, min(at + half, dp))], axis=0)
                for at in range(0, dp, half)
            ]
        strides = [1 << b for b in reversed(range(code.bit_length() - 1))]
        far = strides[:-1]
        count = len(held)
        for even, odd in zip(far, far[::-1]):
            later = held
            if held[count:]:
                last, _ = lax.optimization_barrier((held[count - 1], held[2 * count - 1]))
                later = held[: count - 1] + [last] + held[count:]
            held = held + [swap(t, "code", code, even, odd) for t in later]
        for stride in strides[-1:]:
            held = held + [swap(t, "code", code, stride) for t in held]
        rotation_t = polar(held, own, 1 if thin else dp)
        scratch = [pltpu.VMEM((own, words), f32)]
        operands = (rotation_t, res_v, codes_v, onehot, counts)
        sums = small_call(sums_kernel, "sums", (own + subs, words), bf16, *operands, scratch=scratch)
        rotated = small_call(rotated_kernel, "rotated", (rows, own), f32, rotation_t, res_v)
        others = [swap(sums, "dp", dp, k) for k in range(1, dp)]
        book = small_call(book_kernel, "book", (own, words), f32, book_v, sums, *others)
        return rotated, jnp.transpose(book.reshape(subs, width, words), (0, 2, 1))

    return body


def solution(mesh):
    dp, code = mesh.shape["dp"], mesh.shape["code"]
    in_specs = (P("dp", None), P("dp", "code"), P("code", None, None))
    out_specs = (P("dp", "code"), P("code", None, None))
    return jax.shard_map(
        make_body(dp, code), mesh=mesh, in_specs=in_specs, out_specs=out_specs, check_vma=False
    )
```

```python
import functools

import jax
import jax.numpy as jnp
from jax import lax
from jax.experimental import pallas as pl
from jax.experimental.pallas import tpu as pltpu
from jax.sharding import PartitionSpec as P

quintic_a = 3.4445
quintic_b = -4.775
quintic_c = 2.0315
prior_weight = 8.0
epsilon = 1e-06
f32, bf16 = jnp.float32, jnp.bfloat16
MIB = 1024 * 1024
ROW_CHUNKS = 4
NT = (((1,), (1,)), ((), ()))


def dot(left, right):
    return jnp.dot(left, right, preferred_element_type=f32)


def dot_nt(left, right):
    return lax.dot_general(left, right, NT, preferred_element_type=f32)


def cross_kernel(codes_hbm, book_hbm, res_hbm, *refs, dp):
    outs = refs[: dp or 1]
    codes_ref, book_ref, res_ref, recon, cross, sems = refs[dp or 1 :]
    subs, rows = codes_ref.shape
    width = book_ref.shape[0] // subs
    words = book_ref.shape[1]
    lanes = 128
    chunks = sems.shape[0] - 2
    step = rows // chunks
    loads = [
        pltpu.make_async_copy(codes_hbm, codes_ref, sems.at[0]),
        pltpu.make_async_copy(book_hbm, book_ref, sems.at[1]),
    ]
    for i in range(chunks):
        part = pl.ds(i * step, step)
        loads.append(pltpu.make_async_copy(res_hbm.at[part], res_ref.at[part], sems.at[2 + i]))
    for load in loads:
        load.start()
    loads[0].wait()
    loads[1].wait()
    total = outs[0] if dp is None else cross
    for i in range(chunks):
        part = pl.ds(i * step, step)
        for m in range(subs):
            band = pl.ds(m * width, width)
            tables = [book_ref[band, pl.ds(t * lanes, lanes)] for t in range(words // lanes)]
            for c in range(i * step // lanes, (i + 1) * step // lanes):
                cols = pl.ds(c * lanes, lanes)
                code = jnp.broadcast_to(codes_ref[pl.ds(m, 1), cols], (width, lanes))
                low = jnp.bitwise_and(code, lanes - 1)
                value = jnp.take_along_axis(tables[0], low, axis=1, mode="promise_in_bounds")
                for t in range(1, len(tables)):
                    other = jnp.take_along_axis(tables[t], low, axis=1, mode="promise_in_bounds")
                    value = jnp.where(code >= t * lanes, other, value)
                recon[band, cols] = value
        loads[2 + i].wait()
        product = dot(recon[:, part].astype(bf16), res_ref[part, :])
        total[...] = product if i == 0 else total[...] + product
    if dp is None:
        return
    place = lax.axis_index("dp")
    size = outs[0].shape[0]
    for k, out in enumerate(outs):
        at = pl.multiple_of(jnp.bitwise_xor(place, k) * size, size)
        out[...] = cross[pl.ds(at, size), :].astype(out.dtype)


def cross_partial(codes_t, book_t, residuals, dp):
    rows, dim = residuals.shape
    cols = book_t.shape[0]
    if dp is None:
        shapes = (jax.ShapeDtypeStruct((cols, dim), f32),)
    else:
        shapes = tuple(
            jax.ShapeDtypeStruct((cols // dp, dim), bf16 if k else f32) for k in range(dp)
        )
    shapes += tuple(jax.ShapeDtypeStruct(x.shape, x.dtype) for x in (codes_t, book_t, residuals))
    return pl.pallas_call(
        functools.partial(cross_kernel, dp=dp),
        out_shape=shapes,
        in_specs=[pl.BlockSpec(memory_space=pltpu.HBM)] * 3,
        out_specs=(pl.BlockSpec(memory_space=pltpu.VMEM),) * len(shapes),
        scratch_shapes=[
            pltpu.VMEM((cols, rows), f32),
            pltpu.VMEM((cols, dim), f32),
            pltpu.SemaphoreType.DMA((2 + ROW_CHUNKS,)),
        ],
        compiler_params=pltpu.CompilerParams(vmem_limit_bytes=24 * MIB),
        name="cross_partial",
    )(*[pltpu.with_memory_space_constraint(x, pltpu.HBM) for x in (codes_t, book_t, residuals)])


def polar_kernel(*refs, blocks, pieces, chunk):
    block_refs = refs[:blocks]
    rot_b = refs[blocks]
    raw, gram, gram_b, poly_b, iterate, iterate_b = refs[blocks + 1 :]
    dim = raw.shape[0]
    own = rot_b.shape[0]
    steps = dim // chunk
    at = 0
    for block in block_refs:
        raw[pl.ds(at, block.shape[0]), :] = block[...]
        at += block.shape[0]

    def band_of(i):
        return pl.ds(i * chunk, chunk)

    def lower(j):
        return pl.ds(j * chunk, dim - j * chunk), pl.ds(j * chunk, chunk)

    def mirror(target, j, value):
        rows, cols = lower(j)
        target[rows, cols] = value.astype(bf16)
        for i in range(j + 1, steps):
            at = (i - j) * chunk
            target[cols, pl.ds(i * chunk, chunk)] = value[at : at + chunk, :].T.astype(bf16)

    def gram_of(source):
        r = lax.broadcasted_iota(jnp.int32, (chunk, chunk), 0)
        c = lax.broadcasted_iota(jnp.int32, (chunk, chunk), 1)
        trace = jnp.zeros((), f32)
        for j in range(steps):
            rows, cols = lower(j)
            part = dot_nt(source[rows, :], source[cols, :])
            gram[rows, cols] = part
            mirror(gram_b, j, part)
            trace = trace + jnp.sum(jnp.where(r == c, part[:chunk, :], 0.0))
        return trace

    def poly_of(wb, wc):
        for j in range(steps):
            rows, cols = lower(j)
            square = dot(gram_b[rows, :], gram_b[:, cols])
            mirror(poly_b, j, wb * gram[rows, cols] + wc * square)

    frob = gram_of(raw)
    scale2 = 1.0 / (frob + epsilon)
    scale = lax.rsqrt(frob + epsilon)
    poly_of(quintic_b * scale2, quintic_c * scale2 * scale2)

    for i in range(steps):
        cols = band_of(i)
        value = scale * (quintic_a * raw[:, cols].astype(f32) + dot(poly_b[...], raw[:, cols]))
        iterate[:, cols] = value
        iterate_b[:, cols] = value.astype(bf16)

    gram_of(iterate_b)
    poly_of(quintic_b, quintic_c)

    for i in range(steps):
        cols = band_of(i)
        value = quintic_a * iterate[:, cols] + dot(poly_b[...], iterate_b[:, cols])
        iterate[pl.ds(0, own), cols] = value[:own, :]
        raw[:, cols] = value.astype(bf16)
        part = dot_nt(raw[pl.ds(0, own), cols], raw[:, cols])
        g = part if i == 0 else g + part

    mine = pl.ds(0, own)
    image = dot(g.astype(bf16), raw[...])
    square = dot_nt(image.astype(bf16), raw[...])
    last = quintic_a * iterate[mine, :] + dot(
        (quintic_b * g + quintic_c * square).astype(bf16), raw[...]
    )
    size = own // pieces
    for p in range(pieces):
        to = 0
        if pieces > 1:
            to = pl.multiple_of(jnp.bitwise_xor(lax.axis_index("dp"), p) * size, size)
        rot_b[pl.ds(to, size), :] = last[p * size : (p + 1) * size, :].astype(bf16)


LOWS = 64


def onehot_kernel(codes_ref, onehot_ref, masks_ref, counts_ref):
    subs, rows_all = codes_ref.shape
    highs = counts_ref.shape[1] // LOWS
    low_word = lax.broadcasted_iota(jnp.int32, (LOWS, rows_all), 0)
    high_word = lax.broadcasted_iota(jnp.int32, (8, rows_all), 0)
    for m in range(subs):
        code = codes_ref[pl.ds(m, 1), :]
        low, high = jnp.bitwise_and(code, LOWS - 1), jnp.right_shift(code, 6)
        onehot = jnp.where(low_word == low, 1.0, 0.0).astype(bf16)
        onehot_ref[pl.ds(m * LOWS, LOWS), :] = onehot
        wide = masks_ref.shape[0] // subs
        row = lax.broadcasted_iota(jnp.int32, (wide, rows_all), 0)
        mask = jnp.where(row // (wide // highs) == high, 1.0, 0.0).astype(bf16)
        masks_ref[pl.ds(m * wide, wide), :] = mask
        part = dot_nt(jnp.where(high_word == high, 1.0, 0.0).astype(bf16), onehot)
        for h in range(highs):
            counts_ref[pl.ds(m, 1), pl.ds(h * LOWS, LOWS)] = part[h : h + 1, :]


def onehot_call(codes_t, words, width):
    subs, rows = codes_t.shape
    vmem = pl.BlockSpec(memory_space=pltpu.VMEM)
    return pl.pallas_call(
        onehot_kernel,
        out_shape=(
            jax.ShapeDtypeStruct((subs * LOWS, rows), bf16),
            jax.ShapeDtypeStruct((subs * width * (words // LOWS), rows), bf16),
            jax.ShapeDtypeStruct((subs, words), f32),
        ),
        in_specs=[vmem],
        out_specs=(vmem, vmem, vmem),
        compiler_params=pltpu.CompilerParams(vmem_limit_bytes=24 * MIB),
        cost_estimate=pl.CostEstimate(
            flops=2 * 256 * subs * LOWS * rows, bytes_accessed=2 * subs * LOWS * rows, transcendentals=0
        ),
        name="onehot",
    )(codes_t)


def sums_kernel(rot_ref, res_ref, onehot_ref, masks_ref, counts_ref, sent_ref, sums_ref):
    subs, words = counts_ref.shape
    own = rot_ref.shape[0]
    width = own // subs
    highs = words // LOWS
    group = min(subs, 256 // LOWS)
    rot_t = dot_nt(rot_ref[...], res_ref[...])
    for first in range(0, subs, group):
        values = []
        for m in range(first, first + group):
            band = rot_t[m * width : (m + 1) * width, :]
            values.append(jnp.concatenate([band] * highs, axis=0).astype(bf16))
        wide = group * highs * width
        tall = jnp.concatenate(values, axis=0) * masks_ref[pl.ds(first // group * wide, wide), :]
        part = dot_nt(tall, onehot_ref[pl.ds(first * LOWS, group * LOWS), :])
        for s in range(group):
            for h in range(highs):
                at = (s * highs + h) * width
                sums_ref[pl.ds((first + s) * width, width), pl.ds(h * LOWS, LOWS)] = part[
                    at : at + width, s * LOWS : (s + 1) * LOWS
                ]
    sent_ref[pl.ds(0, own), :] = sums_ref[...].astype(bf16)
    sent_ref[pl.ds(own, subs), :] = counts_ref[...].astype(bf16)


def rotated_kernel(rot_ref, res_ref, rotated_ref):
    rows_all = res_ref.shape[0]
    step = 512

    @pl.loop(0, rows_all // step)
    def _(i):
        rows = pl.ds(pl.multiple_of(i * step, step), step)
        rotated_ref[rows, :] = dot_nt(res_ref[rows, :], rot_ref[...])


def polar(block_list, own, pieces):
    dim = block_list[0].shape[1]
    vmem = pl.BlockSpec(memory_space=pltpu.VMEM)
    kernel = functools.partial(polar_kernel, blocks=len(block_list), pieces=pieces, chunk=256)
    return pl.pallas_call(
        kernel,
        out_shape=jax.ShapeDtypeStruct((own, dim), bf16),
        in_specs=[vmem] * len(block_list),
        out_specs=vmem,
        scratch_shapes=[
            pltpu.VMEM((dim, dim), bf16),
            pltpu.VMEM((dim, dim), f32),
            pltpu.VMEM((dim, dim), bf16),
            pltpu.VMEM((dim, dim), bf16),
            pltpu.VMEM((dim, dim), f32),
            pltpu.VMEM((dim, dim), bf16),
        ],
        compiler_params=pltpu.CompilerParams(vmem_limit_bytes=36 * MIB),
        name="polar",
    )(*block_list)


def share_kernel(*refs):
    total = refs[0][...].astype(f32)
    for part in refs[1:-1]:
        total = total + part[...].astype(f32)
    refs[-1][...] = total.astype(refs[-1].dtype)


def book_kernel(book_ref, *refs):
    sums, out_ref = refs[:-1], refs[-1]
    own = book_ref.shape[0]
    subs = sums[0].shape[0] - own
    width = own // subs
    total = sums[0][...].astype(f32)
    for part in sums[1:]:
        total = total + part[...].astype(f32)
    for m in range(subs):
        band = pl.ds(m * width, width)
        count = total[own + m : own + m + 1, :] + prior_weight
        part = total[m * width : (m + 1) * width, :]
        out_ref[band, :] = (part + prior_weight * book_ref[band, :]) / count


def small_call(kernel, name, shape, dtype, *operands, scratch=()):
    vmem = pl.BlockSpec(memory_space=pltpu.VMEM)
    return pl.pallas_call(
        kernel,
        out_shape=jax.ShapeDtypeStruct(shape, dtype),
        in_specs=[vmem] * len(operands),
        out_specs=vmem,
        scratch_shapes=scratch,
        compiler_params=pltpu.CompilerParams(vmem_limit_bytes=24 * MIB),
        name=name,
    )(*operands)


def swap(value, axis, size, mask, odd_mask=None):
    odd_mask = mask if odd_mask is None else odd_mask
    return lax.ppermute(value, axis, [(i, i ^ (odd_mask if i % 2 else mask)) for i in range(size)])


def make_body(dp, code):
    def body(residuals, codes, codebook):
        rows, dim = residuals.shape
        subs, words, width = codebook.shape
        own = subs * width
        codes_t = codes.T
        book_t = jnp.transpose(codebook, (0, 2, 1)).reshape(own, words)
        size = own // dp
        thin = size % 16 != 0
        if thin:
            place = lax.axis_index("dp")
            partial, codes_v, book_v, res_v = cross_partial(codes_t, book_t, residuals, None)
            cut = [
                lax.dynamic_slice_in_dim(partial, (place ^ k) * size, size, 0) for k in range(dp)
            ]
            parts = [cut[0]] + [part.astype(bf16) for part in cut[1:]]
        else:
            *parts, codes_v, book_v, res_v = cross_partial(codes_t, book_t, residuals, dp)
        far_first = range(dp - 1, 0, -1)
        got = [swap(parts[k], "dp", dp, k) for k in far_first]
        ready = onehot_call(codes_v, words, width)
        got, ready = lax.optimization_barrier((got, ready))
        piece = small_call(share_kernel, "share", (size, dim), bf16, parts[0], *got)
        pieces = {0: piece}
        for k in far_first:
            pieces[k] = swap(piece, "dp", dp, k)
        if thin:
            block = jnp.zeros((own, dim), bf16)
            for k in range(dp):
                block = lax.dynamic_update_slice_in_dim(block, pieces[k], (place ^ k) * size, 0)
            held = [block]
        else:
            half = max(dp // 2, 1)
            held = [
                jnp.concatenate([pieces[k] for k in range(at, min(at + half, dp))], axis=0)
                for at in range(0, dp, half)
            ]
        strides = [1 << b for b in reversed(range(code.bit_length() - 1))]
        far = strides[:-1]
        for even, odd in zip(far, far[::-1]):
            held = held + [swap(t, "code", code, even, odd) for t in held]
        for stride in strides[-1:]:
            held = held + [swap(t, "code", code, stride) for t in held]
        rotation_t = polar(held, own, 1 if thin else dp)
        scratch = [pltpu.VMEM((own, words), f32)]
        operands = (rotation_t, res_v, *ready)
        sums = small_call(sums_kernel, "sums", (own + subs, words), bf16, *operands, scratch=scratch)
        rotated = small_call(rotated_kernel, "rotated", (rows, own), f32, rotation_t, res_v)
        others = [swap(sums, "dp", dp, k) for k in range(1, dp)]
        book = small_call(book_kernel, "book", (own, words), f32, book_v, sums, *others)
        return rotated, jnp.transpose(book.reshape(subs, width, words), (0, 2, 1))

    return body


def solution(mesh):
    dp, code = mesh.shape["dp"], mesh.shape["code"]
    in_specs = (P("dp", None), P("dp", "code"), P("code", None, None))
    out_specs = (P("dp", "code"), P("code", None, None))
    return jax.shard_map(
        make_body(dp, code), mesh=mesh, in_specs=in_specs, out_specs=out_specs, check_vma=False
    )
```

```python
import functools

import jax
import jax.numpy as jnp
from jax import lax
from jax.experimental import pallas as pl
from jax.experimental.pallas import tpu as pltpu
from jax.sharding import PartitionSpec as P

quintic_a = 3.4445
quintic_b = -4.775
quintic_c = 2.0315
prior_weight = 8.0
epsilon = 1e-06
f32, bf16 = jnp.float32, jnp.bfloat16
MIB = 1024 * 1024
ROW_CHUNKS = 4
NT = (((1,), (1,)), ((), ()))


def dot(left, right):
    return jnp.dot(left, right, preferred_element_type=f32)


def dot_nt(left, right):
    return lax.dot_general(left, right, NT, preferred_element_type=f32)


def cross_kernel(codes_hbm, book_hbm, res_hbm, *refs, dp):
    outs = refs[: dp or 1]
    codes_ref, book_ref, res_ref, recon, cross, sems = refs[dp or 1 :]
    subs, rows = codes_ref.shape
    width = book_ref.shape[0] // subs
    words = book_ref.shape[1]
    lanes = 128
    chunks = sems.shape[0] - 2
    step = rows // chunks
    loads = [
        pltpu.make_async_copy(codes_hbm, codes_ref, sems.at[0]),
        pltpu.make_async_copy(book_hbm, book_ref, sems.at[1]),
    ]
    for i in range(chunks):
        part = pl.ds(i * step, step)
        loads.append(pltpu.make_async_copy(res_hbm.at[part], res_ref.at[part], sems.at[2 + i]))
    for load in loads:
        load.start()
    loads[0].wait()
    loads[1].wait()
    total = outs[0] if dp is None else cross
    for i in range(chunks):
        part = pl.ds(i * step, step)
        for m in range(subs):
            band = pl.ds(m * width, width)
            tables = [book_ref[band, pl.ds(t * lanes, lanes)] for t in range(words // lanes)]
            for c in range(i * step // lanes, (i + 1) * step // lanes):
                cols = pl.ds(c * lanes, lanes)
                code = jnp.broadcast_to(codes_ref[pl.ds(m, 1), cols], (width, lanes))
                low = jnp.bitwise_and(code, lanes - 1)
                value = jnp.take_along_axis(tables[0], low, axis=1, mode="promise_in_bounds")
                for t in range(1, len(tables)):
                    other = jnp.take_along_axis(tables[t], low, axis=1, mode="promise_in_bounds")
                    value = jnp.where(code >= t * lanes, other, value)
                recon[band, cols] = value
        loads[2 + i].wait()
        product = dot(recon[:, part].astype(bf16), res_ref[part, :])
        total[...] = product if i == 0 else total[...] + product
    if dp is None:
        return
    place = lax.axis_index("dp")
    size = outs[0].shape[0]
    for k, out in enumerate(outs):
        at = pl.multiple_of(jnp.bitwise_xor(place, k) * size, size)
        out[...] = cross[pl.ds(at, size), :].astype(out.dtype)


def cross_partial(codes_t, book_t, residuals, dp):
    rows, dim = residuals.shape
    cols = book_t.shape[0]
    if dp is None:
        shapes = (jax.ShapeDtypeStruct((cols, dim), f32),)
    else:
        shapes = tuple(
            jax.ShapeDtypeStruct((cols // dp, dim), bf16 if k else f32) for k in range(dp)
        )
    shapes += tuple(jax.ShapeDtypeStruct(x.shape, x.dtype) for x in (codes_t, book_t, residuals))
    return pl.pallas_call(
        functools.partial(cross_kernel, dp=dp),
        out_shape=shapes,
        in_specs=[pl.BlockSpec(memory_space=pltpu.HBM)] * 3,
        out_specs=(pl.BlockSpec(memory_space=pltpu.VMEM),) * len(shapes),
        scratch_shapes=[
            pltpu.VMEM((cols, rows), f32),
            pltpu.VMEM((cols, dim), f32),
            pltpu.SemaphoreType.DMA((2 + ROW_CHUNKS,)),
        ],
        compiler_params=pltpu.CompilerParams(vmem_limit_bytes=24 * MIB),
        name="cross_partial",
    )(*[pltpu.with_memory_space_constraint(x, pltpu.HBM) for x in (codes_t, book_t, residuals)])


def polar_kernel(*refs, blocks, pieces, chunk):
    block_refs = refs[:blocks]
    rot_b = refs[blocks]
    raw, gram, gram_b, poly_b, iterate, iterate_b = refs[blocks + 1 :]
    dim = raw.shape[0]
    own = rot_b.shape[0]
    steps = dim // chunk
    at = 0
    for block in block_refs:
        raw[pl.ds(at, block.shape[0]), :] = block[...]
        at += block.shape[0]

    def band_of(i):
        return pl.ds(i * chunk, chunk)

    def lower(j):
        return pl.ds(j * chunk, dim - j * chunk), pl.ds(j * chunk, chunk)

    def mirror(target, j, value):
        rows, cols = lower(j)
        target[rows, cols] = value.astype(bf16)
        for i in range(j + 1, steps):
            at = (i - j) * chunk
            target[cols, pl.ds(i * chunk, chunk)] = value[at : at + chunk, :].T.astype(bf16)

    def gram_of(source):
        r = lax.broadcasted_iota(jnp.int32, (chunk, chunk), 0)
        c = lax.broadcasted_iota(jnp.int32, (chunk, chunk), 1)
        trace = jnp.zeros((), f32)
        for j in range(steps):
            rows, cols = lower(j)
            part = dot_nt(source[rows, :], source[cols, :])
            gram[rows, cols] = part
            mirror(gram_b, j, part)
            trace = trace + jnp.sum(jnp.where(r == c, part[:chunk, :], 0.0))
        return trace

    def poly_of(wb, wc):
        for j in range(steps):
            rows, cols = lower(j)
            square = dot(gram_b[rows, :], gram_b[:, cols])
            mirror(poly_b, j, wb * gram[rows, cols] + wc * square)

    frob = gram_of(raw)
    scale2 = 1.0 / (frob + epsilon)
    scale = lax.rsqrt(frob + epsilon)
    poly_of(quintic_b * scale2, quintic_c * scale2 * scale2)

    for i in range(steps):
        cols = band_of(i)
        value = scale * (quintic_a * raw[:, cols].astype(f32) + dot(poly_b[...], raw[:, cols]))
        iterate[:, cols] = value
        iterate_b[:, cols] = value.astype(bf16)

    gram_of(iterate_b)
    poly_of(quintic_b, quintic_c)

    for i in range(steps):
        cols = band_of(i)
        value = quintic_a * iterate[:, cols] + dot(poly_b[...], iterate_b[:, cols])
        iterate[pl.ds(0, own), cols] = value[:own, :]
        raw[:, cols] = value.astype(bf16)

    mine = pl.ds(0, own)
    g = dot_nt(raw[mine, :], raw[...])
    image = dot(g.astype(bf16), raw[...])
    square = dot_nt(image.astype(bf16), raw[...])
    last = quintic_a * iterate[mine, :] + dot(
        (quintic_b * g + quintic_c * square).astype(bf16), raw[...]
    )
    size = own // pieces
    for p in range(pieces):
        to = 0
        if pieces > 1:
            to = pl.multiple_of(jnp.bitwise_xor(lax.axis_index("dp"), p) * size, size)
        rot_b[pl.ds(to, size), :] = last[p * size : (p + 1) * size, :].astype(bf16)


LOWS = 64


def onehot_kernel(codes_ref, onehot_ref, masks_ref, counts_ref):
    subs, rows_all = codes_ref.shape
    highs = counts_ref.shape[1] // LOWS
    wide = masks_ref.shape[0] // subs
    group = min(subs, 256 // LOWS)
    low_word = lax.broadcasted_iota(jnp.int32, (LOWS, rows_all), 0)
    high_word = lax.broadcasted_iota(jnp.int32, (8, rows_all), 0)
    row = lax.broadcasted_iota(jnp.int32, (wide, rows_all), 0)
    for first in range(0, subs, group):
        onehots, marks = [], []
        for m in range(first, first + group):
            code = codes_ref[pl.ds(m, 1), :]
            low, high = jnp.bitwise_and(code, LOWS - 1), jnp.right_shift(code, 6)
            onehots.append(jnp.where(low_word == low, 1.0, 0.0).astype(bf16))
            marks.append(jnp.where(high_word == high, 1.0, 0.0))
            mask = jnp.where(row // (wide // highs) == high, 1.0, 0.0).astype(bf16)
            masks_ref[pl.ds(m * wide, wide), :] = mask
        onehot = jnp.concatenate(onehots, axis=0).T
        onehot_ref[:, pl.ds(first * LOWS, group * LOWS)] = onehot
        part = dot(jnp.concatenate(marks, axis=0).astype(bf16), onehot)
        for s in range(group):
            for h in range(highs):
                counts_ref[pl.ds(first + s, 1), pl.ds(h * LOWS, LOWS)] = part[
                    s * 8 + h : s * 8 + h + 1, s * LOWS : (s + 1) * LOWS
                ]


def onehot_call(codes_t, words, width):
    subs, rows = codes_t.shape
    vmem = pl.BlockSpec(memory_space=pltpu.VMEM)
    return pl.pallas_call(
        onehot_kernel,
        out_shape=(
            jax.ShapeDtypeStruct((rows, subs * LOWS), bf16),
            jax.ShapeDtypeStruct((subs * width * (words // LOWS), rows), bf16),
            jax.ShapeDtypeStruct((subs, words), f32),
        ),
        in_specs=[vmem],
        out_specs=(vmem, vmem, vmem),
        compiler_params=pltpu.CompilerParams(vmem_limit_bytes=24 * MIB),
        cost_estimate=pl.CostEstimate(
            flops=2 * 256 * subs * LOWS * rows, bytes_accessed=2 * subs * LOWS * rows, transcendentals=0
        ),
        name="onehot",
    )(codes_t)


def sums_kernel(rot_ref, res_ref, onehot_ref, masks_ref, counts_ref, sent_ref, sums_ref):
    subs, words = counts_ref.shape
    own = rot_ref.shape[0]
    width = own // subs
    highs = words // LOWS
    group = min(subs, 256 // LOWS)
    rot_t = dot_nt(rot_ref[...], res_ref[...])
    for first in range(0, subs, group):
        values = []
        for m in range(first, first + group):
            band = rot_t[m * width : (m + 1) * width, :]
            values.append(jnp.concatenate([band] * highs, axis=0).astype(bf16))
        wide = group * highs * width
        tall = jnp.concatenate(values, axis=0) * masks_ref[pl.ds(first // group * wide, wide), :]
        part = dot(tall, onehot_ref[:, pl.ds(first * LOWS, group * LOWS)])
        for s in range(group):
            for h in range(highs):
                at = (s * highs + h) * width
                sums_ref[pl.ds((first + s) * width, width), pl.ds(h * LOWS, LOWS)] = part[
                    at : at + width, s * LOWS : (s + 1) * LOWS
                ]
    sent_ref[pl.ds(0, own), :] = sums_ref[...].astype(bf16)
    sent_ref[pl.ds(own, subs), :] = counts_ref[...].astype(bf16)


def rotated_kernel(rot_ref, res_ref, rotated_ref):
    rows_all = res_ref.shape[0]
    step = 512

    @pl.loop(0, rows_all // step)
    def _(i):
        rows = pl.ds(pl.multiple_of(i * step, step), step)
        rotated_ref[rows, :] = dot_nt(res_ref[rows, :], rot_ref[...])


def polar(block_list, own, pieces):
    dim = block_list[0].shape[1]
    vmem = pl.BlockSpec(memory_space=pltpu.VMEM)
    kernel = functools.partial(polar_kernel, blocks=len(block_list), pieces=pieces, chunk=256)
    return pl.pallas_call(
        kernel,
        out_shape=jax.ShapeDtypeStruct((own, dim), bf16),
        in_specs=[vmem] * len(block_list),
        out_specs=vmem,
        scratch_shapes=[
            pltpu.VMEM((dim, dim), bf16),
            pltpu.VMEM((dim, dim), f32),
            pltpu.VMEM((dim, dim), bf16),
            pltpu.VMEM((dim, dim), bf16),
            pltpu.VMEM((dim, dim), f32),
            pltpu.VMEM((dim, dim), bf16),
        ],
        compiler_params=pltpu.CompilerParams(vmem_limit_bytes=36 * MIB),
        name="polar",
    )(*block_list)


def share_kernel(*refs):
    total = refs[0][...].astype(f32)
    for part in refs[1:-1]:
        total = total + part[...].astype(f32)
    refs[-1][...] = total.astype(refs[-1].dtype)


def book_kernel(book_ref, *refs):
    sums, out_ref = refs[:-1], refs[-1]
    own = book_ref.shape[0]
    subs = sums[0].shape[0] - own
    width = own // subs
    total = sums[0][...].astype(f32)
    for part in sums[1:]:
        total = total + part[...].astype(f32)
    for m in range(subs):
        band = pl.ds(m * width, width)
        count = total[own + m : own + m + 1, :] + prior_weight
        part = total[m * width : (m + 1) * width, :]
        out_ref[band, :] = (part + prior_weight * book_ref[band, :]) / count


def small_call(kernel, name, shape, dtype, *operands, scratch=()):
    vmem = pl.BlockSpec(memory_space=pltpu.VMEM)
    return pl.pallas_call(
        kernel,
        out_shape=jax.ShapeDtypeStruct(shape, dtype),
        in_specs=[vmem] * len(operands),
        out_specs=vmem,
        scratch_shapes=scratch,
        compiler_params=pltpu.CompilerParams(vmem_limit_bytes=24 * MIB),
        name=name,
    )(*operands)


def swap(value, axis, size, mask, odd_mask=None):
    odd_mask = mask if odd_mask is None else odd_mask
    return lax.ppermute(value, axis, [(i, i ^ (odd_mask if i % 2 else mask)) for i in range(size)])


def make_body(dp, code):
    def body(residuals, codes, codebook):
        rows, dim = residuals.shape
        subs, words, width = codebook.shape
        own = subs * width
        codes_t = codes.T
        book_t = jnp.transpose(codebook, (0, 2, 1)).reshape(own, words)
        size = own // dp
        thin = size % 16 != 0
        if thin:
            place = lax.axis_index("dp")
            partial, codes_v, book_v, res_v = cross_partial(codes_t, book_t, residuals, None)
            cut = [
                lax.dynamic_slice_in_dim(partial, (place ^ k) * size, size, 0) for k in range(dp)
            ]
            parts = [cut[0]] + [part.astype(bf16) for part in cut[1:]]
        else:
            *parts, codes_v, book_v, res_v = cross_partial(codes_t, book_t, residuals, dp)
        far_first = range(dp - 1, 0, -1)
        got = [swap(parts[k], "dp", dp, k) for k in far_first]
        ready = onehot_call(codes_v, words, width)
        got, ready = lax.optimization_barrier((got, ready))
        piece = small_call(share_kernel, "share", (size, dim), bf16, parts[0], *got)
        pieces = {0: piece}
        for k in far_first:
            pieces[k] = swap(piece, "dp", dp, k)
        if thin:
            block = jnp.zeros((own, dim), bf16)
            for k in range(dp):
                block = lax.dynamic_update_slice_in_dim(block, pieces[k], (place ^ k) * size, 0)
            held = [block]
        else:
            half = max(dp // 2, 1)
            held = [
                jnp.concatenate([pieces[k] for k in range(at, min(at + half, dp))], axis=0)
                for at in range(0, dp, half)
            ]
        strides = [1 << b for b in reversed(range(code.bit_length() - 1))]
        far = strides[:-1]
        for even, odd in zip(far, far[::-1]):
            held = held + [swap(t, "code", code, even, odd) for t in held]
        for stride in strides[-1:]:
            held = held + [swap(t, "code", code, stride) for t in held]
        rotation_t = polar(held, own, 1 if thin else dp)
        scratch = [pltpu.VMEM((own, words), f32)]
        operands = (rotation_t, res_v, *ready)
        sums = small_call(sums_kernel, "sums", (own + subs, words), bf16, *operands, scratch=scratch)
        rotated = small_call(rotated_kernel, "rotated", (rows, own), f32, rotation_t, res_v)
        others = [swap(sums, "dp", dp, k) for k in range(1, dp)]
        book = small_call(book_kernel, "book", (own, words), f32, book_v, sums, *others)
        return rotated, jnp.transpose(book.reshape(subs, width, words), (0, 2, 1))

    return body


def solution(mesh):
    dp, code = mesh.shape["dp"], mesh.shape["code"]
    in_specs = (P("dp", None), P("dp", "code"), P("code", None, None))
    out_specs = (P("dp", "code"), P("code", None, None))
    return jax.shard_map(
        make_body(dp, code), mesh=mesh, in_specs=in_specs, out_specs=out_specs, check_vma=False
    )
```

```python
import functools

import jax
import jax.numpy as jnp
from jax import lax
from jax.experimental import pallas as pl
from jax.experimental.pallas import tpu as pltpu
from jax.sharding import PartitionSpec as P

quintic_a = 3.4445
quintic_b = -4.775
quintic_c = 2.0315
prior_weight = 8.0
epsilon = 1e-06
f32, bf16 = jnp.float32, jnp.bfloat16
MIB = 1024 * 1024
ROW_CHUNKS = 4
NT = (((1,), (1,)), ((), ()))


def dot(left, right):
    return jnp.dot(left, right, preferred_element_type=f32)


def dot_nt(left, right):
    return lax.dot_general(left, right, NT, preferred_element_type=f32)


def cross_kernel(codes_hbm, book_hbm, res_hbm, *refs, dp):
    outs = refs[: dp or 1]
    codes_ref, book_ref, res_ref, recon, cross, sems = refs[dp or 1 :]
    subs, rows = codes_ref.shape
    width = book_ref.shape[0] // subs
    words = book_ref.shape[1]
    lanes = 128
    chunks = sems.shape[0] - 2
    step = rows // chunks
    loads = [
        pltpu.make_async_copy(codes_hbm, codes_ref, sems.at[0]),
        pltpu.make_async_copy(book_hbm, book_ref, sems.at[1]),
    ]
    for i in range(chunks):
        part = pl.ds(i * step, step)
        loads.append(pltpu.make_async_copy(res_hbm.at[part], res_ref.at[part], sems.at[2 + i]))
    for load in loads:
        load.start()
    loads[0].wait()
    loads[1].wait()
    total = outs[0] if dp is None else cross
    for i in range(chunks):
        part = pl.ds(i * step, step)
        for m in range(subs):
            band = pl.ds(m * width, width)
            tables = [book_ref[band, pl.ds(t * lanes, lanes)] for t in range(words // lanes)]
            for c in range(i * step // lanes, (i + 1) * step // lanes):
                cols = pl.ds(c * lanes, lanes)
                code = jnp.broadcast_to(codes_ref[pl.ds(m, 1), cols], (width, lanes))
                low = jnp.bitwise_and(code, lanes - 1)
                value = jnp.take_along_axis(tables[0], low, axis=1, mode="promise_in_bounds")
                for t in range(1, len(tables)):
                    other = jnp.take_along_axis(tables[t], low, axis=1, mode="promise_in_bounds")
                    value = jnp.where(code >= t * lanes, other, value)
                recon[band, cols] = value
        loads[2 + i].wait()
        product = dot(recon[:, part].astype(bf16), res_ref[part, :])
        total[...] = product if i == 0 else total[...] + product
    if dp is None:
        return
    place = lax.axis_index("dp")
    size = outs[0].shape[0]
    for k, out in enumerate(outs):
        at = pl.multiple_of(jnp.bitwise_xor(place, k) * size, size)
        out[...] = cross[pl.ds(at, size), :].astype(out.dtype)


def cross_partial(codes_t, book_t, residuals, dp):
    rows, dim = residuals.shape
    cols = book_t.shape[0]
    if dp is None:
        shapes = (jax.ShapeDtypeStruct((cols, dim), f32),)
    else:
        shapes = tuple(
            jax.ShapeDtypeStruct((cols // dp, dim), bf16 if k else f32) for k in range(dp)
        )
    shapes += tuple(jax.ShapeDtypeStruct(x.shape, x.dtype) for x in (codes_t, book_t, residuals))
    return pl.pallas_call(
        functools.partial(cross_kernel, dp=dp),
        out_shape=shapes,
        in_specs=[pl.BlockSpec(memory_space=pltpu.HBM)] * 3,
        out_specs=(pl.BlockSpec(memory_space=pltpu.VMEM),) * len(shapes),
        scratch_shapes=[
            pltpu.VMEM((cols, rows), f32),
            pltpu.VMEM((cols, dim), f32),
            pltpu.SemaphoreType.DMA((2 + ROW_CHUNKS,)),
        ],
        compiler_params=pltpu.CompilerParams(vmem_limit_bytes=24 * MIB),
        name="cross_partial",
    )(*[pltpu.with_memory_space_constraint(x, pltpu.HBM) for x in (codes_t, book_t, residuals)])


def polar_kernel(*refs, blocks, pieces, chunk):
    block_refs = refs[:blocks]
    rot_b = refs[blocks]
    raw, gram, gram_b, poly_b, iterate, iterate_b, turned = refs[blocks + 1 :]
    dim = raw.shape[0]
    own = rot_b.shape[0]
    steps = dim // chunk
    at = 0
    for block in block_refs:
        raw[pl.ds(at, block.shape[0]), :] = block[...]
        at += block.shape[0]

    def band_of(i):
        return pl.ds(i * chunk, chunk)

    def lower(j):
        return pl.ds(j * chunk, dim - j * chunk), pl.ds(j * chunk, chunk)

    def mirror(target, j, value):
        rows, cols = lower(j)
        target[rows, cols] = value.astype(bf16)
        for i in range(j + 1, steps):
            at = (i - j) * chunk
            target[cols, pl.ds(i * chunk, chunk)] = value[at : at + chunk, :].T.astype(bf16)

    def gram_of(source, transposed=None):
        r = lax.broadcasted_iota(jnp.int32, (chunk, chunk), 0)
        c = lax.broadcasted_iota(jnp.int32, (chunk, chunk), 1)
        trace = jnp.zeros((), f32)
        for j in range(steps):
            rows, cols = lower(j)
            if transposed is None:
                part = dot_nt(source[rows, :], source[cols, :])
            else:
                part = dot(source[rows, :], transposed[:, cols])
            gram[rows, cols] = part
            mirror(gram_b, j, part)
            trace = trace + jnp.sum(jnp.where(r == c, part[:chunk, :], 0.0))
        return trace

    def poly_of(wb, wc):
        for j in range(steps):
            rows, cols = lower(j)
            square = dot(gram_b[rows, :], gram_b[:, cols])
            mirror(poly_b, j, wb * gram[rows, cols] + wc * square)

    frob = gram_of(raw)
    scale2 = 1.0 / (frob + epsilon)
    scale = lax.rsqrt(frob + epsilon)
    poly_of(quintic_b * scale2, quintic_c * scale2 * scale2)

    for i in range(steps):
        cols = band_of(i)
        value = scale * (quintic_a * raw[:, cols].astype(f32) + dot(poly_b[...], raw[:, cols]))
        iterate[:, cols] = value
        rounded = value.astype(bf16)
        iterate_b[:, cols] = rounded
        turned[cols, :] = rounded.T

    gram_of(iterate_b, turned)
    poly_of(quintic_b, quintic_c)

    for i in range(steps):
        cols = band_of(i)
        value = quintic_a * iterate[:, cols] + dot(poly_b[...], iterate_b[:, cols])
        iterate[pl.ds(0, own), cols] = value[:own, :]
        rounded = value.astype(bf16)
        raw[:, cols] = rounded
        turned[cols, :] = rounded.T

    mine = pl.ds(0, own)
    g = dot(raw[mine, :], turned[...])
    image = dot(g.astype(bf16), raw[...])
    square = dot(image.astype(bf16), turned[...])
    last = quintic_a * iterate[mine, :] + dot(
        (quintic_b * g + quintic_c * square).astype(bf16), raw[...]
    )
    size = own // pieces
    for p in range(pieces):
        to = 0
        if pieces > 1:
            to = pl.multiple_of(jnp.bitwise_xor(lax.axis_index("dp"), p) * size, size)
        rot_b[pl.ds(to, size), :] = last[p * size : (p + 1) * size, :].astype(bf16)


LOWS = 64


def onehot_kernel(codes_ref, res_ref, onehot_ref, masks_ref, counts_ref, turned_ref):
    subs, rows_all = codes_ref.shape
    step = 256
    for i in range(rows_all // step):
        rows = pl.ds(i * step, step)
        turned_ref[:, rows] = res_ref[rows, :].T
    highs = counts_ref.shape[1] // LOWS
    wide = masks_ref.shape[0] // subs
    group = min(subs, 256 // LOWS)
    low_word = lax.broadcasted_iota(jnp.int32, (LOWS, rows_all), 0)
    high_word = lax.broadcasted_iota(jnp.int32, (8, rows_all), 0)
    row = lax.broadcasted_iota(jnp.int32, (wide, rows_all), 0)
    for first in range(0, subs, group):
        onehots, marks = [], []
        for m in range(first, first + group):
            code = codes_ref[pl.ds(m, 1), :]
            low, high = jnp.bitwise_and(code, LOWS - 1), jnp.right_shift(code, 6)
            onehots.append(jnp.where(low_word == low, 1.0, 0.0).astype(bf16))
            marks.append(jnp.where(high_word == high, 1.0, 0.0))
            mask = jnp.where(row // (wide // highs) == high, 1.0, 0.0).astype(bf16)
            masks_ref[pl.ds(m * wide, wide), :] = mask
        onehot = jnp.concatenate(onehots, axis=0).T
        onehot_ref[:, pl.ds(first * LOWS, group * LOWS)] = onehot
        part = dot(jnp.concatenate(marks, axis=0).astype(bf16), onehot)
        for s in range(group):
            for h in range(highs):
                counts_ref[pl.ds(first + s, 1), pl.ds(h * LOWS, LOWS)] = part[
                    s * 8 + h : s * 8 + h + 1, s * LOWS : (s + 1) * LOWS
                ]


def onehot_call(codes_t, residuals, words, width):
    subs, rows = codes_t.shape
    vmem = pl.BlockSpec(memory_space=pltpu.VMEM)
    return pl.pallas_call(
        onehot_kernel,
        out_shape=(
            jax.ShapeDtypeStruct((rows, subs * LOWS), bf16),
            jax.ShapeDtypeStruct((subs * width * (words // LOWS), rows), bf16),
            jax.ShapeDtypeStruct((subs, words), f32),
            jax.ShapeDtypeStruct(residuals.shape[::-1], bf16),
        ),
        in_specs=[vmem, vmem],
        out_specs=(vmem,) * 4,
        compiler_params=pltpu.CompilerParams(vmem_limit_bytes=24 * MIB),
        cost_estimate=pl.CostEstimate(
            flops=2 * 256 * subs * LOWS * rows, bytes_accessed=2 * subs * LOWS * rows, transcendentals=0
        ),
        name="onehot",
    )(codes_t, residuals)


def sums_kernel(rot_ref, res_ref, onehot_ref, masks_ref, counts_ref, sent_ref, sums_ref):
    subs, words = counts_ref.shape
    own = rot_ref.shape[0]
    width = own // subs
    highs = words // LOWS
    group = min(subs, 256 // LOWS)
    rot_t = dot(rot_ref[...], res_ref[...])
    for first in range(0, subs, group):
        values = []
        for m in range(first, first + group):
            band = rot_t[m * width : (m + 1) * width, :]
            values.append(jnp.concatenate([band] * highs, axis=0).astype(bf16))
        wide = group * highs * width
        tall = jnp.concatenate(values, axis=0) * masks_ref[pl.ds(first // group * wide, wide), :]
        part = dot(tall, onehot_ref[:, pl.ds(first * LOWS, group * LOWS)])
        for s in range(group):
            for h in range(highs):
                at = (s * highs + h) * width
                sums_ref[pl.ds((first + s) * width, width), pl.ds(h * LOWS, LOWS)] = part[
                    at : at + width, s * LOWS : (s + 1) * LOWS
                ]
    sent_ref[pl.ds(0, own), :] = sums_ref[...].astype(bf16)
    sent_ref[pl.ds(own, subs), :] = counts_ref[...].astype(bf16)


def rotated_kernel(rot_ref, res_ref, rotated_ref):
    rows_all = res_ref.shape[0]
    step = 512

    @pl.loop(0, rows_all // step)
    def _(i):
        rows = pl.ds(pl.multiple_of(i * step, step), step)
        rotated_ref[rows, :] = dot_nt(res_ref[rows, :], rot_ref[...])


def polar(block_list, own, pieces):
    dim = block_list[0].shape[1]
    vmem = pl.BlockSpec(memory_space=pltpu.VMEM)
    kernel = functools.partial(polar_kernel, blocks=len(block_list), pieces=pieces, chunk=256)
    return pl.pallas_call(
        kernel,
        out_shape=jax.ShapeDtypeStruct((own, dim), bf16),
        in_specs=[vmem] * len(block_list),
        out_specs=vmem,
        scratch_shapes=[
            pltpu.VMEM((dim, dim), bf16),
            pltpu.VMEM((dim, dim), f32),
            pltpu.VMEM((dim, dim), bf16),
            pltpu.VMEM((dim, dim), bf16),
            pltpu.VMEM((dim, dim), f32),
            pltpu.VMEM((dim, dim), bf16),
            pltpu.VMEM((dim, dim), bf16),
        ],
        compiler_params=pltpu.CompilerParams(vmem_limit_bytes=30 * MIB),
        name="polar",
    )(*block_list)


def share_kernel(*refs):
    total = refs[0][...].astype(f32)
    for part in refs[1:-1]:
        total = total + part[...].astype(f32)
    refs[-1][...] = total.astype(refs[-1].dtype)


def book_kernel(book_ref, *refs):
    sums, out_ref = refs[:-1], refs[-1]
    own = book_ref.shape[0]
    subs = sums[0].shape[0] - own
    width = own // subs
    total = sums[0][...].astype(f32)
    for part in sums[1:]:
        total = total + part[...].astype(f32)
    for m in range(subs):
        band = pl.ds(m * width, width)
        count = total[own + m : own + m + 1, :] + prior_weight
        part = total[m * width : (m + 1) * width, :]
        out_ref[band, :] = (part + prior_weight * book_ref[band, :]) / count


def small_call(kernel, name, shape, dtype, *operands, scratch=()):
    vmem = pl.BlockSpec(memory_space=pltpu.VMEM)
    return pl.pallas_call(
        kernel,
        out_shape=jax.ShapeDtypeStruct(shape, dtype),
        in_specs=[vmem] * len(operands),
        out_specs=vmem,
        scratch_shapes=scratch,
        compiler_params=pltpu.CompilerParams(vmem_limit_bytes=24 * MIB),
        name=name,
    )(*operands)


def swap(value, axis, size, mask, odd_mask=None):
    odd_mask = mask if odd_mask is None else odd_mask
    return lax.ppermute(value, axis, [(i, i ^ (odd_mask if i % 2 else mask)) for i in range(size)])


def make_body(dp, code):
    def body(residuals, codes, codebook):
        rows, dim = residuals.shape
        subs, words, width = codebook.shape
        own = subs * width
        codes_t = codes.T
        book_t = jnp.transpose(codebook, (0, 2, 1)).reshape(own, words)
        size = own // dp
        thin = size % 16 != 0
        if thin:
            place = lax.axis_index("dp")
            partial, codes_v, book_v, res_v = cross_partial(codes_t, book_t, residuals, None)
            cut = [
                lax.dynamic_slice_in_dim(partial, (place ^ k) * size, size, 0) for k in range(dp)
            ]
            parts = [cut[0]] + [part.astype(bf16) for part in cut[1:]]
        else:
            *parts, codes_v, book_v, res_v = cross_partial(codes_t, book_t, residuals, dp)
        far_first = range(dp - 1, 0, -1)
        got = [swap(parts[k], "dp", dp, k) for k in far_first]
        *ready, res_t = onehot_call(codes_v, res_v, words, width)
        got, ready, res_t = lax.optimization_barrier((got, ready, res_t))
        piece = small_call(share_kernel, "share", (size, dim), bf16, parts[0], *got)
        pieces = {0: piece}
        for k in far_first:
            pieces[k] = swap(piece, "dp", dp, k)
        if thin:
            block = jnp.zeros((own, dim), bf16)
            for k in range(dp):
                block = lax.dynamic_update_slice_in_dim(block, pieces[k], (place ^ k) * size, 0)
            held = [block]
        else:
            half = max(dp // 2, 1)
            held = [
                jnp.concatenate([pieces[k] for k in range(at, min(at + half, dp))], axis=0)
                for at in range(0, dp, half)
            ]
        strides = [1 << b for b in reversed(range(code.bit_length() - 1))]
        far = strides[:-1]
        for even, odd in zip(far, far[::-1]):
            held = held + [swap(t, "code", code, even, odd) for t in held]
        for stride in strides[-1:]:
            held = held + [swap(t, "code", code, stride) for t in held]
        rotation_t = polar(held, own, 1 if thin else dp)
        scratch = [pltpu.VMEM((own, words), f32)]
        operands = (rotation_t, res_t, *ready)
        sums = small_call(sums_kernel, "sums", (own + subs, words), bf16, *operands, scratch=scratch)
        rotated = small_call(rotated_kernel, "rotated", (rows, own), f32, rotation_t, res_v)
        others = [swap(sums, "dp", dp, k) for k in range(1, dp)]
        book = small_call(book_kernel, "book", (own, words), f32, book_v, sums, *others)
        return rotated, jnp.transpose(book.reshape(subs, width, words), (0, 2, 1))

    return body


def solution(mesh):
    dp, code = mesh.shape["dp"], mesh.shape["code"]
    in_specs = (P("dp", None), P("dp", "code"), P("code", None, None))
    out_specs = (P("dp", "code"), P("code", None, None))
    return jax.shard_map(
        make_body(dp, code), mesh=mesh, in_specs=in_specs, out_specs=out_specs, check_vma=False
    )
```

```python
import functools

import jax
import jax.numpy as jnp
from jax import lax
from jax.experimental import pallas as pl
from jax.experimental.pallas import tpu as pltpu
from jax.sharding import PartitionSpec as P

quintic_a = 3.4445
quintic_b = -4.775
quintic_c = 2.0315
prior_weight = 8.0
epsilon = 1e-06
f32, bf16 = jnp.float32, jnp.bfloat16
MIB = 1024 * 1024
ROW_CHUNKS = 4
NT = (((1,), (1,)), ((), ()))


def dot(left, right):
    return jnp.dot(left, right, preferred_element_type=f32)


def dot_nt(left, right):
    return lax.dot_general(left, right, NT, preferred_element_type=f32)


def cross_kernel(codes_hbm, book_hbm, res_hbm, *refs, dp):
    outs = refs[: dp or 1]
    codes_ref, book_ref, res_ref, recon, cross, sems = refs[dp or 1 :]
    subs, rows = codes_ref.shape
    width = book_ref.shape[0] // subs
    words = book_ref.shape[1]
    lanes = 128
    chunks = sems.shape[0] - 2
    step = rows // chunks
    loads = [
        pltpu.make_async_copy(codes_hbm, codes_ref, sems.at[0]),
        pltpu.make_async_copy(book_hbm, book_ref, sems.at[1]),
    ]
    for i in range(chunks):
        part = pl.ds(i * step, step)
        loads.append(pltpu.make_async_copy(res_hbm.at[part], res_ref.at[part], sems.at[2 + i]))
    for load in loads:
        load.start()
    loads[0].wait()
    loads[1].wait()
    total = outs[0] if dp is None else cross
    for i in range(chunks):
        part = pl.ds(i * step, step)
        for m in range(subs):
            band = pl.ds(m * width, width)
            tables = [book_ref[band, pl.ds(t * lanes, lanes)] for t in range(words // lanes)]
            for c in range(i * step // lanes, (i + 1) * step // lanes):
                cols = pl.ds(c * lanes, lanes)
                code = jnp.broadcast_to(codes_ref[pl.ds(m, 1), cols], (width, lanes))
                low = jnp.bitwise_and(code, lanes - 1)
                value = jnp.take_along_axis(tables[0], low, axis=1, mode="promise_in_bounds")
                for t in range(1, len(tables)):
                    other = jnp.take_along_axis(tables[t], low, axis=1, mode="promise_in_bounds")
                    value = jnp.where(code >= t * lanes, other, value)
                recon[band, cols] = value
        loads[2 + i].wait()
        product = dot(recon[:, part].astype(bf16), res_ref[part, :])
        total[...] = product if i == 0 else total[...] + product
    if dp is None:
        return
    place = lax.axis_index("dp")
    size = outs[0].shape[0]
    for k, out in enumerate(outs):
        at = pl.multiple_of(jnp.bitwise_xor(place, k) * size, size)
        out[...] = cross[pl.ds(at, size), :].astype(out.dtype)


def cross_partial(codes_t, book_t, residuals, dp):
    rows, dim = residuals.shape
    cols = book_t.shape[0]
    if dp is None:
        shapes = (jax.ShapeDtypeStruct((cols, dim), f32),)
    else:
        shapes = tuple(
            jax.ShapeDtypeStruct((cols // dp, dim), bf16 if k else f32) for k in range(dp)
        )
    shapes += tuple(jax.ShapeDtypeStruct(x.shape, x.dtype) for x in (codes_t, book_t, residuals))
    return pl.pallas_call(
        functools.partial(cross_kernel, dp=dp),
        out_shape=shapes,
        in_specs=[pl.BlockSpec(memory_space=pltpu.HBM)] * 3,
        out_specs=(pl.BlockSpec(memory_space=pltpu.VMEM),) * len(shapes),
        scratch_shapes=[
            pltpu.VMEM((cols, rows), f32),
            pltpu.VMEM((cols, dim), f32),
            pltpu.SemaphoreType.DMA((2 + ROW_CHUNKS,)),
        ],
        compiler_params=pltpu.CompilerParams(vmem_limit_bytes=24 * MIB),
        name="cross_partial",
    )(*[pltpu.with_memory_space_constraint(x, pltpu.HBM) for x in (codes_t, book_t, residuals)])


def polar_kernel(*refs, blocks, pieces, chunk):
    block_refs = refs[:blocks]
    rot_b = refs[blocks]
    raw, gram, gram_b, poly_b, iterate, iterate_b, turned = refs[blocks + 1 :]
    dim = raw.shape[0]
    own = rot_b.shape[0]
    steps = dim // chunk
    at = 0
    for block in block_refs:
        raw[pl.ds(at, block.shape[0]), :] = block[...]
        at += block.shape[0]

    def band_of(i):
        return pl.ds(i * chunk, chunk)

    def lower(j):
        return pl.ds(j * chunk, dim - j * chunk), pl.ds(j * chunk, chunk)

    def mirror(target, j, value):
        rows, cols = lower(j)
        rounded = value.astype(bf16)
        target[rows, cols] = rounded
        if j < steps - 1:
            target[cols, pl.ds((j + 1) * chunk, dim - (j + 1) * chunk)] = rounded[chunk:, :].T

    def gram_of(source, transposed=None):
        r = lax.broadcasted_iota(jnp.int32, (chunk, chunk), 0)
        c = lax.broadcasted_iota(jnp.int32, (chunk, chunk), 1)
        trace = jnp.zeros((), f32)
        for j in range(steps):
            rows, cols = lower(j)
            if transposed is None:
                part = dot_nt(source[rows, :], source[cols, :])
            else:
                part = dot(source[rows, :], transposed[:, cols])
            gram[rows, cols] = part
            mirror(gram_b, j, part)
            trace = trace + jnp.sum(jnp.where(r == c, part[:chunk, :], 0.0))
        return trace

    def poly_of(wb, wc):
        for j in range(steps):
            rows, cols = lower(j)
            square = dot(gram_b[rows, :], gram_b[:, cols])
            mirror(poly_b, j, wb * gram[rows, cols] + wc * square)

    frob = gram_of(raw)
    scale2 = 1.0 / (frob + epsilon)
    scale = lax.rsqrt(frob + epsilon)
    poly_of(quintic_b * scale2, quintic_c * scale2 * scale2)

    for i in range(steps):
        cols = band_of(i)
        value = scale * (quintic_a * raw[:, cols].astype(f32) + dot(poly_b[...], raw[:, cols]))
        iterate[:, cols] = value
        rounded = value.astype(bf16)
        iterate_b[:, cols] = rounded
        turned[cols, :] = rounded.T

    gram_of(iterate_b, turned)
    poly_of(quintic_b, quintic_c)

    for i in range(steps):
        cols = band_of(i)
        value = quintic_a * iterate[:, cols] + dot(poly_b[...], iterate_b[:, cols])
        iterate[pl.ds(0, own), cols] = value[:own, :]
        rounded = value.astype(bf16)
        raw[:, cols] = rounded
        turned[cols, :] = rounded.T

    mine = pl.ds(0, own)
    g = dot(raw[mine, :], turned[...])
    image = dot(g.astype(bf16), raw[...])
    square = dot(image.astype(bf16), turned[...])
    last = quintic_a * iterate[mine, :] + dot(
        (quintic_b * g + quintic_c * square).astype(bf16), raw[...]
    )
    size = own // pieces
    for p in range(pieces):
        to = 0
        if pieces > 1:
            to = pl.multiple_of(jnp.bitwise_xor(lax.axis_index("dp"), p) * size, size)
        rot_b[pl.ds(to, size), :] = last[p * size : (p + 1) * size, :].astype(bf16)


LOWS = 64


def onehot_kernel(codes_ref, res_ref, onehot_ref, masks_ref, counts_ref, turned_ref):
    subs, rows_all = codes_ref.shape
    step = 256
    for i in range(rows_all // step):
        rows = pl.ds(i * step, step)
        turned_ref[:, rows] = res_ref[rows, :].T
    highs = counts_ref.shape[1] // LOWS
    wide = masks_ref.shape[0] // subs
    group = min(subs, 256 // LOWS)
    low_word = lax.broadcasted_iota(jnp.int32, (LOWS, rows_all), 0)
    high_word = lax.broadcasted_iota(jnp.int32, (8, rows_all), 0)
    row = lax.broadcasted_iota(jnp.int32, (wide, rows_all), 0)
    for first in range(0, subs, group):
        onehots, marks = [], []
        for m in range(first, first + group):
            code = codes_ref[pl.ds(m, 1), :]
            low, high = jnp.bitwise_and(code, LOWS - 1), jnp.right_shift(code, 6)
            onehots.append(jnp.where(low_word == low, 1.0, 0.0).astype(bf16))
            marks.append(jnp.where(high_word == high, 1.0, 0.0))
            mask = jnp.where(row // (wide // highs) == high, 1.0, 0.0).astype(bf16)
            masks_ref[pl.ds(m * wide, wide), :] = mask
        onehot = jnp.concatenate(onehots, axis=0).T
        onehot_ref[:, pl.ds(first * LOWS, group * LOWS)] = onehot
        part = dot(jnp.concatenate(marks, axis=0).astype(bf16), onehot)
        for s in range(group):
            for h in range(highs):
                counts_ref[pl.ds(first + s, 1), pl.ds(h * LOWS, LOWS)] = part[
                    s * 8 + h : s * 8 + h + 1, s * LOWS : (s + 1) * LOWS
                ]


def onehot_call(codes_t, residuals, words, width):
    subs, rows = codes_t.shape
    vmem = pl.BlockSpec(memory_space=pltpu.VMEM)
    return pl.pallas_call(
        onehot_kernel,
        out_shape=(
            jax.ShapeDtypeStruct((rows, subs * LOWS), bf16),
            jax.ShapeDtypeStruct((subs * width * (words // LOWS), rows), bf16),
            jax.ShapeDtypeStruct((subs, words), f32),
            jax.ShapeDtypeStruct(residuals.shape[::-1], bf16),
        ),
        in_specs=[vmem, vmem],
        out_specs=(vmem,) * 4,
        compiler_params=pltpu.CompilerParams(vmem_limit_bytes=24 * MIB),
        cost_estimate=pl.CostEstimate(
            flops=2 * 256 * subs * LOWS * rows, bytes_accessed=2 * subs * LOWS * rows, transcendentals=0
        ),
        name="onehot",
    )(codes_t, residuals)


def sums_kernel(rot_ref, res_ref, onehot_ref, masks_ref, counts_ref, sent_ref, sums_ref):
    subs, words = counts_ref.shape
    own = rot_ref.shape[0]
    width = own // subs
    highs = words // LOWS
    group = min(subs, 256 // LOWS)
    rot_t = dot(rot_ref[...], res_ref[...])
    for first in range(0, subs, group):
        values = []
        for m in range(first, first + group):
            band = rot_t[m * width : (m + 1) * width, :]
            values.append(jnp.concatenate([band] * highs, axis=0).astype(bf16))
        wide = group * highs * width
        tall = jnp.concatenate(values, axis=0) * masks_ref[pl.ds(first // group * wide, wide), :]
        part = dot(tall, onehot_ref[:, pl.ds(first * LOWS, group * LOWS)])
        for s in range(group):
            for h in range(highs):
                at = (s * highs + h) * width
                sums_ref[pl.ds((first + s) * width, width), pl.ds(h * LOWS, LOWS)] = part[
                    at : at + width, s * LOWS : (s + 1) * LOWS
                ]
    sent_ref[pl.ds(0, own), :] = sums_ref[...].astype(bf16)
    sent_ref[pl.ds(own, subs), :] = counts_ref[...].astype(bf16)


def rotated_kernel(rot_ref, res_ref, rotated_ref):
    rows_all = res_ref.shape[0]
    step = 512

    @pl.loop(0, rows_all // step)
    def _(i):
        rows = pl.ds(pl.multiple_of(i * step, step), step)
        rotated_ref[rows, :] = dot_nt(res_ref[rows, :], rot_ref[...])


def polar(block_list, own, pieces):
    dim = block_list[0].shape[1]
    vmem = pl.BlockSpec(memory_space=pltpu.VMEM)
    kernel = functools.partial(polar_kernel, blocks=len(block_list), pieces=pieces, chunk=256)
    return pl.pallas_call(
        kernel,
        out_shape=jax.ShapeDtypeStruct((own, dim), bf16),
        in_specs=[vmem] * len(block_list),
        out_specs=vmem,
        scratch_shapes=[
            pltpu.VMEM((dim, dim), bf16),
            pltpu.VMEM((dim, dim), f32),
            pltpu.VMEM((dim, dim), bf16),
            pltpu.VMEM((dim, dim), bf16),
            pltpu.VMEM((dim, dim), f32),
            pltpu.VMEM((dim, dim), bf16),
            pltpu.VMEM((dim, dim), bf16),
        ],
        compiler_params=pltpu.CompilerParams(vmem_limit_bytes=30 * MIB),
        name="polar",
    )(*block_list)


def share_kernel(*refs):
    total = refs[0][...].astype(f32)
    for part in refs[1:-1]:
        total = total + part[...].astype(f32)
    refs[-1][...] = total.astype(refs[-1].dtype)


def book_kernel(book_ref, *refs):
    sums, out_ref = refs[:-1], refs[-1]
    own = book_ref.shape[0]
    subs = sums[0].shape[0] - own
    width = own // subs
    total = sums[0][...].astype(f32)
    for part in sums[1:]:
        total = total + part[...].astype(f32)
    for m in range(subs):
        band = pl.ds(m * width, width)
        count = total[own + m : own + m + 1, :] + prior_weight
        part = total[m * width : (m + 1) * width, :]
        out_ref[band, :] = (part + prior_weight * book_ref[band, :]) / count


def small_call(kernel, name, shape, dtype, *operands, scratch=()):
    vmem = pl.BlockSpec(memory_space=pltpu.VMEM)
    return pl.pallas_call(
        kernel,
        out_shape=jax.ShapeDtypeStruct(shape, dtype),
        in_specs=[vmem] * len(operands),
        out_specs=vmem,
        scratch_shapes=scratch,
        compiler_params=pltpu.CompilerParams(vmem_limit_bytes=24 * MIB),
        name=name,
    )(*operands)


def swap(value, axis, size, mask, odd_mask=None):
    odd_mask = mask if odd_mask is None else odd_mask
    return lax.ppermute(value, axis, [(i, i ^ (odd_mask if i % 2 else mask)) for i in range(size)])


def make_body(dp, code):
    def body(residuals, codes, codebook):
        rows, dim = residuals.shape
        subs, words, width = codebook.shape
        own = subs * width
        codes_t = codes.T
        book_t = jnp.transpose(codebook, (0, 2, 1)).reshape(own, words)
        size = own // dp
        thin = size % 16 != 0
        if thin:
            place = lax.axis_index("dp")
            partial, codes_v, book_v, res_v = cross_partial(codes_t, book_t, residuals, None)
            cut = [
                lax.dynamic_slice_in_dim(partial, (place ^ k) * size, size, 0) for k in range(dp)
            ]
            parts = [cut[0]] + [part.astype(bf16) for part in cut[1:]]
        else:
            *parts, codes_v, book_v, res_v = cross_partial(codes_t, book_t, residuals, dp)
        far_first = range(dp - 1, 0, -1)
        got = [swap(parts[k], "dp", dp, k) for k in far_first]
        *ready, res_t = onehot_call(codes_v, res_v, words, width)
        got, ready, res_t = lax.optimization_barrier((got, ready, res_t))
        piece = small_call(share_kernel, "share", (size, dim), bf16, parts[0], *got)
        pieces = {0: piece}
        for k in far_first:
            pieces[k] = swap(piece, "dp", dp, k)
        if thin:
            block = jnp.zeros((own, dim), bf16)
            for k in range(dp):
                block = lax.dynamic_update_slice_in_dim(block, pieces[k], (place ^ k) * size, 0)
            held = [block]
        else:
            half = max(dp // 2, 1)
            held = [
                jnp.concatenate([pieces[k] for k in range(at, min(at + half, dp))], axis=0)
                for at in range(0, dp, half)
            ]
        strides = [1 << b for b in reversed(range(code.bit_length() - 1))]
        far = strides[:-1]
        for even, odd in zip(far, far[::-1]):
            held = held + [swap(t, "code", code, even, odd) for t in held]
        for stride in strides[-1:]:
            held = held + [swap(t, "code", code, stride) for t in held]
        rotation_t = polar(held, own, 1 if thin else dp)
        scratch = [pltpu.VMEM((own, words), f32)]
        operands = (rotation_t, res_t, *ready)
        sums = small_call(sums_kernel, "sums", (own + subs, words), bf16, *operands, scratch=scratch)
        rotated = small_call(rotated_kernel, "rotated", (rows, own), f32, rotation_t, res_v)
        totals = {0: sums}
        for k in sorted(range(1, dp), key=lambda k: (bin(k).count("1"), k)):
            totals[k] = swap(totals[k & (k - 1)], "dp", dp, k & -k)
        totals = [totals[k] for k in range(dp)]
        book = small_call(book_kernel, "book", (own, words), f32, book_v, *totals)
        return rotated, jnp.transpose(book.reshape(subs, width, words), (0, 2, 1))

    return body


def solution(mesh):
    dp, code = mesh.shape["dp"], mesh.shape["code"]
    in_specs = (P("dp", None), P("dp", "code"), P("code", None, None))
    out_specs = (P("dp", "code"), P("code", None, None))
    return jax.shard_map(
        make_body(dp, code), mesh=mesh, in_specs=in_specs, out_specs=out_specs, check_vma=False
    )
```

```python
import functools

import jax
import jax.numpy as jnp
from jax import lax
from jax.experimental import pallas as pl
from jax.experimental.pallas import tpu as pltpu
from jax.sharding import PartitionSpec as P

quintic_a = 3.4445
quintic_b = -4.775
quintic_c = 2.0315
prior_weight = 8.0
epsilon = 1e-06
f32, bf16 = jnp.float32, jnp.bfloat16
MIB = 1024 * 1024
ROW_CHUNKS = 4
NT = (((1,), (1,)), ((), ()))


def dot(left, right):
    return jnp.dot(left, right, preferred_element_type=f32)


def dot_nt(left, right):
    return lax.dot_general(left, right, NT, preferred_element_type=f32)


def cross_kernel(codes_hbm, book_hbm, res_hbm, *refs, dp):
    outs = refs[: dp or 1]
    codes_ref, book_ref, res_ref, recon, cross, sems = refs[dp or 1 :]
    subs, rows = codes_ref.shape
    width = book_ref.shape[0] // subs
    words = book_ref.shape[1]
    lanes = 128
    chunks = sems.shape[0] - 2
    step = rows // chunks
    loads = [
        pltpu.make_async_copy(codes_hbm, codes_ref, sems.at[0]),
        pltpu.make_async_copy(book_hbm, book_ref, sems.at[1]),
    ]
    for i in range(chunks):
        part = pl.ds(i * step, step)
        loads.append(pltpu.make_async_copy(res_hbm.at[part], res_ref.at[part], sems.at[2 + i]))
    for load in loads:
        load.start()
    loads[0].wait()
    loads[1].wait()
    total = outs[0] if dp is None else cross
    for i in range(chunks):
        part = pl.ds(i * step, step)
        for m in range(subs):
            band = pl.ds(m * width, width)
            tables = [book_ref[band, pl.ds(t * lanes, lanes)] for t in range(words // lanes)]
            for c in range(i * step // lanes, (i + 1) * step // lanes):
                cols = pl.ds(c * lanes, lanes)
                code = jnp.broadcast_to(codes_ref[pl.ds(m, 1), cols], (width, lanes))
                low = jnp.bitwise_and(code, lanes - 1)
                value = jnp.take_along_axis(tables[0], low, axis=1, mode="promise_in_bounds")
                for t in range(1, len(tables)):
                    other = jnp.take_along_axis(tables[t], low, axis=1, mode="promise_in_bounds")
                    value = jnp.where(code >= t * lanes, other, value)
                recon[band, cols] = value
        loads[2 + i].wait()
        product = dot(recon[:, part].astype(bf16), res_ref[part, :])
        total[...] = product if i == 0 else total[...] + product
    if dp is None:
        return
    place = lax.axis_index("dp")
    size = outs[0].shape[0]
    for k, out in enumerate(outs):
        at = pl.multiple_of(jnp.bitwise_xor(place, k) * size, size)
        out[...] = cross[pl.ds(at, size), :].astype(out.dtype)


def cross_partial(codes_t, book_t, residuals, dp):
    rows, dim = residuals.shape
    cols = book_t.shape[0]
    if dp is None:
        shapes = (jax.ShapeDtypeStruct((cols, dim), f32),)
    else:
        shapes = tuple(
            jax.ShapeDtypeStruct((cols // dp, dim), bf16 if k else f32) for k in range(dp)
        )
    shapes += tuple(jax.ShapeDtypeStruct(x.shape, x.dtype) for x in (codes_t, book_t, residuals))
    return pl.pallas_call(
        functools.partial(cross_kernel, dp=dp),
        out_shape=shapes,
        in_specs=[pl.BlockSpec(memory_space=pltpu.HBM)] * 3,
        out_specs=(pl.BlockSpec(memory_space=pltpu.VMEM),) * len(shapes),
        scratch_shapes=[
            pltpu.VMEM((cols, rows), f32),
            pltpu.VMEM((cols, dim), f32),
            pltpu.SemaphoreType.DMA((2 + ROW_CHUNKS,)),
        ],
        compiler_params=pltpu.CompilerParams(vmem_limit_bytes=24 * MIB),
        name="cross_partial",
    )(*[pltpu.with_memory_space_constraint(x, pltpu.HBM) for x in (codes_t, book_t, residuals)])


def early_kernel(*refs, chunk):
    *block_refs, raw, gram, gram_b = refs
    at = 0
    for block in block_refs:
        raw[pl.ds(at, block.shape[0]), :] = block[...]
        at += block.shape[0]
    for j in range(at // chunk):
        cols = pl.ds(j * chunk, chunk)
        rows = pl.ds(j * chunk, at - j * chunk)
        part = dot_nt(raw[rows, :], raw[cols, :])
        gram[rows, cols] = part
        rounded = part.astype(bf16)
        gram_b[rows, cols] = rounded
        if (j + 1) * chunk < at:
            gram_b[cols, pl.ds((j + 1) * chunk, at - (j + 1) * chunk)] = rounded[chunk:, :].T


def early_gram(blocks, chunk):
    rows, dim = sum(block.shape[0] for block in blocks), blocks[0].shape[1]
    vmem = pl.BlockSpec(memory_space=pltpu.VMEM)
    return pl.pallas_call(
        functools.partial(early_kernel, chunk=chunk),
        out_shape=(
            jax.ShapeDtypeStruct((rows, dim), bf16),
            jax.ShapeDtypeStruct((rows, rows), f32),
            jax.ShapeDtypeStruct((rows, rows), bf16),
        ),
        in_specs=[vmem] * len(blocks),
        out_specs=(vmem,) * 3,
        compiler_params=pltpu.CompilerParams(vmem_limit_bytes=16 * MIB),
        name="early_gram",
    )(*blocks)


def polar_kernel(early_raw, early, early_b, *refs, blocks, pieces, chunk):
    block_refs = refs[:blocks]
    rot_b = refs[blocks]
    raw, gram, gram_b, poly_b, iterate, iterate_b, turned = refs[blocks + 1 :]
    dim = raw.shape[0]
    own = rot_b.shape[0]
    steps = dim // chunk
    known = early_raw.shape[0]
    raw[pl.ds(0, known), :] = early_raw[...]
    at = known
    for block in block_refs:
        raw[pl.ds(at, block.shape[0]), :] = block[...]
        at += block.shape[0]

    def band_of(i):
        return pl.ds(i * chunk, chunk)

    def lower(j):
        return pl.ds(j * chunk, dim - j * chunk), pl.ds(j * chunk, chunk)

    def mirror(target, j, value):
        rows, cols = lower(j)
        rounded = value.astype(bf16)
        target[rows, cols] = rounded
        if j < steps - 1:
            target[cols, pl.ds((j + 1) * chunk, dim - (j + 1) * chunk)] = rounded[chunk:, :].T

    def first_gram():
        r = lax.broadcasted_iota(jnp.int32, (chunk, chunk), 0)
        c = lax.broadcasted_iota(jnp.int32, (chunk, chunk), 1)
        rest = pl.ds(known, dim - known)
        part = dot_nt(raw[...], raw[rest, :])
        rounded = part.astype(bf16)
        gram_b[pl.ds(0, known), pl.ds(0, known)] = early_b[...]
        gram_b[:, rest] = rounded
        gram_b[rest, pl.ds(0, known)] = rounded[:known, :].T
        gram[rest, rest] = part[known:, :]
        trace = jnp.sum(jnp.where(r == c, part[known:, :], 0.0))
        for j in range(known // chunk):
            rows, cols = pl.ds(j * chunk, known - j * chunk), band_of(j)
            gram[rows, cols] = early[rows, cols]
            gram[rest, cols] = part[j * chunk : (j + 1) * chunk, :].T
            trace = trace + jnp.sum(jnp.where(r == c, early[cols, cols], 0.0))
        return trace

    def gram_of(source, transposed):
        for j in range(steps):
            rows, cols = lower(j)
            part = dot(source[rows, :], transposed[:, cols])
            gram[rows, cols] = part
            mirror(gram_b, j, part)

    def poly_of(wb, wc):
        for j in range(steps):
            rows, cols = lower(j)
            square = dot(gram_b[rows, :], gram_b[:, cols])
            mirror(poly_b, j, wb * gram[rows, cols] + wc * square)

    frob = first_gram()
    scale2 = 1.0 / (frob + epsilon)
    scale = lax.rsqrt(frob + epsilon)
    poly_of(quintic_b * scale2, quintic_c * scale2 * scale2)

    for i in range(steps):
        cols = band_of(i)
        value = scale * (quintic_a * raw[:, cols].astype(f32) + dot(poly_b[...], raw[:, cols]))
        iterate[:, cols] = value
        rounded = value.astype(bf16)
        iterate_b[:, cols] = rounded
        turned[cols, :] = rounded.T

    gram_of(iterate_b, turned)
    poly_of(quintic_b, quintic_c)

    for i in range(steps):
        cols = band_of(i)
        value = quintic_a * iterate[:, cols] + dot(poly_b[...], iterate_b[:, cols])
        iterate[pl.ds(0, own), cols] = value[:own, :]
        rounded = value.astype(bf16)
        raw[:, cols] = rounded
        turned[cols, :] = rounded.T

    mine = pl.ds(0, own)
    g = dot(raw[mine, :], turned[...])
    image = dot(g.astype(bf16), raw[...])
    square = dot(image.astype(bf16), turned[...])
    last = quintic_a * iterate[mine, :] + dot(
        (quintic_b * g + quintic_c * square).astype(bf16), raw[...]
    )
    size = own // pieces
    for p in range(pieces):
        to = 0
        if pieces > 1:
            to = pl.multiple_of(jnp.bitwise_xor(lax.axis_index("dp"), p) * size, size)
        rot_b[pl.ds(to, size), :] = last[p * size : (p + 1) * size, :].astype(bf16)


LOWS = 64


def onehot_kernel(codes_ref, res_ref, onehot_ref, masks_ref, counts_ref, turned_ref):
    subs, rows_all = codes_ref.shape
    step = 256
    for i in range(rows_all // step):
        rows = pl.ds(i * step, step)
        turned_ref[:, rows] = res_ref[rows, :].T
    highs = counts_ref.shape[1] // LOWS
    wide = masks_ref.shape[0] // subs
    group = min(subs, 256 // LOWS)
    low_word = lax.broadcasted_iota(jnp.int32, (LOWS, rows_all), 0)
    high_word = lax.broadcasted_iota(jnp.int32, (8, rows_all), 0)
    row = lax.broadcasted_iota(jnp.int32, (wide, rows_all), 0)
    for first in range(0, subs, group):
        onehots, marks = [], []
        for m in range(first, first + group):
            code = codes_ref[pl.ds(m, 1), :]
            low, high = jnp.bitwise_and(code, LOWS - 1), jnp.right_shift(code, 6)
            onehots.append(jnp.where(low_word == low, 1.0, 0.0).astype(bf16))
            marks.append(jnp.where(high_word == high, 1.0, 0.0))
            mask = jnp.where(row // (wide // highs) == high, 1.0, 0.0).astype(bf16)
            masks_ref[pl.ds(m * wide, wide), :] = mask
        onehot = jnp.concatenate(onehots, axis=0).T
        onehot_ref[:, pl.ds(first * LOWS, group * LOWS)] = onehot
        part = dot(jnp.concatenate(marks, axis=0).astype(bf16), onehot)
        for s in range(group):
            for h in range(highs):
                counts_ref[pl.ds(first + s, 1), pl.ds(h * LOWS, LOWS)] = part[
                    s * 8 + h : s * 8 + h + 1, s * LOWS : (s + 1) * LOWS
                ]


def onehot_call(codes_t, residuals, words, width):
    subs, rows = codes_t.shape
    vmem = pl.BlockSpec(memory_space=pltpu.VMEM)
    return pl.pallas_call(
        onehot_kernel,
        out_shape=(
            jax.ShapeDtypeStruct((rows, subs * LOWS), bf16),
            jax.ShapeDtypeStruct((subs * width * (words // LOWS), rows), bf16),
            jax.ShapeDtypeStruct((subs, words), f32),
            jax.ShapeDtypeStruct(residuals.shape[::-1], bf16),
        ),
        in_specs=[vmem, vmem],
        out_specs=(vmem,) * 4,
        compiler_params=pltpu.CompilerParams(vmem_limit_bytes=24 * MIB),
        cost_estimate=pl.CostEstimate(
            flops=2 * 256 * subs * LOWS * rows, bytes_accessed=2 * subs * LOWS * rows, transcendentals=0
        ),
        name="onehot",
    )(codes_t, residuals)


def sums_kernel(rot_ref, res_ref, onehot_ref, masks_ref, counts_ref, sent_ref, sums_ref):
    subs, words = counts_ref.shape
    own = rot_ref.shape[0]
    width = own // subs
    highs = words // LOWS
    group = min(subs, 256 // LOWS)
    rot_t = dot(rot_ref[...], res_ref[...])
    for first in range(0, subs, group):
        values = []
        for m in range(first, first + group):
            band = rot_t[m * width : (m + 1) * width, :]
            values.append(jnp.concatenate([band] * highs, axis=0).astype(bf16))
        wide = group * highs * width
        tall = jnp.concatenate(values, axis=0) * masks_ref[pl.ds(first // group * wide, wide), :]
        part = dot(tall, onehot_ref[:, pl.ds(first * LOWS, group * LOWS)])
        for s in range(group):
            for h in range(highs):
                at = (s * highs + h) * width
                sums_ref[pl.ds((first + s) * width, width), pl.ds(h * LOWS, LOWS)] = part[
                    at : at + width, s * LOWS : (s + 1) * LOWS
                ]
    sent_ref[pl.ds(0, own), :] = sums_ref[...].astype(bf16)
    sent_ref[pl.ds(own, subs), :] = counts_ref[...].astype(bf16)


def rotated_kernel(rot_ref, res_ref, rotated_ref):
    rows_all = res_ref.shape[0]
    step = 512

    @pl.loop(0, rows_all // step)
    def _(i):
        rows = pl.ds(pl.multiple_of(i * step, step), step)
        rotated_ref[rows, :] = dot_nt(res_ref[rows, :], rot_ref[...])


def polar(early, block_list, own, pieces, chunk):
    dim = block_list[0].shape[1]
    vmem = pl.BlockSpec(memory_space=pltpu.VMEM)
    kernel = functools.partial(polar_kernel, blocks=len(block_list), pieces=pieces, chunk=chunk)
    return pl.pallas_call(
        kernel,
        out_shape=jax.ShapeDtypeStruct((own, dim), bf16),
        in_specs=[vmem] * (3 + len(block_list)),
        out_specs=vmem,
        scratch_shapes=[
            pltpu.VMEM((dim, dim), bf16),
            pltpu.VMEM((dim, dim), f32),
            pltpu.VMEM((dim, dim), bf16),
            pltpu.VMEM((dim, dim), bf16),
            pltpu.VMEM((dim, dim), f32),
            pltpu.VMEM((dim, dim), bf16),
            pltpu.VMEM((dim, dim), bf16),
        ],
        compiler_params=pltpu.CompilerParams(vmem_limit_bytes=30 * MIB),
        name="polar",
    )(*early, *block_list)


def share_kernel(*refs):
    total = refs[0][...].astype(f32)
    for part in refs[1:-1]:
        total = total + part[...].astype(f32)
    refs[-1][...] = total.astype(refs[-1].dtype)


def book_kernel(book_ref, *refs):
    sums, out_ref = refs[:-1], refs[-1]
    own = book_ref.shape[0]
    subs = sums[0].shape[0] - own
    width = own // subs
    total = sums[0][...].astype(f32)
    for part in sums[1:]:
        total = total + part[...].astype(f32)
    for m in range(subs):
        band = pl.ds(m * width, width)
        count = total[own + m : own + m + 1, :] + prior_weight
        part = total[m * width : (m + 1) * width, :]
        out_ref[band, :] = (part + prior_weight * book_ref[band, :]) / count


def small_call(kernel, name, shape, dtype, *operands, scratch=()):
    vmem = pl.BlockSpec(memory_space=pltpu.VMEM)
    return pl.pallas_call(
        kernel,
        out_shape=jax.ShapeDtypeStruct(shape, dtype),
        in_specs=[vmem] * len(operands),
        out_specs=vmem,
        scratch_shapes=scratch,
        compiler_params=pltpu.CompilerParams(vmem_limit_bytes=24 * MIB),
        name=name,
    )(*operands)


def swap(value, axis, size, mask, odd_mask=None):
    odd_mask = mask if odd_mask is None else odd_mask
    return lax.ppermute(value, axis, [(i, i ^ (odd_mask if i % 2 else mask)) for i in range(size)])


def make_body(dp, code):
    def body(residuals, codes, codebook):
        rows, dim = residuals.shape
        subs, words, width = codebook.shape
        own = subs * width
        codes_t = codes.T
        book_t = jnp.transpose(codebook, (0, 2, 1)).reshape(own, words)
        size = own // dp
        thin = size % 16 != 0
        if thin:
            place = lax.axis_index("dp")
            partial, codes_v, book_v, res_v = cross_partial(codes_t, book_t, residuals, None)
            cut = [
                lax.dynamic_slice_in_dim(partial, (place ^ k) * size, size, 0) for k in range(dp)
            ]
            parts = [cut[0]] + [part.astype(bf16) for part in cut[1:]]
        else:
            *parts, codes_v, book_v, res_v = cross_partial(codes_t, book_t, residuals, dp)
        far_first = range(dp - 1, 0, -1)
        got = [swap(parts[k], "dp", dp, k) for k in far_first]
        *ready, res_t = onehot_call(codes_v, res_v, words, width)
        got, ready, res_t = lax.optimization_barrier((got, ready, res_t))
        piece = small_call(share_kernel, "share", (size, dim), bf16, parts[0], *got)
        pieces = {0: piece}
        for k in far_first:
            pieces[k] = swap(piece, "dp", dp, k)
        if thin:
            block = jnp.zeros((own, dim), bf16)
            for k in range(dp):
                block = lax.dynamic_update_slice_in_dim(block, pieces[k], (place ^ k) * size, 0)
            held = [block]
        else:
            half = max(dp // 2, 1)
            held = [
                jnp.concatenate([pieces[k] for k in range(at, min(at + half, dp))], axis=0)
                for at in range(0, dp, half)
            ]
        strides = [1 << b for b in reversed(range(code.bit_length() - 1))]
        far = strides[:-1]
        for even, odd in zip(far, far[::-1]):
            held = held + [swap(t, "code", code, even, odd) for t in held]
        chunk = 256
        near, last = strides[-1:], held.pop()
        held += [swap(t, "code", code, stride) for stride in near for t in held]
        count = (dim - chunk) // last.shape[0]
        early = early_gram(held[:count], chunk)
        last, early = lax.optimization_barrier((last, early))
        held = held[count:] + [last] + [swap(last, "code", code, stride) for stride in near]
        rotation_t = polar(early, held, own, 1 if thin else dp, chunk)
        scratch = [pltpu.VMEM((own, words), f32)]
        operands = (rotation_t, res_t, *ready)
        sums = small_call(sums_kernel, "sums", (own + subs, words), bf16, *operands, scratch=scratch)
        rotated = small_call(rotated_kernel, "rotated", (rows, own), f32, rotation_t, res_v)
        others = [swap(sums, "dp", dp, k) for k in far_first]
        book = small_call(book_kernel, "book", (own, words), f32, book_v, sums, *others)
        return rotated, jnp.transpose(book.reshape(subs, width, words), (0, 2, 1))

    return body


def solution(mesh):
    dp, code = mesh.shape["dp"], mesh.shape["code"]
    in_specs = (P("dp", None), P("dp", "code"), P("code", None, None))
    out_specs = (P("dp", "code"), P("code", None, None))
    return jax.shard_map(
        make_body(dp, code), mesh=mesh, in_specs=in_specs, out_specs=out_specs, check_vma=False
    )
```

```python
import functools

import jax
import jax.numpy as jnp
from jax import lax
from jax.experimental import pallas as pl
from jax.experimental.pallas import tpu as pltpu
from jax.sharding import PartitionSpec as P

quintic_a = 3.4445
quintic_b = -4.775
quintic_c = 2.0315
prior_weight = 8.0
epsilon = 1e-06
f32, bf16 = jnp.float32, jnp.bfloat16
MIB = 1024 * 1024
ROW_CHUNKS = 4
NT = (((1,), (1,)), ((), ()))


def dot(left, right):
    return jnp.dot(left, right, preferred_element_type=f32)


def dot_nt(left, right):
    return lax.dot_general(left, right, NT, preferred_element_type=f32)


def cross_kernel(codes_hbm, book_hbm, res_hbm, *refs, dp):
    outs = refs[: dp or 1]
    codes_ref, book_ref, res_ref, recon, cross, sems = refs[dp or 1 :]
    subs, rows = codes_ref.shape
    width = book_ref.shape[0] // subs
    words = book_ref.shape[1]
    lanes = 128
    chunks = sems.shape[0] - 2
    step = rows // chunks
    loads = [
        pltpu.make_async_copy(codes_hbm, codes_ref, sems.at[0]),
        pltpu.make_async_copy(book_hbm, book_ref, sems.at[1]),
    ]
    for i in range(chunks):
        part = pl.ds(i * step, step)
        loads.append(pltpu.make_async_copy(res_hbm.at[part], res_ref.at[part], sems.at[2 + i]))
    for load in loads:
        load.start()
    loads[0].wait()
    loads[1].wait()
    total = outs[0] if dp is None else cross
    for i in range(chunks):
        part = pl.ds(i * step, step)
        for m in range(subs):
            band = pl.ds(m * width, width)
            tables = [book_ref[band, pl.ds(t * lanes, lanes)] for t in range(words // lanes)]
            for c in range(i * step // lanes, (i + 1) * step // lanes):
                cols = pl.ds(c * lanes, lanes)
                code = jnp.broadcast_to(codes_ref[pl.ds(m, 1), cols], (width, lanes))
                low = jnp.bitwise_and(code, lanes - 1)
                value = jnp.take_along_axis(tables[0], low, axis=1, mode="promise_in_bounds")
                for t in range(1, len(tables)):
                    other = jnp.take_along_axis(tables[t], low, axis=1, mode="promise_in_bounds")
                    value = jnp.where(code >= t * lanes, other, value)
                recon[band, cols] = value
        loads[2 + i].wait()
        product = dot(recon[:, part].astype(bf16), res_ref[part, :])
        total[...] = product if i == 0 else total[...] + product
    if dp is None:
        return
    place = lax.axis_index("dp")
    size = outs[0].shape[0]
    for k, out in enumerate(outs):
        at = pl.multiple_of(jnp.bitwise_xor(place, k) * size, size)
        out[...] = cross[pl.ds(at, size), :].astype(out.dtype)


def cross_partial(codes_t, book_t, residuals, dp):
    rows, dim = residuals.shape
    cols = book_t.shape[0]
    if dp is None:
        shapes = (jax.ShapeDtypeStruct((cols, dim), f32),)
    else:
        shapes = tuple(
            jax.ShapeDtypeStruct((cols // dp, dim), bf16 if k else f32) for k in range(dp)
        )
    shapes += tuple(jax.ShapeDtypeStruct(x.shape, x.dtype) for x in (codes_t, book_t, residuals))
    return pl.pallas_call(
        functools.partial(cross_kernel, dp=dp),
        out_shape=shapes,
        in_specs=[pl.BlockSpec(memory_space=pltpu.HBM)] * 3,
        out_specs=(pl.BlockSpec(memory_space=pltpu.VMEM),) * len(shapes),
        scratch_shapes=[
            pltpu.VMEM((cols, rows), f32),
            pltpu.VMEM((cols, dim), f32),
            pltpu.SemaphoreType.DMA((2 + ROW_CHUNKS,)),
        ],
        compiler_params=pltpu.CompilerParams(vmem_limit_bytes=24 * MIB),
        name="cross_partial",
    )(*[pltpu.with_memory_space_constraint(x, pltpu.HBM) for x in (codes_t, book_t, residuals)])


def polar_kernel(*refs, blocks, pieces, chunk):
    block_refs = refs[:blocks]
    rot_b = refs[blocks]
    raw, gram, gram_b, poly_b, iterate, iterate_b, turned = refs[blocks + 1 :]
    dim = raw.shape[0]
    own = rot_b.shape[0]
    steps = dim // chunk
    at = 0
    for block in block_refs:
        raw[pl.ds(at, block.shape[0]), :] = block[...]
        at += block.shape[0]

    def band_of(i):
        return pl.ds(i * chunk, chunk)

    def lower(j):
        return pl.ds(j * chunk, dim - j * chunk), pl.ds(j * chunk, chunk)

    def mirror(target, j, value):
        rows, cols = lower(j)
        rounded = value.astype(bf16)
        target[rows, cols] = rounded
        if j < steps - 1:
            target[cols, pl.ds((j + 1) * chunk, dim - (j + 1) * chunk)] = rounded[chunk:, :].T

    def gram_of(source, transposed=None):
        r = lax.broadcasted_iota(jnp.int32, (chunk, chunk), 0)
        c = lax.broadcasted_iota(jnp.int32, (chunk, chunk), 1)
        trace = jnp.zeros((), f32)
        for j in range(steps):
            rows, cols = lower(j)
            if transposed is None:
                part = dot_nt(source[rows, :], source[cols, :])
            else:
                part = dot(source[rows, :], transposed[:, cols])
            gram[rows, cols] = part
            mirror(gram_b, j, part)
            trace = trace + jnp.sum(jnp.where(r == c, part[:chunk, :], 0.0))
        return trace

    def poly_of(wb, wc):
        for j in range(steps):
            rows, cols = lower(j)
            square = dot(gram_b[rows, :], gram_b[:, cols])
            mirror(poly_b, j, wb * gram[rows, cols] + wc * square)

    frob = gram_of(raw)
    scale2 = 1.0 / (frob + epsilon)
    scale = lax.rsqrt(frob + epsilon)
    poly_of(quintic_b * scale2, quintic_c * scale2 * scale2)

    for i in range(steps):
        cols = band_of(i)
        value = scale * (quintic_a * raw[:, cols].astype(f32) + dot(poly_b[...], raw[:, cols]))
        iterate[:, cols] = value
        rounded = value.astype(bf16)
        iterate_b[:, cols] = rounded
        turned[cols, :] = rounded.T

    gram_of(iterate_b, turned)
    poly_of(quintic_b, quintic_c)

    for i in range(steps):
        cols = band_of(i)
        value = quintic_a * iterate[:, cols] + dot(poly_b[...], iterate_b[:, cols])
        iterate[pl.ds(0, own), cols] = value[:own, :]
        rounded = value.astype(bf16)
        raw[:, cols] = rounded
        turned[cols, :] = rounded.T

    mine = pl.ds(0, own)
    g = dot(raw[mine, :], turned[...])
    image = dot(g.astype(bf16), raw[...])
    square = dot(image.astype(bf16), turned[...])
    last = quintic_a * iterate[mine, :] + dot(
        (quintic_b * g + quintic_c * square).astype(bf16), raw[...]
    )
    size = own // pieces
    for p in range(pieces):
        to = 0
        if pieces > 1:
            to = pl.multiple_of(jnp.bitwise_xor(lax.axis_index("dp"), p) * size, size)
        rot_b[pl.ds(to, size), :] = last[p * size : (p + 1) * size, :].astype(bf16)


LOWS = 64


def onehot_kernel(codes_ref, res_ref, onehot_ref, masks_ref, counts_ref, turned_ref):
    subs, rows_all = codes_ref.shape
    step = 256
    for i in range(rows_all // step):
        rows = pl.ds(i * step, step)
        turned_ref[:, rows] = res_ref[rows, :].T
    highs = counts_ref.shape[1] // LOWS
    wide = masks_ref.shape[0] // subs
    group = min(subs, 256 // LOWS)
    low_word = lax.broadcasted_iota(jnp.int32, (LOWS, rows_all), 0)
    high_word = lax.broadcasted_iota(jnp.int32, (8, rows_all), 0)
    row = lax.broadcasted_iota(jnp.int32, (wide, rows_all), 0)
    for first in range(0, subs, group):
        onehots, marks = [], []
        for m in range(first, first + group):
            code = codes_ref[pl.ds(m, 1), :]
            low, high = jnp.bitwise_and(code, LOWS - 1), jnp.right_shift(code, 6)
            onehots.append(jnp.where(low_word == low, 1.0, 0.0).astype(bf16))
            marks.append(jnp.where(high_word == high, 1.0, 0.0))
            mask = jnp.where(row // (wide // highs) == high, 1.0, 0.0).astype(bf16)
            masks_ref[pl.ds(m * wide, wide), :] = mask
        onehot = jnp.concatenate(onehots, axis=0).T
        onehot_ref[:, pl.ds(first * LOWS, group * LOWS)] = onehot
        part = dot(jnp.concatenate(marks, axis=0).astype(bf16), onehot)
        for s in range(group):
            for h in range(highs):
                counts_ref[pl.ds(first + s, 1), pl.ds(h * LOWS, LOWS)] = part[
                    s * 8 + h : s * 8 + h + 1, s * LOWS : (s + 1) * LOWS
                ]


def onehot_call(codes_t, residuals, words, width):
    subs, rows = codes_t.shape
    vmem = pl.BlockSpec(memory_space=pltpu.VMEM)
    return pl.pallas_call(
        onehot_kernel,
        out_shape=(
            jax.ShapeDtypeStruct((rows, subs * LOWS), bf16),
            jax.ShapeDtypeStruct((subs * width * (words // LOWS), rows), bf16),
            jax.ShapeDtypeStruct((subs, words), f32),
            jax.ShapeDtypeStruct(residuals.shape[::-1], bf16),
        ),
        in_specs=[vmem, vmem],
        out_specs=(vmem,) * 4,
        compiler_params=pltpu.CompilerParams(vmem_limit_bytes=24 * MIB),
        cost_estimate=pl.CostEstimate(
            flops=2 * 256 * subs * LOWS * rows, bytes_accessed=2 * subs * LOWS * rows, transcendentals=0
        ),
        name="onehot",
    )(codes_t, residuals)


def sums_kernel(rot_ref, res_ref, onehot_ref, masks_ref, counts_ref, sent_ref, sums_ref):
    subs, words = counts_ref.shape
    own = rot_ref.shape[0]
    width = own // subs
    highs = words // LOWS
    group = min(subs, 256 // LOWS)
    rot_t = dot(rot_ref[...], res_ref[...])
    for first in range(0, subs, group):
        values = []
        for m in range(first, first + group):
            band = rot_t[m * width : (m + 1) * width, :]
            values.append(jnp.concatenate([band] * highs, axis=0).astype(bf16))
        wide = group * highs * width
        tall = jnp.concatenate(values, axis=0) * masks_ref[pl.ds(first // group * wide, wide), :]
        part = dot(tall, onehot_ref[:, pl.ds(first * LOWS, group * LOWS)])
        for s in range(group):
            for h in range(highs):
                at = (s * highs + h) * width
                sums_ref[pl.ds((first + s) * width, width), pl.ds(h * LOWS, LOWS)] = part[
                    at : at + width, s * LOWS : (s + 1) * LOWS
                ]
    sent_ref[pl.ds(0, own), :] = sums_ref[...].astype(bf16)
    sent_ref[pl.ds(own, subs), :] = counts_ref[...].astype(bf16)


def rotated_kernel(rot_ref, res_ref, rotated_ref):
    rows_all = res_ref.shape[0]
    step = 512

    @pl.loop(0, rows_all // step)
    def _(i):
        rows = pl.ds(pl.multiple_of(i * step, step), step)
        rotated_ref[rows, :] = dot_nt(res_ref[rows, :], rot_ref[...])


def polar(block_list, own, pieces):
    dim = block_list[0].shape[1]
    vmem = pl.BlockSpec(memory_space=pltpu.VMEM)
    kernel = functools.partial(polar_kernel, blocks=len(block_list), pieces=pieces, chunk=256)
    return pl.pallas_call(
        kernel,
        out_shape=jax.ShapeDtypeStruct((own, dim), bf16),
        in_specs=[vmem] * len(block_list),
        out_specs=vmem,
        scratch_shapes=[
            pltpu.VMEM((dim, dim), bf16),
            pltpu.VMEM((dim, dim), f32),
            pltpu.VMEM((dim, dim), bf16),
            pltpu.VMEM((dim, dim), bf16),
            pltpu.VMEM((dim, dim), f32),
            pltpu.VMEM((dim, dim), bf16),
            pltpu.VMEM((dim, dim), bf16),
        ],
        compiler_params=pltpu.CompilerParams(vmem_limit_bytes=30 * MIB),
        name="polar",
    )(*block_list)


def share_kernel(*refs):
    total = refs[0][...].astype(f32)
    for part in refs[1:-1]:
        total = total + part[...].astype(f32)
    refs[-1][...] = total.astype(refs[-1].dtype)


def book_kernel(book_ref, *refs):
    sums, out_ref = refs[:-1], refs[-1]
    own = book_ref.shape[0]
    subs = sums[0].shape[0] - own
    width = own // subs
    total = sums[0][...].astype(f32)
    for part in sums[1:]:
        total = total + part[...].astype(f32)
    for m in range(subs):
        band = pl.ds(m * width, width)
        count = total[own + m : own + m + 1, :] + prior_weight
        part = total[m * width : (m + 1) * width, :]
        out_ref[band, :] = (part + prior_weight * book_ref[band, :]) / count


def small_call(kernel, name, shape, dtype, *operands, scratch=()):
    vmem = pl.BlockSpec(memory_space=pltpu.VMEM)
    return pl.pallas_call(
        kernel,
        out_shape=jax.ShapeDtypeStruct(shape, dtype),
        in_specs=[vmem] * len(operands),
        out_specs=vmem,
        scratch_shapes=scratch,
        compiler_params=pltpu.CompilerParams(vmem_limit_bytes=24 * MIB),
        name=name,
    )(*operands)


def swap(value, axis, size, mask, odd_mask=None):
    odd_mask = mask if odd_mask is None else odd_mask
    return lax.ppermute(value, axis, [(i, i ^ (odd_mask if i % 2 else mask)) for i in range(size)])


def make_body(dp, code):
    def body(residuals, codes, codebook):
        rows, dim = residuals.shape
        subs, words, width = codebook.shape
        own = subs * width
        codes_t = codes.T
        book_t = jnp.transpose(codebook, (0, 2, 1)).reshape(own, words)
        size = own // dp
        thin = size % 16 != 0
        if thin:
            place = lax.axis_index("dp")
            partial, codes_v, book_v, res_v = cross_partial(codes_t, book_t, residuals, None)
            cut = [
                lax.dynamic_slice_in_dim(partial, (place ^ k) * size, size, 0) for k in range(dp)
            ]
            parts = [cut[0]] + [part.astype(bf16) for part in cut[1:]]
        else:
            *parts, codes_v, book_v, res_v = cross_partial(codes_t, book_t, residuals, dp)
        far_first = range(dp - 1, 0, -1)
        got = [swap(parts[k], "dp", dp, k) for k in far_first]
        *ready, res_t = onehot_call(codes_v, res_v, words, width)
        got, ready, res_t = lax.optimization_barrier((got, ready, res_t))
        piece = small_call(share_kernel, "share", (size, dim), bf16, parts[0], *got)
        pieces = {0: piece}
        for k in far_first:
            pieces[k] = swap(piece, "dp", dp, k)
        if thin:
            block = jnp.zeros((own, dim), bf16)
            for k in range(dp):
                block = lax.dynamic_update_slice_in_dim(block, pieces[k], (place ^ k) * size, 0)
            held = [block]
        else:
            half = max(dp // 2, 1)
            held = [
                jnp.concatenate([pieces[k] for k in range(at, min(at + half, dp))], axis=0)
                for at in range(0, dp, half)
            ]
        strides = [1 << b for b in reversed(range(code.bit_length() - 1))]
        far = strides[:-1]
        for even, odd in zip(far, far[::-1]):
            held = held + [swap(t, "code", code, even, odd) for t in held]
        near = strides[-1:]
        crossed = [swap(t, "code", code, stride) for stride in near for t in held[:-1]]
        last, early = lax.optimization_barrier((held[-1], crossed[: len(held) // 2 + 1]))
        held = held[:-1] + [last] + early + crossed[len(held) // 2 + 1 :]
        held += [swap(last, "code", code, stride) for stride in near]
        rotation_t = polar(held, own, 1 if thin else dp)
        scratch = [pltpu.VMEM((own, words), f32)]
        operands = (rotation_t, res_t, *ready)
        sums = small_call(sums_kernel, "sums", (own + subs, words), bf16, *operands, scratch=scratch)
        rotated = small_call(rotated_kernel, "rotated", (rows, own), f32, rotation_t, res_v)
        others = [swap(sums, "dp", dp, k) for k in range(1, dp)]
        book = small_call(book_kernel, "book", (own, words), f32, book_v, sums, *others)
        return rotated, jnp.transpose(book.reshape(subs, width, words), (0, 2, 1))

    return body


def solution(mesh):
    dp, code = mesh.shape["dp"], mesh.shape["code"]
    in_specs = (P("dp", None), P("dp", "code"), P("code", None, None))
    out_specs = (P("dp", "code"), P("code", None, None))
    return jax.shard_map(
        make_body(dp, code), mesh=mesh, in_specs=in_specs, out_specs=out_specs, check_vma=False
    )
```

```python
import functools

import jax
import jax.numpy as jnp
from jax import lax
from jax.experimental import pallas as pl
from jax.experimental.pallas import tpu as pltpu
from jax.sharding import PartitionSpec as P

quintic_a = 3.4445
quintic_b = -4.775
quintic_c = 2.0315
prior_weight = 8.0
epsilon = 1e-06
f32, bf16 = jnp.float32, jnp.bfloat16
MIB = 1024 * 1024
ROW_CHUNKS = 8
NT = (((1,), (1,)), ((), ()))


def dot(left, right):
    return jnp.dot(left, right, preferred_element_type=f32)


def dot_nt(left, right):
    return lax.dot_general(left, right, NT, preferred_element_type=f32)


def cross_kernel(codes_hbm, book_hbm, res_hbm, *refs, dp):
    outs = refs[: dp or 1]
    codes_ref, book_ref, res_ref, recon, cross, sems = refs[dp or 1 :]
    subs, rows = codes_ref.shape
    width = book_ref.shape[0] // subs
    words = book_ref.shape[1]
    lanes = 128
    chunks = sems.shape[0] - 2
    step = rows // chunks
    loads = [
        pltpu.make_async_copy(codes_hbm, codes_ref, sems.at[0]),
        pltpu.make_async_copy(book_hbm, book_ref, sems.at[1]),
    ]
    for i in range(chunks):
        part = pl.ds(i * step, step)
        loads.append(pltpu.make_async_copy(res_hbm.at[part], res_ref.at[part], sems.at[2 + i]))
    for load in loads:
        load.start()
    loads[0].wait()
    loads[1].wait()
    total = outs[0] if dp is None else cross
    for i in range(chunks):
        part = pl.ds(i * step, step)
        for m in range(subs):
            band = pl.ds(m * width, width)
            tables = [book_ref[band, pl.ds(t * lanes, lanes)] for t in range(words // lanes)]
            for c in range(i * step // lanes, (i + 1) * step // lanes):
                cols = pl.ds(c * lanes, lanes)
                code = jnp.broadcast_to(codes_ref[pl.ds(m, 1), cols], (width, lanes))
                low = jnp.bitwise_and(code, lanes - 1)
                value = jnp.take_along_axis(tables[0], low, axis=1, mode="promise_in_bounds")
                for t in range(1, len(tables)):
                    other = jnp.take_along_axis(tables[t], low, axis=1, mode="promise_in_bounds")
                    value = jnp.where(code >= t * lanes, other, value)
                recon[band, cols] = value
        loads[2 + i].wait()
        product = dot(recon[:, part].astype(bf16), res_ref[part, :])
        total[...] = product if i == 0 else total[...] + product
    if dp is None:
        return
    place = lax.axis_index("dp")
    size = outs[0].shape[0]
    for k, out in enumerate(outs):
        at = pl.multiple_of(jnp.bitwise_xor(place, k) * size, size)
        out[...] = cross[pl.ds(at, size), :].astype(out.dtype)


def cross_partial(codes_t, book_t, residuals, dp):
    rows, dim = residuals.shape
    cols = book_t.shape[0]
    if dp is None:
        shapes = (jax.ShapeDtypeStruct((cols, dim), f32),)
    else:
        shapes = tuple(
            jax.ShapeDtypeStruct((cols // dp, dim), bf16 if k else f32) for k in range(dp)
        )
    shapes += tuple(jax.ShapeDtypeStruct(x.shape, x.dtype) for x in (codes_t, book_t, residuals))
    return pl.pallas_call(
        functools.partial(cross_kernel, dp=dp),
        out_shape=shapes,
        in_specs=[pl.BlockSpec(memory_space=pltpu.HBM)] * 3,
        out_specs=(pl.BlockSpec(memory_space=pltpu.VMEM),) * len(shapes),
        scratch_shapes=[
            pltpu.VMEM((cols, rows), f32),
            pltpu.VMEM((cols, dim), f32),
            pltpu.SemaphoreType.DMA((2 + ROW_CHUNKS,)),
        ],
        compiler_params=pltpu.CompilerParams(vmem_limit_bytes=24 * MIB),
        name="cross_partial",
    )(*[pltpu.with_memory_space_constraint(x, pltpu.HBM) for x in (codes_t, book_t, residuals)])


def polar_kernel(*refs, blocks, pieces, chunk):
    block_refs = refs[:blocks]
    rot_b = refs[blocks]
    raw, gram, gram_b, poly_b, iterate, iterate_b, turned = refs[blocks + 1 :]
    dim = raw.shape[0]
    own = rot_b.shape[0]
    steps = dim // chunk
    at = 0
    for block in block_refs:
        raw[pl.ds(at, block.shape[0]), :] = block[...]
        at += block.shape[0]

    def band_of(i):
        return pl.ds(i * chunk, chunk)

    def lower(j):
        return pl.ds(j * chunk, dim - j * chunk), pl.ds(j * chunk, chunk)

    def mirror(target, j, value):
        rows, cols = lower(j)
        rounded = value.astype(bf16)
        target[rows, cols] = rounded
        if j < steps - 1:
            target[cols, pl.ds((j + 1) * chunk, dim - (j + 1) * chunk)] = rounded[chunk:, :].T

    def gram_of(source, transposed=None):
        r = lax.broadcasted_iota(jnp.int32, (chunk, chunk), 0)
        c = lax.broadcasted_iota(jnp.int32, (chunk, chunk), 1)
        trace = jnp.zeros((), f32)
        for j in range(steps):
            rows, cols = lower(j)
            if transposed is None:
                part = dot_nt(source[rows, :], source[cols, :])
            else:
                part = dot(source[rows, :], transposed[:, cols])
            gram[rows, cols] = part
            mirror(gram_b, j, part)
            trace = trace + jnp.sum(jnp.where(r == c, part[:chunk, :], 0.0))
        return trace

    def poly_of(wb, wc):
        for j in range(steps):
            rows, cols = lower(j)
            square = dot(gram_b[rows, :], gram_b[:, cols])
            mirror(poly_b, j, wb * gram[rows, cols] + wc * square)

    frob = gram_of(raw)
    scale2 = 1.0 / (frob + epsilon)
    scale = lax.rsqrt(frob + epsilon)
    poly_of(quintic_b * scale2, quintic_c * scale2 * scale2)

    for i in range(steps):
        cols = band_of(i)
        value = scale * (quintic_a * raw[:, cols].astype(f32) + dot(poly_b[...], raw[:, cols]))
        iterate[:, cols] = value
        rounded = value.astype(bf16)
        iterate_b[:, cols] = rounded
        turned[cols, :] = rounded.T

    gram_of(iterate_b, turned)
    poly_of(quintic_b, quintic_c)

    for i in range(steps):
        cols = band_of(i)
        value = quintic_a * iterate[:, cols] + dot(poly_b[...], iterate_b[:, cols])
        iterate[pl.ds(0, own), cols] = value[:own, :]
        rounded = value.astype(bf16)
        raw[:, cols] = rounded
        turned[cols, :] = rounded.T

    mine = pl.ds(0, own)
    g = dot(raw[mine, :], turned[...])
    image = dot(g.astype(bf16), raw[...])
    square = dot(image.astype(bf16), turned[...])
    last = quintic_a * iterate[mine, :] + dot(
        (quintic_b * g + quintic_c * square).astype(bf16), raw[...]
    )
    size = own // pieces
    for p in range(pieces):
        to = 0
        if pieces > 1:
            to = pl.multiple_of(jnp.bitwise_xor(lax.axis_index("dp"), p) * size, size)
        rot_b[pl.ds(to, size), :] = last[p * size : (p + 1) * size, :].astype(bf16)


LOWS = 64


def onehot_kernel(codes_ref, res_ref, onehot_ref, masks_ref, counts_ref, turned_ref):
    subs, rows_all = codes_ref.shape
    step = 256
    for i in range(rows_all // step):
        rows = pl.ds(i * step, step)
        turned_ref[:, rows] = res_ref[rows, :].T
    highs = counts_ref.shape[1] // LOWS
    wide = masks_ref.shape[0] // subs
    group = min(subs, 256 // LOWS)
    low_word = lax.broadcasted_iota(jnp.int32, (LOWS, rows_all), 0)
    high_word = lax.broadcasted_iota(jnp.int32, (8, rows_all), 0)
    row = lax.broadcasted_iota(jnp.int32, (wide, rows_all), 0)
    for first in range(0, subs, group):
        onehots, marks = [], []
        for m in range(first, first + group):
            code = codes_ref[pl.ds(m, 1), :]
            low, high = jnp.bitwise_and(code, LOWS - 1), jnp.right_shift(code, 6)
            onehots.append(jnp.where(low_word == low, 1.0, 0.0).astype(bf16))
            marks.append(jnp.where(high_word == high, 1.0, 0.0))
            mask = jnp.where(row // (wide // highs) == high, 1.0, 0.0).astype(bf16)
            masks_ref[pl.ds(m * wide, wide), :] = mask
        onehot = jnp.concatenate(onehots, axis=0).T
        onehot_ref[:, pl.ds(first * LOWS, group * LOWS)] = onehot
        part = dot(jnp.concatenate(marks, axis=0).astype(bf16), onehot)
        for s in range(group):
            for h in range(highs):
                counts_ref[pl.ds(first + s, 1), pl.ds(h * LOWS, LOWS)] = part[
                    s * 8 + h : s * 8 + h + 1, s * LOWS : (s + 1) * LOWS
                ]


def onehot_call(codes_t, residuals, words, width):
    subs, rows = codes_t.shape
    vmem = pl.BlockSpec(memory_space=pltpu.VMEM)
    return pl.pallas_call(
        onehot_kernel,
        out_shape=(
            jax.ShapeDtypeStruct((rows, subs * LOWS), bf16),
            jax.ShapeDtypeStruct((subs * width * (words // LOWS), rows), bf16),
            jax.ShapeDtypeStruct((subs, words), f32),
            jax.ShapeDtypeStruct(residuals.shape[::-1], bf16),
        ),
        in_specs=[vmem, vmem],
        out_specs=(vmem,) * 4,
        compiler_params=pltpu.CompilerParams(vmem_limit_bytes=24 * MIB),
        cost_estimate=pl.CostEstimate(
            flops=2 * 256 * subs * LOWS * rows, bytes_accessed=2 * subs * LOWS * rows, transcendentals=0
        ),
        name="onehot",
    )(codes_t, residuals)


def sums_kernel(rot_ref, res_ref, onehot_ref, masks_ref, counts_ref, sent_ref, sums_ref):
    subs, words = counts_ref.shape
    own = rot_ref.shape[0]
    width = own // subs
    highs = words // LOWS
    group = min(subs, 256 // LOWS)
    rot_t = dot(rot_ref[...], res_ref[...])
    for first in range(0, subs, group):
        values = []
        for m in range(first, first + group):
            band = rot_t[m * width : (m + 1) * width, :]
            values.append(jnp.concatenate([band] * highs, axis=0).astype(bf16))
        wide = group * highs * width
        tall = jnp.concatenate(values, axis=0) * masks_ref[pl.ds(first // group * wide, wide), :]
        part = dot(tall, onehot_ref[:, pl.ds(first * LOWS, group * LOWS)])
        for s in range(group):
            for h in range(highs):
                at = (s * highs + h) * width
                sums_ref[pl.ds((first + s) * width, width), pl.ds(h * LOWS, LOWS)] = part[
                    at : at + width, s * LOWS : (s + 1) * LOWS
                ]
    sent_ref[pl.ds(0, own), :] = sums_ref[...].astype(bf16)
    sent_ref[pl.ds(own, subs), :] = counts_ref[...].astype(bf16)


def rotated_kernel(rot_ref, res_ref, rotated_ref):
    rows_all = res_ref.shape[0]
    step = 512

    @pl.loop(0, rows_all // step)
    def _(i):
        rows = pl.ds(pl.multiple_of(i * step, step), step)
        rotated_ref[rows, :] = dot_nt(res_ref[rows, :], rot_ref[...])


def polar(block_list, own, pieces):
    dim = block_list[0].shape[1]
    vmem = pl.BlockSpec(memory_space=pltpu.VMEM)
    kernel = functools.partial(polar_kernel, blocks=len(block_list), pieces=pieces, chunk=256)
    return pl.pallas_call(
        kernel,
        out_shape=jax.ShapeDtypeStruct((own, dim), bf16),
        in_specs=[vmem] * len(block_list),
        out_specs=vmem,
        scratch_shapes=[
            pltpu.VMEM((dim, dim), bf16),
            pltpu.VMEM((dim, dim), f32),
            pltpu.VMEM((dim, dim), bf16),
            pltpu.VMEM((dim, dim), bf16),
            pltpu.VMEM((dim, dim), f32),
            pltpu.VMEM((dim, dim), bf16),
            pltpu.VMEM((dim, dim), bf16),
        ],
        compiler_params=pltpu.CompilerParams(vmem_limit_bytes=30 * MIB),
        name="polar",
    )(*block_list)


def share_kernel(*refs):
    total = refs[0][...].astype(f32)
    for part in refs[1:-1]:
        total = total + part[...].astype(f32)
    refs[-1][...] = total.astype(refs[-1].dtype)


def book_kernel(book_ref, *refs):
    sums, out_ref = refs[:-1], refs[-1]
    own = book_ref.shape[0]
    subs = sums[0].shape[0] - own
    width = own // subs
    total = sums[0][...].astype(f32)
    for part in sums[1:]:
        total = total + part[...].astype(f32)
    for m in range(subs):
        band = pl.ds(m * width, width)
        count = total[own + m : own + m + 1, :] + prior_weight
        part = total[m * width : (m + 1) * width, :]
        out_ref[band, :] = (part + prior_weight * book_ref[band, :]) / count


def small_call(kernel, name, shape, dtype, *operands, scratch=()):
    vmem = pl.BlockSpec(memory_space=pltpu.VMEM)
    return pl.pallas_call(
        kernel,
        out_shape=jax.ShapeDtypeStruct(shape, dtype),
        in_specs=[vmem] * len(operands),
        out_specs=vmem,
        scratch_shapes=scratch,
        compiler_params=pltpu.CompilerParams(vmem_limit_bytes=24 * MIB),
        name=name,
    )(*operands)


def swap(value, axis, size, mask, odd_mask=None):
    odd_mask = mask if odd_mask is None else odd_mask
    return lax.ppermute(value, axis, [(i, i ^ (odd_mask if i % 2 else mask)) for i in range(size)])


def make_body(dp, code):
    def body(residuals, codes, codebook):
        rows, dim = residuals.shape
        subs, words, width = codebook.shape
        own = subs * width
        codes_t = codes.T
        book_t = jnp.transpose(codebook, (0, 2, 1)).reshape(own, words)
        size = own // dp
        thin = size % 16 != 0
        if thin:
            place = lax.axis_index("dp")
            partial, codes_v, book_v, res_v = cross_partial(codes_t, book_t, residuals, None)
            cut = [
                lax.dynamic_slice_in_dim(partial, (place ^ k) * size, size, 0) for k in range(dp)
            ]
            parts = [cut[0]] + [part.astype(bf16) for part in cut[1:]]
        else:
            *parts, codes_v, book_v, res_v = cross_partial(codes_t, book_t, residuals, dp)
        far_first = range(dp - 1, 0, -1)
        got = [swap(parts[k], "dp", dp, k) for k in far_first]
        *ready, res_t = onehot_call(codes_v, res_v, words, width)
        got, ready, res_t = lax.optimization_barrier((got, ready, res_t))
        piece = small_call(share_kernel, "share", (size, dim), bf16, parts[0], *got)
        pieces = {0: piece}
        for k in far_first:
            pieces[k] = swap(piece, "dp", dp, k)
        if thin:
            block = jnp.zeros((own, dim), bf16)
            for k in range(dp):
                block = lax.dynamic_update_slice_in_dim(block, pieces[k], (place ^ k) * size, 0)
            held = [block]
        else:
            half = max(dp // 2, 1)
            held = [
                jnp.concatenate([pieces[k] for k in range(at, min(at + half, dp))], axis=0)
                for at in range(0, dp, half)
            ]
        strides = [1 << b for b in reversed(range(code.bit_length() - 1))]
        far = strides[:-1]
        for even, odd in zip(far, far[::-1]):
            held = held + [swap(t, "code", code, even, odd) for t in held]
        for stride in strides[-1:]:
            held = held + [swap(t, "code", code, stride) for t in held]
        rotation_t = polar(held, own, 1 if thin else dp)
        scratch = [pltpu.VMEM((own, words), f32)]
        operands = (rotation_t, res_t, *ready)
        sums = small_call(sums_kernel, "sums", (own + subs, words), bf16, *operands, scratch=scratch)
        rotated = small_call(rotated_kernel, "rotated", (rows, own), f32, rotation_t, res_v)
        others = [swap(sums, "dp", dp, k) for k in range(1, dp)]
        book = small_call(book_kernel, "book", (own, words), f32, book_v, sums, *others)
        return rotated, jnp.transpose(book.reshape(subs, width, words), (0, 2, 1))

    return body


def solution(mesh):
    dp, code = mesh.shape["dp"], mesh.shape["code"]
    in_specs = (P("dp", None), P("dp", "code"), P("code", None, None))
    out_specs = (P("dp", "code"), P("code", None, None))
    return jax.shard_map(
        make_body(dp, code), mesh=mesh, in_specs=in_specs, out_specs=out_specs, check_vma=False
    )
```

```python
import functools

import jax
import jax.numpy as jnp
from jax import lax
from jax.experimental import pallas as pl
from jax.experimental.pallas import tpu as pltpu
from jax.sharding import PartitionSpec as P

quintic_a = 3.4445
quintic_b = -4.775
quintic_c = 2.0315
prior_weight = 8.0
epsilon = 1e-06
f32, bf16 = jnp.float32, jnp.bfloat16
MIB = 1024 * 1024
ROW_CHUNKS = 2
NT = (((1,), (1,)), ((), ()))


def dot(left, right):
    return jnp.dot(left, right, preferred_element_type=f32)


def dot_nt(left, right):
    return lax.dot_general(left, right, NT, preferred_element_type=f32)


def cross_kernel(codes_hbm, book_hbm, res_hbm, *refs, dp):
    outs = refs[: dp or 1]
    codes_ref, book_ref, res_ref, recon, cross, sems = refs[dp or 1 :]
    subs, rows = codes_ref.shape
    width = book_ref.shape[0] // subs
    words = book_ref.shape[1]
    lanes = 128
    chunks = sems.shape[0] - 2
    step = rows // chunks
    loads = [
        pltpu.make_async_copy(codes_hbm, codes_ref, sems.at[0]),
        pltpu.make_async_copy(book_hbm, book_ref, sems.at[1]),
    ]
    for i in range(chunks):
        part = pl.ds(i * step, step)
        loads.append(pltpu.make_async_copy(res_hbm.at[part], res_ref.at[part], sems.at[2 + i]))
    for load in loads:
        load.start()
    loads[0].wait()
    loads[1].wait()
    total = outs[0] if dp is None else cross
    for i in range(chunks):
        part = pl.ds(i * step, step)
        for m in range(subs):
            band = pl.ds(m * width, width)
            tables = [book_ref[band, pl.ds(t * lanes, lanes)] for t in range(words // lanes)]
            for c in range(i * step // lanes, (i + 1) * step // lanes):
                cols = pl.ds(c * lanes, lanes)
                code = jnp.broadcast_to(codes_ref[pl.ds(m, 1), cols], (width, lanes))
                low = jnp.bitwise_and(code, lanes - 1)
                value = jnp.take_along_axis(tables[0], low, axis=1, mode="promise_in_bounds")
                for t in range(1, len(tables)):
                    other = jnp.take_along_axis(tables[t], low, axis=1, mode="promise_in_bounds")
                    value = jnp.where(code >= t * lanes, other, value)
                recon[band, cols] = value
        loads[2 + i].wait()
        product = dot(recon[:, part].astype(bf16), res_ref[part, :])
        total[...] = product if i == 0 else total[...] + product
    if dp is None:
        return
    place = lax.axis_index("dp")
    size = outs[0].shape[0]
    for k, out in enumerate(outs):
        at = pl.multiple_of(jnp.bitwise_xor(place, k) * size, size)
        out[...] = cross[pl.ds(at, size), :].astype(out.dtype)


def cross_partial(codes_t, book_t, residuals, dp):
    rows, dim = residuals.shape
    cols = book_t.shape[0]
    if dp is None:
        shapes = (jax.ShapeDtypeStruct((cols, dim), f32),)
    else:
        shapes = tuple(
            jax.ShapeDtypeStruct((cols // dp, dim), bf16 if k else f32) for k in range(dp)
        )
    shapes += tuple(jax.ShapeDtypeStruct(x.shape, x.dtype) for x in (codes_t, book_t, residuals))
    return pl.pallas_call(
        functools.partial(cross_kernel, dp=dp),
        out_shape=shapes,
        in_specs=[pl.BlockSpec(memory_space=pltpu.HBM)] * 3,
        out_specs=(pl.BlockSpec(memory_space=pltpu.VMEM),) * len(shapes),
        scratch_shapes=[
            pltpu.VMEM((cols, rows), f32),
            pltpu.VMEM((cols, dim), f32),
            pltpu.SemaphoreType.DMA((2 + ROW_CHUNKS,)),
        ],
        compiler_params=pltpu.CompilerParams(vmem_limit_bytes=24 * MIB),
        name="cross_partial",
    )(*[pltpu.with_memory_space_constraint(x, pltpu.HBM) for x in (codes_t, book_t, residuals)])


def polar_kernel(*refs, blocks, pieces, chunk):
    block_refs = refs[:blocks]
    rot_b = refs[blocks]
    raw, gram, gram_b, poly_b, iterate, iterate_b, turned = refs[blocks + 1 :]
    dim = raw.shape[0]
    own = rot_b.shape[0]
    steps = dim // chunk
    at = 0
    for block in block_refs:
        raw[pl.ds(at, block.shape[0]), :] = block[...]
        at += block.shape[0]

    def band_of(i):
        return pl.ds(i * chunk, chunk)

    def lower(j):
        return pl.ds(j * chunk, dim - j * chunk), pl.ds(j * chunk, chunk)

    def mirror(target, j, value):
        rows, cols = lower(j)
        rounded = value.astype(bf16)
        target[rows, cols] = rounded
        if j < steps - 1:
            target[cols, pl.ds((j + 1) * chunk, dim - (j + 1) * chunk)] = rounded[chunk:, :].T

    def gram_of(source, transposed=None):
        r = lax.broadcasted_iota(jnp.int32, (chunk, chunk), 0)
        c = lax.broadcasted_iota(jnp.int32, (chunk, chunk), 1)
        trace = jnp.zeros((), f32)
        for j in range(steps):
            rows, cols = lower(j)
            if transposed is None:
                part = dot_nt(source[rows, :], source[cols, :])
            else:
                part = dot(source[rows, :], transposed[:, cols])
            gram[rows, cols] = part
            mirror(gram_b, j, part)
            trace = trace + jnp.sum(jnp.where(r == c, part[:chunk, :], 0.0))
        return trace

    def poly_of(wb, wc):
        for j in range(steps):
            rows, cols = lower(j)
            square = dot(gram_b[rows, :], gram_b[:, cols])
            mirror(poly_b, j, wb * gram[rows, cols] + wc * square)

    frob = gram_of(raw)
    scale2 = 1.0 / (frob + epsilon)
    scale = lax.rsqrt(frob + epsilon)
    poly_of(quintic_b * scale2, quintic_c * scale2 * scale2)

    for i in range(steps):
        cols = band_of(i)
        value = scale * (quintic_a * raw[:, cols].astype(f32) + dot(poly_b[...], raw[:, cols]))
        iterate[:, cols] = value
        rounded = value.astype(bf16)
        iterate_b[:, cols] = rounded
        turned[cols, :] = rounded.T

    gram_of(iterate_b, turned)
    poly_of(quintic_b, quintic_c)

    for i in range(steps):
        cols = band_of(i)
        value = quintic_a * iterate[:, cols] + dot(poly_b[...], iterate_b[:, cols])
        iterate[pl.ds(0, own), cols] = value[:own, :]
        rounded = value.astype(bf16)
        raw[:, cols] = rounded
        turned[cols, :] = rounded.T

    mine = pl.ds(0, own)
    g = dot(raw[mine, :], turned[...])
    image = dot(g.astype(bf16), raw[...])
    square = dot(image.astype(bf16), turned[...])
    last = quintic_a * iterate[mine, :] + dot(
        (quintic_b * g + quintic_c * square).astype(bf16), raw[...]
    )
    size = own // pieces
    for p in range(pieces):
        to = 0
        if pieces > 1:
            to = pl.multiple_of(jnp.bitwise_xor(lax.axis_index("dp"), p) * size, size)
        rot_b[pl.ds(to, size), :] = last[p * size : (p + 1) * size, :].astype(bf16)


LOWS = 64


def onehot_kernel(codes_ref, res_ref, onehot_ref, masks_ref, counts_ref, turned_ref):
    subs, rows_all = codes_ref.shape
    step = 256
    for i in range(rows_all // step):
        rows = pl.ds(i * step, step)
        turned_ref[:, rows] = res_ref[rows, :].T
    highs = counts_ref.shape[1] // LOWS
    wide = masks_ref.shape[0] // subs
    group = min(subs, 256 // LOWS)
    low_word = lax.broadcasted_iota(jnp.int32, (LOWS, rows_all), 0)
    high_word = lax.broadcasted_iota(jnp.int32, (8, rows_all), 0)
    row = lax.broadcasted_iota(jnp.int32, (wide, rows_all), 0)
    for first in range(0, subs, group):
        onehots, marks = [], []
        for m in range(first, first + group):
            code = codes_ref[pl.ds(m, 1), :]
            low, high = jnp.bitwise_and(code, LOWS - 1), jnp.right_shift(code, 6)
            onehots.append(jnp.where(low_word == low, 1.0, 0.0).astype(bf16))
            marks.append(jnp.where(high_word == high, 1.0, 0.0))
            mask = jnp.where(row // (wide // highs) == high, 1.0, 0.0).astype(bf16)
            masks_ref[pl.ds(m * wide, wide), :] = mask
        onehot = jnp.concatenate(onehots, axis=0).T
        onehot_ref[:, pl.ds(first * LOWS, group * LOWS)] = onehot
        part = dot(jnp.concatenate(marks, axis=0).astype(bf16), onehot)
        for s in range(group):
            for h in range(highs):
                counts_ref[pl.ds(first + s, 1), pl.ds(h * LOWS, LOWS)] = part[
                    s * 8 + h : s * 8 + h + 1, s * LOWS : (s + 1) * LOWS
                ]


def onehot_call(codes_t, residuals, words, width):
    subs, rows = codes_t.shape
    vmem = pl.BlockSpec(memory_space=pltpu.VMEM)
    return pl.pallas_call(
        onehot_kernel,
        out_shape=(
            jax.ShapeDtypeStruct((rows, subs * LOWS), bf16),
            jax.ShapeDtypeStruct((subs * width * (words // LOWS), rows), bf16),
            jax.ShapeDtypeStruct((subs, words), f32),
            jax.ShapeDtypeStruct(residuals.shape[::-1], bf16),
        ),
        in_specs=[vmem, vmem],
        out_specs=(vmem,) * 4,
        compiler_params=pltpu.CompilerParams(vmem_limit_bytes=24 * MIB),
        cost_estimate=pl.CostEstimate(
            flops=2 * 256 * subs * LOWS * rows, bytes_accessed=2 * subs * LOWS * rows, transcendentals=0
        ),
        name="onehot",
    )(codes_t, residuals)


def sums_kernel(rot_ref, res_ref, onehot_ref, masks_ref, counts_ref, sent_ref, sums_ref):
    subs, words = counts_ref.shape
    own = rot_ref.shape[0]
    width = own // subs
    highs = words // LOWS
    group = min(subs, 256 // LOWS)
    rot_t = dot(rot_ref[...], res_ref[...])
    for first in range(0, subs, group):
        values = []
        for m in range(first, first + group):
            band = rot_t[m * width : (m + 1) * width, :]
            values.append(jnp.concatenate([band] * highs, axis=0).astype(bf16))
        wide = group * highs * width
        tall = jnp.concatenate(values, axis=0) * masks_ref[pl.ds(first // group * wide, wide), :]
        part = dot(tall, onehot_ref[:, pl.ds(first * LOWS, group * LOWS)])
        for s in range(group):
            for h in range(highs):
                at = (s * highs + h) * width
                sums_ref[pl.ds((first + s) * width, width), pl.ds(h * LOWS, LOWS)] = part[
                    at : at + width, s * LOWS : (s + 1) * LOWS
                ]
    sent_ref[pl.ds(0, own), :] = sums_ref[...].astype(bf16)
    sent_ref[pl.ds(own, subs), :] = counts_ref[...].astype(bf16)


def rotated_kernel(rot_ref, res_ref, rotated_ref):
    rows_all = res_ref.shape[0]
    step = 512

    @pl.loop(0, rows_all // step)
    def _(i):
        rows = pl.ds(pl.multiple_of(i * step, step), step)
        rotated_ref[rows, :] = dot_nt(res_ref[rows, :], rot_ref[...])


def polar(block_list, own, pieces):
    dim = block_list[0].shape[1]
    vmem = pl.BlockSpec(memory_space=pltpu.VMEM)
    kernel = functools.partial(polar_kernel, blocks=len(block_list), pieces=pieces, chunk=256)
    return pl.pallas_call(
        kernel,
        out_shape=jax.ShapeDtypeStruct((own, dim), bf16),
        in_specs=[vmem] * len(block_list),
        out_specs=vmem,
        scratch_shapes=[
            pltpu.VMEM((dim, dim), bf16),
            pltpu.VMEM((dim, dim), f32),
            pltpu.VMEM((dim, dim), bf16),
            pltpu.VMEM((dim, dim), bf16),
            pltpu.VMEM((dim, dim), f32),
            pltpu.VMEM((dim, dim), bf16),
            pltpu.VMEM((dim, dim), bf16),
        ],
        compiler_params=pltpu.CompilerParams(vmem_limit_bytes=30 * MIB),
        name="polar",
    )(*block_list)


def share_kernel(*refs):
    total = refs[0][...].astype(f32)
    for part in refs[1:-1]:
        total = total + part[...].astype(f32)
    refs[-1][...] = total.astype(refs[-1].dtype)


def book_kernel(book_ref, *refs):
    sums, out_ref = refs[:-1], refs[-1]
    own = book_ref.shape[0]
    subs = sums[0].shape[0] - own
    width = own // subs
    total = sums[0][...].astype(f32)
    for part in sums[1:]:
        total = total + part[...].astype(f32)
    for m in range(subs):
        band = pl.ds(m * width, width)
        count = total[own + m : own + m + 1, :] + prior_weight
        part = total[m * width : (m + 1) * width, :]
        out_ref[band, :] = (part + prior_weight * book_ref[band, :]) / count


def small_call(kernel, name, shape, dtype, *operands, scratch=()):
    vmem = pl.BlockSpec(memory_space=pltpu.VMEM)
    return pl.pallas_call(
        kernel,
        out_shape=jax.ShapeDtypeStruct(shape, dtype),
        in_specs=[vmem] * len(operands),
        out_specs=vmem,
        scratch_shapes=scratch,
        compiler_params=pltpu.CompilerParams(vmem_limit_bytes=24 * MIB),
        name=name,
    )(*operands)


def swap(value, axis, size, mask, odd_mask=None):
    odd_mask = mask if odd_mask is None else odd_mask
    return lax.ppermute(value, axis, [(i, i ^ (odd_mask if i % 2 else mask)) for i in range(size)])


def make_body(dp, code):
    def body(residuals, codes, codebook):
        rows, dim = residuals.shape
        subs, words, width = codebook.shape
        own = subs * width
        codes_t = codes.T
        book_t = jnp.transpose(codebook, (0, 2, 1)).reshape(own, words)
        size = own // dp
        thin = size % 16 != 0
        if thin:
            place = lax.axis_index("dp")
            partial, codes_v, book_v, res_v = cross_partial(codes_t, book_t, residuals, None)
            cut = [
                lax.dynamic_slice_in_dim(partial, (place ^ k) * size, size, 0) for k in range(dp)
            ]
            parts = [cut[0]] + [part.astype(bf16) for part in cut[1:]]
        else:
            *parts, codes_v, book_v, res_v = cross_partial(codes_t, book_t, residuals, dp)
        far_first = range(dp - 1, 0, -1)
        got = [swap(parts[k], "dp", dp, k) for k in far_first]
        *ready, res_t = onehot_call(codes_v, res_v, words, width)
        got, ready, res_t = lax.optimization_barrier((got, ready, res_t))
        piece = small_call(share_kernel, "share", (size, dim), bf16, parts[0], *got)
        pieces = {0: piece}
        for k in far_first:
            pieces[k] = swap(piece, "dp", dp, k)
        if thin:
            block = jnp.zeros((own, dim), bf16)
            for k in range(dp):
                block = lax.dynamic_update_slice_in_dim(block, pieces[k], (place ^ k) * size, 0)
            held = [block]
        else:
            half = max(dp // 2, 1)
            held = [
                jnp.concatenate([pieces[k] for k in range(at, min(at + half, dp))], axis=0)
                for at in range(0, dp, half)
            ]
        strides = [1 << b for b in reversed(range(code.bit_length() - 1))]
        far = strides[:-1]
        for even, odd in zip(far, far[::-1]):
            held = held + [swap(t, "code", code, even, odd) for t in held]
        for stride in strides[-1:]:
            held = held + [swap(t, "code", code, stride) for t in held]
        rotation_t = polar(held, own, 1 if thin else dp)
        scratch = [pltpu.VMEM((own, words), f32)]
        operands = (rotation_t, res_t, *ready)
        sums = small_call(sums_kernel, "sums", (own + subs, words), bf16, *operands, scratch=scratch)
        rotated = small_call(rotated_kernel, "rotated", (rows, own), f32, rotation_t, res_v)
        others = [swap(sums, "dp", dp, k) for k in range(1, dp)]
        book = small_call(book_kernel, "book", (own, words), f32, book_v, sums, *others)
        return rotated, jnp.transpose(book.reshape(subs, width, words), (0, 2, 1))

    return body


def solution(mesh):
    dp, code = mesh.shape["dp"], mesh.shape["code"]
    in_specs = (P("dp", None), P("dp", "code"), P("code", None, None))
    out_specs = (P("dp", "code"), P("code", None, None))
    return jax.shard_map(
        make_body(dp, code), mesh=mesh, in_specs=in_specs, out_specs=out_specs, check_vma=False
    )
```
